32 devices in a mesh: lat: 4 (over y, x), lon: 8 (over z, core).
Axes of the slice: x: 2, y: 2, z: 4, core: 2. Of those that a mesh axis runs over, the one named last changes fastest.
Arguments:
- height: float32 [256, 8640], P('lat', 'lon'), may hold values from -6 to 6
- east_flow: float32 [256, 8640], P('lat', 'lon'), may hold values from -4 to 4
- north_flow: float32 [256, 8640], P('lat', 'lon'), may hold values from -4 to 4
- legendre: float32 [32, 256, 2048], P('lon', 'lat'), may hold values from -0.375 to 0.375
- love_numbers: float32 [2048], replicated, may hold values from 0.05 to 1
- wavenumbers: int32 [32], replicated, may hold values from 0 to 2047, as said below
- land_sea: int32 [256, 8640], P('lat', 'lon'), may hold values 0 or 1
Outputs:
- loading: float32 [256, 8640], P('lat', 'lon')
- surface: float32 [256, 8640], P('lat', 'lon')
- east_out: float32 [256, 8640], P('lat', 'lon')
- north_out: float32 [256, 8640], P('lat', 'lon')
The draws below stay inside these ranges and needn't reach their ends.
Inputs may be any that keep to these rules, and one draw needn't show every extreme that they name: 32 distinct wavenumbers in no particular order; 0 and 2047 are always among them.
All inputs are finite; a program needn't handle non-finite values. No bound on the sum of `land_sea` on one device may be relied on, other than what follows from the above.
Results may differ from the reference program's by a relative error of at most 0.000078.
Values sent between devices are 32-bit elements; how exact they have to be, the bound alone decides.
No kernel may reach another device: no remote copies, remote signals or barrier semaphores. Data moves between devices by JAX's collectives and lax.ppermute only.
A program may use at most 64 MiB of HBM per device.

```python
import math
import jax
import jax.numpy as jnp
from jax import lax

NLON = 8640
DEGREES = 2048
KMAX = 2048
SUBSTEPS = 4
WAVES = 32
NLAT = 256


def draw_wavenumbers(key, part):
    chosen = jax.random.permutation(key, KMAX - 2)[:WAVES - 2] + 1
    ends = jnp.array([0, KMAX - 1], dtype=jnp.int32)
    mixed = jnp.concatenate([chosen.astype(jnp.int32), ends])
    return jax.random.permutation(jax.random.fold_in(key, 7), mixed).astype(jnp.int32)


def set_ends(entries, stream_key, low, largest):
    place = [jax.random.randint(jax.random.fold_in(stream_key, axis), (), 0, length) for axis, length in enumerate(entries.shape)]
    widest = entries.shape.index(max(entries.shape))
    beside = place[:widest] + [(place[widest] + 1) % entries.shape[widest]] + place[widest + 1:]
    return entries.at[tuple(place)].set(low).at[tuple(beside)].set(largest)


def block_levels(rng, extent, cuts, low, largest):
    gain = 1.0
    for axis_at, blocks in cuts:
        heights = jax.random.uniform(jax.random.fold_in(jax.random.fold_in(rng, 6), axis_at), (blocks,), jnp.float32, low / len(cuts), largest / len(cuts))
        gain = gain * jnp.repeat(jnp.exp(heights), extent[axis_at] // blocks).reshape((-1,) + (1,) * (len(extent) - 1 - axis_at))
    return gain


def noise(key, dims, width, bound, cuts=(), kind=jnp.bfloat16):
    values = jax.random.normal(key, dims, jnp.float32) * width
    if len(cuts) > 0:
        values = block_levels(key, dims, cuts, -0.22, 0.18) * values
    return jnp.clip(values, min=-bound, max=bound).astype(kind)


def setup_inputs(seed: int = 0) -> dict:
    splits = jax.random.split(jax.random.key(seed), 8)
    return {
        "height": noise(splits[0], (NLAT, NLON), 1.0, 6.0, ((0, 4), (1, 8)), jnp.float32),
        "east_flow": noise(splits[1], (NLAT, NLON), 0.5, 4.0, ((0, 4), (1, 8)), jnp.float32),
        "north_flow": noise(splits[2], (NLAT, NLON), 0.5, 4.0, ((0, 4), (1, 8)), jnp.float32),
        "legendre": noise(splits[3], (WAVES, NLAT, DEGREES), NLAT ** -0.5, 0.375, ((0, 8), (1, 4)), jnp.float32),
        "love_numbers": jnp.clip(jnp.exp(jax.random.uniform(splits[4], (DEGREES,), jnp.float32, math.log(0.05), math.log(1.0))), 0.05, 1.0),
        "wavenumbers": draw_wavenumbers(jax.random.fold_in(splits[7], 71), 0),
        "land_sea": set_ends((jax.random.randint(splits[6], (NLAT, NLON), 0, 5) < 4).astype(jnp.int32), jax.random.fold_in(splits[6], 1), 0, 1),
    }


def harmonic_rows(wavenumbers, first_column, column_count, period):
    columns = first_column + jnp.arange(column_count, dtype=jnp.int32)
    product = wavenumbers.astype(jnp.int32)[:, None] * columns[None, :] % period
    angles = 2.0 * math.pi / period * product.astype(jnp.float32)
    stacked = jnp.stack([jnp.cos(angles), jnp.sin(angles)], axis=1)
    return stacked.reshape(2 * wavenumbers.shape[0], column_count)

def reference(height, east_flow, north_flow, legendre, love_numbers, wavenumbers, land_sea):
    hp = lax.Precision.HIGHEST
    harmonics = harmonic_rows(wavenumbers, 0, NLON, NLON)
    fourier = lax.dot_general(harmonics, height, (((1,), (1,)), ((), ())), precision=hp) * (1.0 / math.sqrt(NLON))
    fourier = fourier.reshape(WAVES, 2, NLAT)
    spectral = jnp.einsum('mtl,mpt->mpl', legendre, fourier, precision=hp) * love_numbers[None, None, :]
    synthesized = jnp.einsum('mtl,mpl->mpt', legendre, spectral, precision=hp).reshape(2 * WAVES, NLAT)
    loading = lax.dot_general(synthesized, harmonics, (((0,), (0,)), ((), ())), precision=hp) * (1.0 / math.sqrt(WAVES))
    wet_cells = land_sea.astype(jnp.float32)
    surface = height
    east_out = east_flow
    north_out = north_flow
    for substep in range(SUBSTEPS):
        pressure = surface - loading
        padded = jnp.pad(pressure, ((1, 1), (0, 0)))
        east_out = wet_cells * (east_out - 0.3 * (jnp.roll(pressure, -1, 1) - jnp.roll(pressure, 1, 1)))
        north_out = wet_cells * (north_out - 0.3 * (padded[2:] - padded[:-2]))
        north_pad = jnp.pad(north_out, ((1, 1), (0, 0)))
        change = 0.3 * (jnp.roll(east_out, -1, 1) - jnp.roll(east_out, 1, 1)) + 0.3 * (north_pad[2:] - north_pad[:-2])
        surface = surface - wet_cells * change
    return (loading, surface, east_out, north_out)
```

```python
import functools
import math

import jax
import jax.numpy as jnp
from jax import lax
from jax.experimental import pallas as pl
from jax.experimental.pallas import tpu as pltpu
from jax.sharding import PartitionSpec as P

SUBSTEPS = 4
MARGIN = 2 * SUBSTEPS
STEP = 0.3

f32 = jnp.float32
bf16 = jnp.bfloat16
VMEM = pl.BlockSpec(memory_space=pltpu.VMEM)
SMEM = pl.BlockSpec(memory_space=pltpu.SMEM)


def split2(x):
    hi = x.astype(bf16)
    lo = (x - hi.astype(f32)).astype(bf16)
    return hi, lo


def dft_kernel(period, own_waves, first_ref, waves_ref, height_ref, part_ref, harm_ref, field_ref):
    rows, cols = height_ref.shape
    waves, width = harm_ref.shape[0] // 2, harm_ref.shape[1]
    wave = waves_ref[...]
    start = wave * first_ref[0]
    turns = jnp.floor(start.astype(f32) * (1.0 / period)).astype(jnp.int32)
    start = (start - turns * period).astype(f32)
    wave = wave.astype(f32)
    row = lax.broadcasted_iota(jnp.int32, (waves, 1), 0)
    sine = (lax.rem(row, 2 * own_waves) >= own_waves).astype(f32)
    offset = 4.0 * start - period * sine
    for tile in range(0, width, 128):
        lane = lax.broadcasted_iota(jnp.int32, (1, 128), 1) + tile
        lane = jnp.where(lane < cols + MARGIN, lane, lane - width).astype(f32)
        product = wave * lane
        product = product - period * jnp.floor(product * (1.0 / period))
        quarter = 4.0 * product + offset
        turn = jnp.floor(quarter * (1.0 / period) + 0.5)
        angle = (quarter - period * turn) * (0.5 * math.pi / period)
        square = angle * angle
        cosine = 1.0 + square * (
            -1.0 / 2 + square * (1.0 / 24 + square * (-1.0 / 720 + square * (1.0 / 40320)))
        )
        sine_of = angle * (
            1.0
            + square
            * (-1.0 / 6 + square * (1.0 / 120 + square * (-1.0 / 5040 + square * (1.0 / 362880))))
        )
        phase = turn - 4.0 * jnp.floor(turn * 0.25)
        odd = (phase == 1.0) | (phase == 3.0)
        value = jnp.where(odd, sine_of, cosine)
        value = jnp.where((phase == 1.0) | (phase == 2.0), -value, value)
        hi, lo = split2(value)
        harm_ref[:waves, tile : tile + 128] = hi
        harm_ref[waves:, tile : tile + 128] = lo
        stop = min(cols, tile + 128)
        if stop <= tile:
            block = jnp.zeros((rows, 128), f32)
        elif stop == tile + 128:
            block = height_ref[:, tile : tile + 128]
        else:
            block = jnp.concatenate(
                [height_ref[:, tile:stop], jnp.zeros((rows, tile + 128 - stop), f32)], axis=1
            )
        hi, lo = split2(block)
        field_ref[:rows, tile : tile + 128] = hi
        field_ref[rows:, tile : tile + 128] = lo
    both = lax.dot_general(
        harm_ref[...], field_ref[...], (((1,), (1,)), ((), ())), preferred_element_type=f32
    )
    total = both[:waves] + both[waves:]
    total = (total[:, :rows] + total[:, rows:]) * (1.0 / math.sqrt(period))
    part_ref[...] = total.reshape(part_ref.shape)


def analysis_kernel(part_ref, legendre_ref, spectral_ref):
    slots, rows, degrees = legendre_ref.shape
    fourier = jnp.sum(part_ref[...], axis=0)
    columns = fourier.T
    for slot in range(slots):
        even = [
            jnp.broadcast_to(columns[o : o + 8, slot : slot + 1], (8, 128))
            for o in range(0, rows, 8)
        ]
        odd = [
            jnp.broadcast_to(columns[o : o + 8, slots + slot : slots + slot + 1], (8, 128))
            for o in range(0, rows, 8)
        ]
        for tile in range(0, degrees, 128):
            first = jnp.zeros((8, 128), f32)
            second = jnp.zeros((8, 128), f32)
            for at, o in enumerate(range(0, rows, 8)):
                block = legendre_ref[slot, o : o + 8, tile : tile + 128]
                first = first + block * even[at]
                second = second + block * odd[at]
            spectral_ref[slot : slot + 1, tile : tile + 128] = jnp.sum(
                first, axis=0, keepdims=True
            )
            spectral_ref[slots + slot : slots + slot + 1, tile : tile + 128] = jnp.sum(
                second, axis=0, keepdims=True
            )


def synthesis_kernel(
    parts_refs, love_ref, legendre_ref, low_ref, high_ref, out_ref, spectral_ref
):
    slots, rows, degrees = legendre_ref.shape
    total = parts_refs[0][...]
    for ref in parts_refs[1:]:
        total = total + ref[...]
    spectral_ref[...] = total * love_ref[...]
    taller = rows + 2 * MARGIN
    lanes = lax.broadcasted_iota(jnp.int32, (8, 128), 1)
    octets = [(low_ref, 0)] + [(legendre_ref, o) for o in range(0, rows, 8)] + [(high_ref, 0)]
    sums = [jnp.zeros((8, 128), f32) for _ in octets]
    for slot in range(slots):
        first = [jnp.zeros((8, 128), f32) for _ in octets]
        second = [jnp.zeros((8, 128), f32) for _ in octets]
        for tile in range(0, degrees, 128):
            even = jnp.broadcast_to(spectral_ref[slot : slot + 1, tile : tile + 128], (8, 128))
            odd = jnp.broadcast_to(
                spectral_ref[slots + slot : slots + slot + 1, tile : tile + 128], (8, 128)
            )
            for at, (ref, o) in enumerate(octets):
                block = ref[slot, o : o + 8, tile : tile + 128]
                first[at] = first[at] + block * even
                second[at] = second[at] + block * odd
        for at in range(len(octets)):
            sums[at] = jnp.where(lanes == slot, jnp.sum(first[at], axis=1, keepdims=True), sums[at])
            sums[at] = jnp.where(
                lanes == slots + slot, jnp.sum(second[at], axis=1, keepdims=True), sums[at]
            )
    column = jnp.concatenate(sums + [jnp.zeros((128 - taller, 128), f32)], axis=0)
    out_ref[...] = column.T[: 2 * slots]


def substep_kernel(
    synth_ref,
    harm_ref,
    height_ref,
    east_ref,
    north_ref,
    land_ref,
    low_ref,
    high_ref,
    left_ref,
    right_ref,
    loading_out,
    surface_out,
    east_out,
    north_out,
    load,
    pressure,
    surface,
    east,
    north,
    wet,
):
    rows, cols = height_ref.shape
    taller = rows + 2 * MARGIN
    width = harm_ref.shape[1]
    waves = harm_ref.shape[0] // 2
    synth = synth_ref[...].reshape(waves, 128).T * (1.0 / math.sqrt(waves // 2))
    hi, lo = split2(synth[:taller])
    left = jnp.concatenate(
        [jnp.concatenate([hi, hi], axis=1), jnp.concatenate([lo, lo], axis=1)], axis=0
    )
    both = lax.dot_general(
        left, harm_ref[...], (((1,), (0,)), ((), ())), preferred_element_type=f32
    )
    load[...] = both[:taller] + both[taller:]
    last = (cols // 128) * 128
    own = cols - last
    lanes = lax.broadcasted_iota(jnp.int32, (taller, width - last), 1)
    for at, (target, top, source) in enumerate(
        (
            (surface, 0, height_ref),
            (east, 0, east_ref),
            (north, 8, north_ref),
            (wet, 0, land_ref),
        )
    ):
        lows, middle, highs = (
            pl.ds(top, MARGIN),
            pl.ds(top + MARGIN, rows),
            pl.ds(top + MARGIN + rows, MARGIN),
        )
        target[lows, :last] = low_ref[at, :, :last]
        target[middle, :last] = source[:, :last].astype(f32)
        target[highs, :last] = high_ref[at, :, :last]
        tail = jnp.concatenate(
            [low_ref[at, :, last:cols], source[:, last:].astype(f32), high_ref[at, :, last:cols]],
            axis=0,
        )
        tail = jnp.concatenate([tail, jnp.zeros((taller, width - cols), f32)], axis=1)
        after = pltpu.roll(right_ref[...], (own - 2 * MARGIN * at) % 128, 1)
        before = pltpu.roll(left_ref[...], (-MARGIN - 2 * MARGIN * at - MARGIN) % 128, 1)
        after = jnp.concatenate([after] * ((width - last) // 128), axis=1)
        before = jnp.concatenate([before] * ((width - last) // 128), axis=1)
        tail = jnp.where((lanes >= own) & (lanes < own + MARGIN), after, tail)
        tail = jnp.where(lanes >= width - last - MARGIN, before, tail)
        target[pl.ds(top, taller), last:] = tail
    edge = jnp.zeros((8, width), f32)
    pressure[:8] = edge
    pressure[taller + 8 :] = edge
    north[:8] = edge
    north[taller + 8 :] = edge
    for substep in range(SUBSTEPS):
        for o in range(0, taller, 8):
            pressure[8 + o : 16 + o] = surface[o : o + 8] - load[o : o + 8]
        for o in range(0, taller, 8):
            here = pressure[8 + o : 16 + o]
            damp = wet[o : o + 8]
            east[o : o + 8] = damp * (
                east[o : o + 8]
                - STEP * (pltpu.roll(here, width - 1, 1) - pltpu.roll(here, 1, 1))
            )
            north[8 + o : 16 + o] = damp * (
                north[8 + o : 16 + o] - STEP * (pressure[9 + o : 17 + o] - pressure[7 + o : 15 + o])
            )
        for o in range(0, taller, 8):
            flow = east[o : o + 8]
            change = STEP * (pltpu.roll(flow, width - 1, 1) - pltpu.roll(flow, 1, 1)) + STEP * (
                north[9 + o : 17 + o] - north[7 + o : 15 + o]
            )
            surface[o : o + 8] = surface[o : o + 8] - wet[o : o + 8] * change
    loading_out[...] = load[MARGIN : MARGIN + rows, :cols]
    surface_out[...] = surface[MARGIN : MARGIN + rows, :cols]
    east_out[...] = east[MARGIN : MARGIN + rows, :cols]
    north_out[...] = north[8 + MARGIN : 8 + MARGIN + rows, :cols]


def edges_kernel(
    legendre_ref, height_ref, east_ref, north_ref, land_ref, up_ref, down_ref, semaphore
):
    slots, rows, degrees = legendre_ref.shape
    cols = height_ref.shape[1]
    copies = [
        pltpu.make_async_copy(
            legendre_ref.at[:, pl.ds(first, MARGIN), :],
            ref.at[pl.ds(0, slots), :, pl.ds(0, degrees)],
            semaphore.at[at],
        )
        for at, (ref, first) in enumerate(((up_ref, rows - MARGIN), (down_ref, 0)))
    ]
    for copy in copies:
        copy.start()
    for at, source in enumerate((height_ref, east_ref, north_ref, land_ref)):
        up_ref[at, :, degrees : degrees + cols] = source[rows - MARGIN :].astype(f32)
        down_ref[at, :, degrees : degrees + cols] = source[:MARGIN].astype(f32)
    for copy in copies:
        copy.wait()


def sides_kernel(
    height_ref, east_ref, north_ref, land_ref, low_ref, high_ref, tile_ref
):
    rows, cols = height_ref.shape
    taller = rows + 2 * MARGIN
    pieces = []
    for at, source in enumerate((height_ref, east_ref, north_ref, land_ref)):
        for first in (0, cols - MARGIN):
            window = slice(first, first + MARGIN)
            pieces.append(
                jnp.concatenate(
                    [low_ref[at, :, window], source[:, window].astype(f32), high_ref[at, :, window]],
                    axis=0,
                )
            )
    pieces.append(jnp.zeros((taller, 128 - 8 * MARGIN), f32))
    tile_ref[...] = jnp.concatenate(pieces, axis=1)


def struct(shape, dtype=f32):
    return jax.ShapeDtypeStruct(shape, dtype)


def lat_sum_parts(value):
    count = lax.axis_size("lat")
    if count & (count - 1) or count > 4:
        return [lax.psum(value, "lat")]
    return [value] + [
        lax.ppermute(value, "lat", [(i, i ^ step) for i in range(count)])
        for step in range(1, count)
    ]


def shards(height, east_flow, north_flow, legendre, love_numbers, wavenumbers, land_sea):
    rows, cols = height.shape
    slots, _, degrees = legendre.shape
    sectors, bands = lax.axis_size("lon"), lax.axis_size("lat")
    waves = wavenumbers.shape[0]
    period = cols * sectors
    width = -(-(cols + 2 * MARGIN) // 128) * 128
    taller = rows + 2 * MARGIN
    upward = [(i, i + 1) for i in range(bands - 1)]
    downward = [(target, source) for source, target in upward]
    eastward = [(i, (i + 1) % sectors) for i in range(sectors)]
    westward = [(target, source) for source, target in eastward]

    up, down = pl.pallas_call(
        edges_kernel,
        out_shape=[struct((max(4, slots), MARGIN, degrees + width))] * 2,
        in_specs=[pl.BlockSpec(memory_space=pl.ANY)] + [VMEM] * 4,
        out_specs=[VMEM] * 2,
        scratch_shapes=[pltpu.SemaphoreType.DMA((2,))],
        name="edges",
    )(legendre, height, east_flow, north_flow, land_sea)
    low = lax.ppermute(up, "lat", upward)
    high = lax.ppermute(down, "lat", downward)

    first = (lax.axis_index("lon") * cols).astype(jnp.int32).reshape(1)
    column = jnp.broadcast_to(wavenumbers.reshape(sectors, 1, slots), (sectors, 2, slots))
    part, harmonics = pl.pallas_call(
        functools.partial(dft_kernel, period, slots),
        out_shape=[struct((sectors, 2 * slots, rows)), struct((4 * waves, width), bf16)],
        in_specs=[SMEM, VMEM, VMEM],
        out_specs=[VMEM, VMEM],
        scratch_shapes=[pltpu.VMEM((2 * rows, width), bf16)],
        name="dft",
    )(first, column.reshape(2 * waves, 1), height)
    parts = lax.all_to_all(part, "lon", 0, 0, tiled=True)

    spectral = pl.pallas_call(
        analysis_kernel,
        out_shape=struct((2 * slots, degrees)),
        in_specs=[VMEM, VMEM],
        out_specs=VMEM,
        name="analysis",
    )(parts, legendre)
    pieces = lat_sum_parts(spectral)

    def synthesis(*refs):
        synthesis_kernel(refs[: len(pieces)], *refs[len(pieces) :])

    low_rows, high_rows = low[:, :, degrees : degrees + cols], high[:, :, degrees : degrees + cols]
    synth = pl.pallas_call(
        synthesis,
        out_shape=struct((2 * slots, 128)),
        in_specs=[VMEM] * (len(pieces) + 4),
        out_specs=VMEM,
        scratch_shapes=[pltpu.VMEM((2 * slots, degrees), f32)],
        name="synthesis",
    )(*pieces, love_numbers.reshape(1, degrees), legendre, low, high)
    everyone = lax.all_to_all(
        jnp.broadcast_to(synth[None], (sectors, 2 * slots, 128)), "lon", 0, 0, tiled=True
    )

    sides = pl.pallas_call(
        sides_kernel,
        out_shape=struct((taller, 128)),
        in_specs=[VMEM] * 6,
        out_specs=VMEM,
        name="sides",
    )(height, east_flow, north_flow, land_sea, low_rows, high_rows)
    left = lax.ppermute(sides, "lon", eastward)
    right = lax.ppermute(sides, "lon", westward)

    return pl.pallas_call(
        substep_kernel,
        out_shape=[struct((rows, cols))] * 4,
        in_specs=[VMEM] * 10,
        out_specs=[VMEM] * 4,
        scratch_shapes=[
            pltpu.VMEM((taller, width), f32),
            pltpu.VMEM((taller + 16, width), f32),
            pltpu.VMEM((taller, width), f32),
            pltpu.VMEM((taller, width), f32),
            pltpu.VMEM((taller + 16, width), f32),
            pltpu.VMEM((taller, width), f32),
        ],
        name="substeps",
    )(
        everyone,
        harmonics,
        height,
        east_flow,
        north_flow,
        land_sea,
        low_rows,
        high_rows,
        left,
        right,
    )


def solution(mesh):
    return jax.shard_map(
        shards,
        mesh=mesh,
        in_specs=(
            P("lat", "lon"),
            P("lat", "lon"),
            P("lat", "lon"),
            P("lon", "lat", None),
            P(),
            P(),
            P("lat", "lon"),
        ),
        out_specs=(P("lat", "lon"), P("lat", "lon"), P("lat", "lon"), P("lat", "lon")),
        check_vma=False,
    )
```

```python
import functools
import math

import jax
import jax.numpy as jnp
from jax import lax
from jax.experimental import pallas as pl
from jax.experimental.pallas import tpu as pltpu
from jax.sharding import PartitionSpec as P

SUBSTEPS = 4
MARGIN = 2 * SUBSTEPS
STEP = 0.3

f32 = jnp.float32
bf16 = jnp.bfloat16
VMEM = pl.BlockSpec(memory_space=pltpu.VMEM)
HBM = pl.BlockSpec(memory_space=pltpu.HBM)
SMEM = pl.BlockSpec(memory_space=pltpu.SMEM)


LIMIT = pltpu.CompilerParams(vmem_limit_bytes=24 * 2**20)


def split2(x):
    hi = x.astype(bf16)
    lo = (x - hi.astype(f32)).astype(bf16)
    return hi, lo


def harmonic_rows(period, cols, slots, me_ref, waves_ref, harm_ref):
    waves, width = harm_ref.shape[0] // 2, harm_ref.shape[1]
    sectors = waves // (2 * slots)
    me = me_ref[0]
    row = lax.broadcasted_iota(jnp.int32, (2 * slots, 1), 0)
    groups = []
    for core in range(2):
        for chip in range(sectors // 2):
            owner = lax.bitwise_xor(me, 2 * chip + core)
            group = jnp.zeros((2 * slots, 1), jnp.int32)
            for slot in range(slots):
                value = waves_ref[owner * slots + slot]
                group = jnp.where((row == slot) | (row == slots + slot), value, group)
            groups.append(group)
    wave = jnp.concatenate(groups, axis=0)
    start = wave * (me * cols)
    turns = jnp.floor(start.astype(f32) * (1.0 / period)).astype(jnp.int32)
    start = (start - turns * period).astype(f32)
    wave = wave.astype(f32)
    row = lax.broadcasted_iota(jnp.int32, (waves, 1), 0)
    sine = (lax.rem(row, 2 * slots) >= slots).astype(f32)
    offset = 4.0 * start - period * sine
    for tile in range(0, width, 128):
        lane = lax.broadcasted_iota(jnp.int32, (1, 128), 1) + tile
        lane = jnp.where(lane < cols + MARGIN, lane, lane - width).astype(f32)
        product = wave * lane
        product = product - period * jnp.floor(product * (1.0 / period))
        quarter = 4.0 * product + offset
        turn = jnp.floor(quarter * (1.0 / period) + 0.5)
        angle = (quarter - period * turn) * (0.5 * math.pi / period)
        square = angle * angle
        cosine = 1.0 + square * (
            -1.0 / 2 + square * (1.0 / 24 + square * (-1.0 / 720 + square * (1.0 / 40320)))
        )
        sine_of = angle * (
            1.0
            + square
            * (-1.0 / 6 + square * (1.0 / 120 + square * (-1.0 / 5040 + square * (1.0 / 362880))))
        )
        phase = turn - 4.0 * jnp.floor(turn * 0.25)
        odd = (phase == 1.0) | (phase == 3.0)
        value = jnp.where(odd, sine_of, cosine)
        value = jnp.where((phase == 1.0) | (phase == 2.0), -value, value)
        hi, lo = split2(value)
        harm_ref[:waves, tile : tile + 128] = hi
        harm_ref[waves:, tile : tile + 128] = lo


def dft_kernel(
    period,
    slots,
    me_ref,
    waves_ref,
    height_hbm,
    keep_ref,
    send_ref,
    harm_ref,
    height_ref,
    field_ref,
    semaphore,
):
    copy = pltpu.make_async_copy(height_hbm, height_ref, semaphore)
    copy.start()
    rows, cols = height_ref.shape
    waves, width = harm_ref.shape[0] // 2, harm_ref.shape[1]
    harmonic_rows(period, cols, slots, me_ref, waves_ref, harm_ref)
    copy.wait()
    for tile in range(0, width, 128):
        stop = min(cols, tile + 128)
        if stop <= tile:
            block = jnp.zeros((rows, 128), f32)
        elif stop == tile + 128:
            block = height_ref[:, tile : tile + 128]
        else:
            block = jnp.concatenate(
                [height_ref[:, tile:stop], jnp.zeros((rows, tile + 128 - stop), f32)], axis=1
            )
        hi, lo = split2(block)
        field_ref[:rows, tile : tile + 128] = hi
        field_ref[rows:, tile : tile + 128] = lo
    both = lax.dot_general(
        harm_ref[...], field_ref[...], (((1,), (1,)), ((), ())), preferred_element_type=f32
    )
    total = both[:waves] + both[waves:]
    total = (total[:, :rows] + total[:, rows:]) * (1.0 / math.sqrt(period))
    total = jnp.concatenate([total, jnp.zeros((waves, 128 - rows), f32)], axis=1)
    keep_ref[...] = total[: waves // 2].reshape(keep_ref.shape)
    send_ref[...] = total[waves // 2 :].reshape(send_ref.shape)


def analysis_kernel(part_refs, legendre_ref, spectral_ref):
    slots, rows, degrees = legendre_ref.shape
    fourier = part_refs[0][...]
    for ref in part_refs[1:]:
        fourier = fourier + ref[...]
    columns = fourier.T
    for slot in range(slots):
        even = [
            jnp.broadcast_to(columns[o : o + 8, slot : slot + 1], (8, 128))
            for o in range(0, rows, 8)
        ]
        odd = [
            jnp.broadcast_to(columns[o : o + 8, slots + slot : slots + slot + 1], (8, 128))
            for o in range(0, rows, 8)
        ]
        for tile in range(0, degrees, 128):
            first = jnp.zeros((8, 128), f32)
            second = jnp.zeros((8, 128), f32)
            for at, o in enumerate(range(0, rows, 8)):
                block = legendre_ref[slot, o : o + 8, tile : tile + 128]
                first = first + block * even[at]
                second = second + block * odd[at]
            spectral_ref[slot : slot + 1, tile : tile + 128] = jnp.sum(
                first, axis=0, keepdims=True
            )
            spectral_ref[slots + slot : slots + slot + 1, tile : tile + 128] = jnp.sum(
                second, axis=0, keepdims=True
            )


def synthesis_kernel(
    parts_refs, love_ref, legendre_ref, low_ref, high_ref, out_ref, spectral_ref
):
    slots, rows, degrees = legendre_ref.shape
    total = parts_refs[0][...]
    for ref in parts_refs[1:]:
        total = total + ref[...]
    spectral_ref[...] = total * love_ref[...]
    taller = rows + 2 * MARGIN
    lanes = lax.broadcasted_iota(jnp.int32, (8, 128), 1)
    octets = [(low_ref, 0)] + [(legendre_ref, o) for o in range(0, rows, 8)] + [(high_ref, 0)]
    sums = [jnp.zeros((8, 128), f32) for _ in octets]
    for slot in range(slots):
        first = [jnp.zeros((8, 128), f32) for _ in octets]
        second = [jnp.zeros((8, 128), f32) for _ in octets]
        for tile in range(0, degrees, 128):
            even = jnp.broadcast_to(spectral_ref[slot : slot + 1, tile : tile + 128], (8, 128))
            odd = jnp.broadcast_to(
                spectral_ref[slots + slot : slots + slot + 1, tile : tile + 128], (8, 128)
            )
            for at, (ref, o) in enumerate(octets):
                block = ref[slot, o : o + 8, tile : tile + 128]
                first[at] = first[at] + block * even
                second[at] = second[at] + block * odd
        for at in range(len(octets)):
            sums[at] = jnp.where(lanes == slot, jnp.sum(first[at], axis=1, keepdims=True), sums[at])
            sums[at] = jnp.where(
                lanes == slots + slot, jnp.sum(second[at], axis=1, keepdims=True), sums[at]
            )
    column = jnp.concatenate(sums + [jnp.zeros((128 - taller, 128), f32)], axis=0)
    out_ref[...] = column.T[: 2 * slots]


def substep_kernel(
    cols,
    synth_refs,
    harm_ref,
    surface_ref,
    east_ref,
    north_ref,
    wet,
    left_ref,
    right_ref,
    loading_out,
    surface_out,
    east_out,
    north_out,
    load,
    pressure,
    surface,
    east,
    north,
):
    taller, width = surface_ref.shape
    rows = taller - 2 * MARGIN
    waves = harm_ref.shape[0] // 2
    synth = jnp.concatenate(
        [ref[core] for core in range(2) for ref in synth_refs], axis=0
    )
    synth = synth.T * (1.0 / math.sqrt(waves // 2))
    hi, lo = split2(synth[:taller])
    left = jnp.concatenate(
        [jnp.concatenate([hi, hi], axis=1), jnp.concatenate([lo, lo], axis=1)], axis=0
    )
    both = lax.dot_general(
        left, harm_ref[...], (((1,), (0,)), ((), ())), preferred_element_type=f32
    )
    load[...] = both[:taller] + both[taller:]
    last = (cols // 128) * 128
    own = cols - last
    lanes = lax.broadcasted_iota(jnp.int32, (taller, width - last), 1)
    for at, (target, top, source) in enumerate(
        ((surface, 0, surface_ref), (east, 0, east_ref), (north, 8, north_ref), (wet, 0, wet))
    ):
        inside = pl.ds(top, taller)
        if source is not target:
            target[inside, :last] = source[:, :last]
        after = pltpu.roll(right_ref[...], (own - 2 * MARGIN * at) % 128, 1)
        before = pltpu.roll(left_ref[...], (-MARGIN - 2 * MARGIN * at - MARGIN) % 128, 1)
        after = jnp.concatenate([after] * ((width - last) // 128), axis=1)
        before = jnp.concatenate([before] * ((width - last) // 128), axis=1)
        tail = jnp.where((lanes >= own) & (lanes < own + MARGIN), after, source[:, last:])
        tail = jnp.where(lanes >= width - last - MARGIN, before, tail)
        target[inside, last:] = tail
    edge = jnp.zeros((8, width), f32)
    pressure[:8] = edge
    pressure[taller + 8 :] = edge
    north[:8] = edge
    north[taller + 8 :] = edge
    for substep in range(SUBSTEPS):
        for o in range(0, taller, 8):
            pressure[8 + o : 16 + o] = surface[o : o + 8] - load[o : o + 8]
        for o in range(0, taller, 8):
            here = pressure[8 + o : 16 + o]
            damp = wet[o : o + 8]
            east[o : o + 8] = damp * (
                east[o : o + 8]
                - STEP * (pltpu.roll(here, width - 1, 1) - pltpu.roll(here, 1, 1))
            )
            north[8 + o : 16 + o] = damp * (
                north[8 + o : 16 + o] - STEP * (pressure[9 + o : 17 + o] - pressure[7 + o : 15 + o])
            )
        for o in range(0, taller, 8):
            flow = east[o : o + 8]
            change = STEP * (pltpu.roll(flow, width - 1, 1) - pltpu.roll(flow, 1, 1)) + STEP * (
                north[9 + o : 17 + o] - north[7 + o : 15 + o]
            )
            surface[o : o + 8] = surface[o : o + 8] - wet[o : o + 8] * change
    loading_out[...] = load[MARGIN : MARGIN + rows, :cols]
    surface_out[...] = surface[MARGIN : MARGIN + rows, :cols]
    east_out[...] = east[MARGIN : MARGIN + rows, :cols]
    north_out[...] = north[8 + MARGIN : 8 + MARGIN + rows, :cols]


def edges_kernel(
    legendre_hbm,
    height_hbm,
    east_hbm,
    north_hbm,
    land_hbm,
    up_ref,
    down_ref,
    flows,
    lands,
    semaphores,
):
    slots, rows, degrees = legendre_hbm.shape
    cols = height_hbm.shape[1]
    copies = []
    for side, (ref, first) in enumerate(((up_ref, rows - MARGIN), (down_ref, 0))):
        band = pl.ds(first, MARGIN)
        copies.append((height_hbm.at[band], flows.at[side, 0]))
        copies.append((east_hbm.at[band], flows.at[side, 1]))
        copies.append((north_hbm.at[band], flows.at[side, 2]))
        copies.append((land_hbm.at[band], lands.at[side]))
        copies.append((legendre_hbm.at[:, band], ref.at[pl.ds(0, slots), :, pl.ds(0, degrees)]))
    copies = [
        pltpu.make_async_copy(source, target, semaphores.at[at])
        for at, (source, target) in enumerate(copies)
    ]
    for copy in copies:
        copy.start()
    for copy in copies:
        copy.wait()
    for side, ref in enumerate((up_ref, down_ref)):
        for at in range(3):
            ref[at, :, degrees : degrees + cols] = flows[side, at]
        ref[3, :, degrees : degrees + cols] = lands[side].astype(f32)


def windows_kernel(
    base,
    height_hbm,
    east_hbm,
    north_hbm,
    land_hbm,
    low_ref,
    high_ref,
    surface_ref,
    east_ref,
    north_ref,
    wet_ref,
    tile_ref,
    fields,
    land,
    semaphores,
):
    rows, cols = height_hbm.shape
    width = surface_ref.shape[1]
    taller = rows + 2 * MARGIN
    last = (cols // 128) * 128
    copies = [
        pltpu.make_async_copy(source, target, semaphores.at[at])
        for at, (source, target) in enumerate(
            (
                (height_hbm, fields.at[0]),
                (east_hbm, fields.at[1]),
                (north_hbm, fields.at[2]),
                (land_hbm, land),
            )
        )
    ]
    for copy in copies:
        copy.start()
    pieces = []
    for at, target in enumerate((surface_ref, east_ref, north_ref, wet_ref)):
        copies[at].wait()
        source = fields.at[at] if at < 3 else land
        target[:MARGIN, :last] = low_ref[at, :, base : base + last]
        target[MARGIN : MARGIN + rows, :last] = source[:, :last].astype(f32)
        target[MARGIN + rows :, :last] = high_ref[at, :, base : base + last]
        tail = jnp.concatenate(
            [
                low_ref[at, :, base + last : base + cols],
                source[:, last:].astype(f32),
                high_ref[at, :, base + last : base + cols],
            ],
            axis=0,
        )
        target[:, last:] = jnp.concatenate(
            [tail, jnp.zeros((taller, width - cols), f32)], axis=1
        )
        pieces.append(target[:, :MARGIN])
        pieces.append(target[:, cols - MARGIN : cols])
    pieces.append(jnp.zeros((taller, 128 - 8 * MARGIN), f32))
    tile_ref[...] = jnp.concatenate(pieces, axis=1)


def in_hbm(x):
    return pltpu.with_memory_space_constraint(x, pltpu.HBM)


def struct(shape, dtype=f32):
    return jax.ShapeDtypeStruct(shape, dtype)


def lat_sum_parts(value):
    count = lax.axis_size("lat")
    if count & (count - 1) or count > 4:
        return [lax.psum(value, "lat")]
    return [value] + [
        lax.ppermute(value, "lat", [(i, i ^ step) for i in range(count)])
        for step in range(1, count)
    ]


def shards(height, east_flow, north_flow, legendre, love_numbers, wavenumbers, land_sea):
    rows, cols = height.shape
    slots, _, degrees = legendre.shape
    sectors, bands = lax.axis_size("lon"), lax.axis_size("lat")
    waves = wavenumbers.shape[0]
    period = cols * sectors
    width = -(-(cols + 2 * MARGIN) // 128) * 128
    taller = rows + 2 * MARGIN
    upward = [(i, i + 1) for i in range(bands - 1)]
    downward = [(target, source) for source, target in upward]
    eastward = [(i, (i + 1) % sectors) for i in range(sectors)]
    westward = [(target, source) for source, target in eastward]

    chips = sectors // 2
    pair = [(i, i ^ 1) for i in range(sectors)]
    chain = [[(i, i ^ (2 * chip)) for i in range(sectors)] for chip in range(1, chips)]
    me = lax.axis_index("lon").astype(jnp.int32).reshape(1)
    keep, send, harmonics = pl.pallas_call(
        functools.partial(dft_kernel, period, slots),
        out_shape=[struct((chips, 2 * slots, 128))] * 2 + [struct((4 * waves, width), bf16)],
        in_specs=[SMEM, SMEM, HBM],
        out_specs=[VMEM] * 3,
        scratch_shapes=[
            pltpu.VMEM((rows, cols), f32),
            pltpu.VMEM((2 * rows, width), bf16),
            pltpu.SemaphoreType.DMA,
        ],
        name="dft",
        compiler_params=LIMIT,
    )(me, wavenumbers, in_hbm(height))
    part = keep + lax.ppermute(send, "lon", pair)
    part, legendre_later = lax.optimization_barrier((part, legendre))
    up, down = pl.pallas_call(
        edges_kernel,
        out_shape=[struct((max(4, slots), MARGIN, degrees + width))] * 2,
        in_specs=[HBM] * 5,
        out_specs=[VMEM] * 2,
        scratch_shapes=[
            pltpu.VMEM((2, 3, MARGIN, cols), f32),
            pltpu.VMEM((2, MARGIN, cols), jnp.int32),
            pltpu.SemaphoreType.DMA((10,)),
        ],
        name="edges",
        compiler_params=LIMIT,
    )(*map(in_hbm, (legendre_later, height, east_flow, north_flow, land_sea)))
    low = lax.ppermute(up, "lat", upward)
    high = lax.ppermute(down, "lat", downward)

    parts = [part[0]] + [
        lax.ppermute(part[chip], "lon", links) for chip, links in enumerate(chain, 1)
    ]

    def analysis(*refs):
        analysis_kernel(refs[:chips], *refs[chips:])

    spectral = pl.pallas_call(
        analysis,
        out_shape=struct((2 * slots, degrees)),
        in_specs=[VMEM] * (chips + 1),
        out_specs=VMEM,
        name="analysis",
        compiler_params=LIMIT,
    )(*parts, legendre)
    pieces = lat_sum_parts(spectral)

    def synthesis(*refs):
        synthesis_kernel(refs[: len(pieces)], *refs[len(pieces) :])

    synth = pl.pallas_call(
        synthesis,
        out_shape=struct((2 * slots, 128)),
        in_specs=[VMEM] * (len(pieces) + 4),
        out_specs=VMEM,
        scratch_shapes=[pltpu.VMEM((2 * slots, degrees), f32)],
        name="synthesis",
        compiler_params=LIMIT,
    )(*pieces, love_numbers.reshape(1, degrees), legendre, low, high)
    both = jnp.stack([synth, lax.ppermute(synth, "lon", pair)])
    everyone = [both] + [lax.ppermute(both, "lon", links) for links in chain]

    surface, east, north, wet, sides = pl.pallas_call(
        functools.partial(windows_kernel, degrees),
        out_shape=[struct((taller, width))] * 4 + [struct((taller, 128))],
        in_specs=[HBM] * 4 + [VMEM] * 2,
        out_specs=[VMEM] * 5,
        scratch_shapes=[
            pltpu.VMEM((3, rows, cols), f32),
            pltpu.VMEM((rows, cols), jnp.int32),
            pltpu.SemaphoreType.DMA((4,)),
        ],
        name="windows",
        compiler_params=LIMIT,
    )(*map(in_hbm, (height, east_flow, north_flow, land_sea)), low, high)
    left = lax.ppermute(sides, "lon", eastward)
    right = lax.ppermute(sides, "lon", westward)

    def substeps(*refs):
        substep_kernel(cols, refs[:chips], *refs[chips:])

    return pl.pallas_call(
        substeps,
        out_shape=[struct((rows, cols))] * 4,
        in_specs=[VMEM] * (chips + 7),
        out_specs=[VMEM] * 4,
        scratch_shapes=[
            pltpu.VMEM((taller, width), f32),
            pltpu.VMEM((taller + 16, width), f32),
            pltpu.VMEM((taller, width), f32),
            pltpu.VMEM((taller, width), f32),
            pltpu.VMEM((taller + 16, width), f32),
        ],
        name="substeps",
        compiler_params=LIMIT,
    )(*everyone, harmonics, surface, east, north, wet, left, right)


def solution(mesh):
    return jax.shard_map(
        shards,
        mesh=mesh,
        in_specs=(
            P("lat", "lon"),
            P("lat", "lon"),
            P("lat", "lon"),
            P("lon", "lat", None),
            P(),
            P(),
            P("lat", "lon"),
        ),
        out_specs=(P("lat", "lon"), P("lat", "lon"), P("lat", "lon"), P("lat", "lon")),
        check_vma=False,
    )
```

```python
import functools
import math

import jax
import jax.numpy as jnp
from jax import lax
from jax.experimental import pallas as pl
from jax.experimental.pallas import tpu as pltpu
from jax.sharding import PartitionSpec as P

SUBSTEPS = 4
MARGIN = 2 * SUBSTEPS
STEP = 0.3

f32 = jnp.float32
bf16 = jnp.bfloat16
VMEM = pl.BlockSpec(memory_space=pltpu.VMEM)
HBM = pl.BlockSpec(memory_space=pltpu.HBM)
SMEM = pl.BlockSpec(memory_space=pltpu.SMEM)
LIMIT = pltpu.CompilerParams(vmem_limit_bytes=24 * 2**20)


def struct(shape, dtype=f32):
    return jax.ShapeDtypeStruct(shape, dtype)


def in_hbm(*arrays):
    return [pltpu.with_memory_space_constraint(x, pltpu.HBM) for x in arrays]


def split2(x):
    hi = x.astype(bf16)
    lo = (x - hi.astype(f32)).astype(bf16)
    return hi, lo


def owner(me, sectors, core, shift):
    chips = sectors // 2
    return 2 * lax.rem(me // 2 + shift, chips) + lax.bitwise_xor(lax.rem(me, 2), core)


def harmonic_rows(period, cols, slots, me, waves_ref, harm_ref):
    waves, width = harm_ref.shape[0] // 2, harm_ref.shape[1]
    sectors = waves // (2 * slots)
    row = lax.broadcasted_iota(jnp.int32, (2 * slots, 1), 0)
    groups = []
    for core in range(2):
        for shift in range(sectors // 2):
            first = owner(me, sectors, core, shift) * slots
            group = jnp.zeros((2 * slots, 1), jnp.int32)
            for slot in range(slots):
                value = waves_ref[first + slot]
                group = jnp.where((row == slot) | (row == slots + slot), value, group)
            groups.append(group)
    wave = jnp.concatenate(groups, axis=0)
    start = wave * (me * cols)
    turns = jnp.floor(start.astype(f32) * (1.0 / period)).astype(jnp.int32)
    start = (start - turns * period).astype(f32)
    wave = wave.astype(f32)
    row = lax.broadcasted_iota(jnp.int32, (waves, 1), 0)
    sine = (lax.rem(row, 2 * slots) >= slots).astype(f32)
    offset = 4.0 * start - period * sine
    for tile in range(0, width, 128):
        lane = lax.broadcasted_iota(jnp.int32, (1, 128), 1) + tile
        lane = jnp.where(lane < cols + MARGIN, lane, lane - width).astype(f32)
        product = wave * lane
        product = product - period * jnp.floor(product * (1.0 / period))
        quarter = 4.0 * product + offset
        turn = jnp.floor(quarter * (1.0 / period) + 0.5)
        angle = (quarter - period * turn) * (0.5 * math.pi / period)
        square = angle * angle
        cosine = 1.0 + square * (
            -1.0 / 2 + square * (1.0 / 24 + square * (-1.0 / 720 + square * (1.0 / 40320)))
        )
        sine_of = angle * (
            1.0
            + square
            * (-1.0 / 6 + square * (1.0 / 120 + square * (-1.0 / 5040 + square * (1.0 / 362880))))
        )
        phase = turn - 4.0 * jnp.floor(turn * 0.25)
        odd = (phase == 1.0) | (phase == 3.0)
        value = jnp.where(odd, sine_of, cosine)
        value = jnp.where((phase == 1.0) | (phase == 2.0), -value, value)
        hi, lo = split2(value)
        harm_ref[:waves, tile : tile + 128] = hi
        harm_ref[waves:, tile : tile + 128] = lo


def transform_kernel(
    period,
    slots,
    me_ref,
    waves_hbm,
    height_hbm,
    east_hbm,
    north_hbm,
    land_hbm,
    legendre_hbm,
    keep_ref,
    send_ref,
    bands_ref,
    legendre_ref,
    waves_ref,
    height_ref,
    east_ref,
    north_ref,
    land_ref,
    harm_ref,
    field_ref,
    semaphores,
):
    rows, cols = height_ref.shape
    waves, width = harm_ref.shape[0] // 2, harm_ref.shape[1]
    copies = [
        pltpu.make_async_copy(source, target, semaphores.at[at])
        for at, (source, target) in enumerate(
            (
                (waves_hbm, waves_ref),
                (height_hbm, height_ref),
                (east_hbm, east_ref),
                (north_hbm, north_ref),
                (land_hbm, land_ref),
                (legendre_hbm, legendre_ref),
            )
        )
    ]
    for copy in copies:
        copy.start()
    copies[0].wait()
    harmonic_rows(period, cols, slots, me_ref[0], waves_ref, harm_ref)
    copies[1].wait()
    for tile in range(0, width, 128):
        stop = min(cols, tile + 128)
        if stop <= tile:
            block = jnp.zeros((rows, 128), f32)
        elif stop == tile + 128:
            block = height_ref[:, tile : tile + 128]
        else:
            block = jnp.concatenate(
                [height_ref[:, tile:stop], jnp.zeros((rows, tile + 128 - stop), f32)], axis=1
            )
        hi, lo = split2(block)
        field_ref[:rows, tile : tile + 128] = hi
        field_ref[rows:, tile : tile + 128] = lo
    both = lax.dot_general(
        harm_ref[...], field_ref[...], (((1,), (1,)), ((), ())), preferred_element_type=f32
    )
    total = both[:waves] + both[waves:]
    total = (total[:, :rows] + total[:, rows:]) * (1.0 / math.sqrt(period))
    total = jnp.concatenate([total, jnp.zeros((waves, 128 - rows), f32)], axis=1)
    keep_ref[...] = total[: waves // 2].reshape(keep_ref.shape)
    send_ref[: waves // 2] = total[waves // 2 :]
    for copy in copies[2:5]:
        copy.wait()
    pieces = []
    for at, ref in enumerate((height_ref, east_ref, north_ref, land_ref)):
        pieces += [ref[:, :MARGIN].astype(f32), ref[:, cols - MARGIN :].astype(f32)]
        bands_ref[0, at, :, :cols] = ref[rows - MARGIN :].astype(f32)
        bands_ref[1, at, :, :cols] = ref[:MARGIN].astype(f32)
        if cols < width:
            bands_ref[:, at, :, cols:] = jnp.zeros((2, MARGIN, width - cols), f32)
    half = rows // 2
    send_ref[waves // 2 :] = jnp.concatenate(
        [piece[:half] for piece in pieces] + [piece[half:] for piece in pieces], axis=1
    )
    copies[5].wait()


def mix_kernel(keep_ref, recv_ref, own_ref, *send_refs):
    chips, group, _ = keep_ref.shape
    own_ref[...] = keep_ref[0] + recv_ref[:group]
    for shift, ref in enumerate(send_refs, 1):
        ref[:group] = keep_ref[shift] + recv_ref[shift * group : (shift + 1) * group]
        if ref.shape[0] > group:
            ref[group:] = recv_ref[chips * group :]


def analysis_kernel(
    cols,
    me_ref,
    part_refs,
    core_ref,
    bands_ref,
    legendre_ref,
    spectral_ref,
    even_ref,
    odd_ref,
):
    slots, rows, degrees = legendre_ref.shape
    width = bands_ref.shape[3]
    ahead = even_ref.shape[1] - 4 * width
    fourier = part_refs[0][...]
    for ref in part_refs[1:]:
        fourier = fourier + ref[: 2 * slots]
    columns = fourier.T
    for slot in range(slots):
        even = [
            jnp.broadcast_to(columns[o : o + 8, slot : slot + 1], (8, 128))
            for o in range(0, rows, 8)
        ]
        odd = [
            jnp.broadcast_to(columns[o : o + 8, slots + slot : slots + slot + 1], (8, 128))
            for o in range(0, rows, 8)
        ]
        for tile in range(0, degrees, 128):
            first = jnp.zeros((8, 128), f32)
            second = jnp.zeros((8, 128), f32)
            for at, o in enumerate(range(0, rows, 8)):
                block = legendre_ref[slot, o : o + 8, tile : tile + 128]
                first = first + block * even[at]
                second = second + block * odd[at]
            spectral_ref[slot : slot + 1, tile : tile + 128] = jnp.sum(
                first, axis=0, keepdims=True
            )
            spectral_ref[slots + slot : slots + slot + 1, tile : tile + 128] = jnp.sum(
                second, axis=0, keepdims=True
            )
    if ahead:
        even_ref[:, :ahead] = spectral_ref[...]
        odd_ref[:, :ahead] = spectral_ref[...]
    last = (cols // 128) * 128
    chips = len(part_refs)
    left, right = side_tiles(
        me_ref[0], 2 * slots, chips, core_ref, part_refs[1], part_refs[-1]
    )
    half = rows // 2
    is_even = lax.rem(me_ref[1], 2) == 0
    for at in range(4):
        ends = []
        for side, begin in enumerate((half - MARGIN, 0)):
            before, after = left[begin : begin + MARGIN], right[begin : begin + MARGIN]
            if side == 0:
                before, after = pltpu.roll(before, 64, 1), pltpu.roll(after, 64, 1)
            tail = bands_ref[side, at, :, last:]
            ends.append(
                [bands_ref[side, at, :, :last], with_sides(tail, before, after, cols - last, at)]
            )
        place = ahead + at * width
        for up, down, begin, end in zip(*ends, (0, last), (last, width)):
            even_ref[:, place + begin : place + end] = jnp.where(is_even, up, down)
            odd_ref[:, place + begin : place + end] = jnp.where(is_even, down, up)


def synthesis_kernel(parts_refs, love_ref, legendre_ref, out_ref, spectral_ref):
    slots, rows, degrees = legendre_ref.shape
    total = parts_refs[0][...]
    for ref in parts_refs[1:]:
        total = total + ref[:, :degrees]
    spectral_ref[...] = total * love_ref[...]
    lanes = lax.broadcasted_iota(jnp.int32, (8, 128), 1)
    octets = range(0, rows, 8)
    sums = [jnp.zeros((8, 128), f32) for _ in octets]
    for slot in range(slots):
        first = [jnp.zeros((8, 128), f32) for _ in octets]
        second = [jnp.zeros((8, 128), f32) for _ in octets]
        for tile in range(0, degrees, 128):
            even = jnp.broadcast_to(spectral_ref[slot : slot + 1, tile : tile + 128], (8, 128))
            odd = jnp.broadcast_to(
                spectral_ref[slots + slot : slots + slot + 1, tile : tile + 128], (8, 128)
            )
            for at, o in enumerate(octets):
                block = legendre_ref[slot, o : o + 8, tile : tile + 128]
                first[at] = first[at] + block * even
                second[at] = second[at] + block * odd
        for at in range(len(octets)):
            sums[at] = jnp.where(lanes == slot, jnp.sum(first[at], axis=1, keepdims=True), sums[at])
            sums[at] = jnp.where(
                lanes == slots + slot, jnp.sum(second[at], axis=1, keepdims=True), sums[at]
            )
    column = jnp.concatenate(sums + [jnp.zeros((128 - rows, 128), f32)], axis=0)
    out_ref[...] = jnp.broadcast_to(column.T[None, : 2 * slots], out_ref.shape)


def side_tiles(me, group, chips, core_ref, west_ref, east_ref):
    first = lax.rem(me, 2) == 0
    other = core_ref[chips * group :]
    left = jnp.where(first, west_ref[group:], other)
    right = jnp.where(first, other, east_ref[group:])
    return left, right


def with_sides(tail, left, right, own, at):
    lanes = lax.broadcasted_iota(jnp.int32, tail.shape, 1)
    after = pltpu.roll(right, (own - 2 * MARGIN * at) % 128, 1)
    before = pltpu.roll(left, (-MARGIN - 2 * MARGIN * at - MARGIN) % 128, 1)
    repeat = tail.shape[1] // 128
    after = jnp.concatenate([after] * repeat, axis=1)
    before = jnp.concatenate([before] * repeat, axis=1)
    tail = jnp.where((lanes >= own) & (lanes < own + MARGIN), after, tail)
    return jnp.where(lanes >= tail.shape[1] - MARGIN, before, tail)


def windows_kernel(
    period,
    slots,
    chips,
    bands,
    me_ref,
    waves_hbm,
    height_hbm,
    east_hbm,
    north_hbm,
    land_hbm,
    core_ref,
    west_ref,
    east_ref,
    even_ref,
    odd_ref,
    surface_win,
    east_win,
    north_win,
    wet_win,
    harm_ref,
    waves_ref,
    fields,
    land,
    semaphores,
):
    rows, cols = height_hbm.shape
    width = harm_ref.shape[1]
    last = (cols // 128) * 128
    copies = [
        pltpu.make_async_copy(source, target, semaphores.at[at])
        for at, (source, target) in enumerate(
            (
                (height_hbm, fields.at[0]),
                (east_hbm, fields.at[1]),
                (north_hbm, fields.at[2]),
                (land_hbm, land),
                (waves_hbm, waves_ref),
            )
        )
    ]
    for copy in copies:
        copy.start()
    copies[4].wait()
    harmonic_rows(period, cols, slots, me_ref[0], waves_ref, harm_ref)
    left, right = side_tiles(me_ref[0], 2 * slots, chips, core_ref, west_ref, east_ref)
    left = jnp.concatenate([left, pltpu.roll(left, 64, 1)], axis=0)
    right = jnp.concatenate([right, pltpu.roll(right, 64, 1)], axis=0)
    band = me_ref[1]
    is_even = lax.rem(band, 2) == 0
    for at, target in enumerate((surface_win, east_win, north_win, wet_win)):
        copies[at].wait()
        field = fields.at[at] if at < 3 else land
        place = even_ref.shape[1] - (4 - at) * width
        even, odd = even_ref[:, place : place + width], odd_ref[:, place : place + width]
        target[:MARGIN] = jnp.where(band > 0, jnp.where(is_even, odd, even), 0.0)
        target[MARGIN + rows :] = jnp.where(
            band < bands - 1, jnp.where(is_even, even, odd), 0.0
        )
        target[MARGIN : MARGIN + rows, :last] = field[:, :last].astype(f32)
        tail = jnp.concatenate(
            [field[:, last:].astype(f32), jnp.zeros((rows, width - cols), f32)], axis=1
        )
        target[MARGIN : MARGIN + rows, last:] = with_sides(tail, left, right, cols - last, at)


def substep_kernel(
    sectors,
    bands,
    me_ref,
    synth_ref,
    harm_ref,
    surface_win,
    east_win,
    north_win,
    wet,
    loading_hbm,
    surface_hbm,
    east_hbm,
    north_hbm,
    load,
    pressure,
    surface,
    east,
    north,
    loading_out,
    surface_out,
    east_out,
    north_out,
    semaphores,
):
    rows, cols = loading_hbm.shape
    taller, width = wet.shape
    waves = harm_ref.shape[0] // 2
    me, band = me_ref[0], me_ref[1]
    below, above = jnp.maximum(band - 1, 0), jnp.minimum(band + 1, bands - 1)
    lanes = lax.broadcasted_iota(jnp.int32, synth_ref.shape[1:], 1)
    groups = []
    for core in range(2):
        for shift in range(sectors // 2):
            sector = owner(me, sectors, core, shift)
            low = jnp.where(band > 0, synth_ref[below * sectors + sector], 0.0)
            high = jnp.where(band < bands - 1, synth_ref[above * sectors + sector], 0.0)
            group = pltpu.roll(synth_ref[band * sectors + sector], MARGIN, 1)
            group = jnp.where(lanes < MARGIN, pltpu.roll(low, (MARGIN - rows) % 128, 1), group)
            high = pltpu.roll(high, MARGIN + rows, 1)
            groups.append(jnp.where(lanes >= MARGIN + rows, high, group))
    synth = jnp.concatenate(groups, axis=0).T * (1.0 / math.sqrt(waves // 2))
    hi, lo = split2(synth[:taller])
    left = jnp.concatenate(
        [jnp.concatenate([hi, hi], axis=1), jnp.concatenate([lo, lo], axis=1)], axis=0
    )
    both = lax.dot_general(
        left, harm_ref[...], (((1,), (0,)), ((), ())), preferred_element_type=f32
    )
    load[...] = both[:taller] + both[taller:]
    copies = [
        pltpu.make_async_copy(source, target, semaphores.at[at])
        for at, (source, target) in enumerate(
            (
                (loading_out, loading_hbm),
                (surface_out, surface_hbm),
                (east_out, east_hbm),
                (north_out, north_hbm),
            )
        )
    ]
    inner = pl.ds(MARGIN, rows)
    loading_out[...] = load[inner, :cols]
    copies[0].start()
    edge = jnp.zeros((8, width), f32)
    pressure[:8] = edge
    pressure[taller + 8 :] = edge
    north[:8] = edge
    north[taller + 8 :] = edge
    for o in range(0, taller, 8):
        pressure[8 + o : 16 + o] = surface_win[o : o + 8] - load[o : o + 8]
    for substep in range(SUBSTEPS):
        final = substep == SUBSTEPS - 1
        for o in range(0, taller, 8):
            here = pressure[8 + o : 16 + o]
            damp = wet[o : o + 8]
            flow = east_win[o : o + 8] if substep == 0 else east[o : o + 8]
            flow = damp * (
                flow - STEP * (pltpu.roll(here, width - 1, 1) - pltpu.roll(here, 1, 1))
            )
            east[o : o + 8] = flow
            other = north_win[o : o + 8] if substep == 0 else north[8 + o : 16 + o]
            other = damp * (
                other - STEP * (pressure[9 + o : 17 + o] - pressure[7 + o : 15 + o])
            )
            north[8 + o : 16 + o] = other
            if final and MARGIN <= o < MARGIN + rows:
                east_out[o - MARGIN : o - MARGIN + 8] = flow[:, :cols]
                north_out[o - MARGIN : o - MARGIN + 8] = other[:, :cols]
        if final:
            copies[2].start()
            copies[3].start()
        for o in range(0, taller, 8):
            if final and not MARGIN <= o < MARGIN + rows:
                continue
            flow = east[o : o + 8]
            change = STEP * (pltpu.roll(flow, width - 1, 1) - pltpu.roll(flow, 1, 1)) + STEP * (
                north[9 + o : 17 + o] - north[7 + o : 15 + o]
            )
            level = surface_win[o : o + 8] if substep == 0 else surface[o : o + 8]
            level = level - wet[o : o + 8] * change
            if final:
                surface_out[o - MARGIN : o - MARGIN + 8] = level[:, :cols]
            else:
                surface[o : o + 8] = level
                pressure[8 + o : 16 + o] = level - load[o : o + 8]
    copies[1].start()
    for copy in copies:
        copy.wait()


def shards(height, east_flow, north_flow, legendre, love_numbers, wavenumbers, land_sea):
    rows, cols = height.shape
    slots, _, degrees = legendre.shape
    sectors, bands = lax.axis_size("lon"), lax.axis_size("lat")
    chips = sectors // 2
    waves = wavenumbers.shape[0]
    period = cols * sectors
    width = -(-(cols + 2 * MARGIN) // 128) * 128
    taller = rows + 2 * MARGIN
    group, half = 2 * slots, rows // 2
    DMA = pltpu.SemaphoreType.DMA
    fields = (height, east_flow, north_flow, land_sea)
    me = jnp.stack([lax.axis_index("lon"), lax.axis_index("lat")]).astype(jnp.int32)

    keep, send, bands_rows, legendre = pl.pallas_call(
        functools.partial(transform_kernel, period, slots),
        out_shape=[
            struct((chips, group, 128)),
            struct((chips * group + half, 128)),
            struct((2, 4, MARGIN, width)),
            struct(legendre.shape),
        ],
        in_specs=[SMEM] + [HBM] * 6,
        out_specs=[VMEM] * 4,
        scratch_shapes=[
            pltpu.SMEM((waves,), jnp.int32),
            pltpu.VMEM((rows, cols), f32),
            pltpu.VMEM((rows, cols), f32),
            pltpu.VMEM((rows, cols), f32),
            pltpu.VMEM((rows, cols), jnp.int32),
            pltpu.VMEM((4 * waves, width), bf16),
            pltpu.VMEM((2 * rows, width), bf16),
            DMA((6,)),
        ],
        name="transform",
        compiler_params=LIMIT,
    )(me, *in_hbm(wavenumbers, *fields, legendre))
    core = lax.ppermute(send, "lon", [(i, i ^ 1) for i in range(sectors)])
    neighbours = (1, chips - 1)
    own, *outgoing = pl.pallas_call(
        mix_kernel,
        out_shape=[struct((group, 128))]
        + [
            struct((group + (half if shift in neighbours else 0), 128))
            for shift in range(1, chips)
        ],
        in_specs=[VMEM] * 2,
        out_specs=[VMEM] * chips,
        name="mix",
        compiler_params=LIMIT,
    )(keep, core)
    arrived = [
        lax.ppermute(
            block, "lon", [(i, (i + 2 * shift) % sectors) for i in range(sectors)]
        )
        for shift, block in enumerate(outgoing, 1)
    ]
    sides = (core, arrived[0], arrived[-1])

    def analysis(me_ref, *refs):
        analysis_kernel(cols, me_ref, refs[:chips], *refs[chips:])

    together = bands == 4
    message = 4 * width + (degrees if together else 0)
    spectral, even, odd = pl.pallas_call(
        analysis,
        out_shape=[struct((group, degrees))] + [struct((MARGIN, message))] * 2,
        in_specs=[SMEM] + [VMEM] * (chips + 3),
        out_specs=[VMEM] * 3,
        name="analysis",
        compiler_params=LIMIT,
    )(me, own, *arrived, core, bands_rows, legendre)
    if together:
        even, odd, across = [
            lax.ppermute(block, "lat", [(i, i ^ step) for i in range(bands)])
            for block, step in ((even, 1), (odd, 3), (spectral, 2))
        ]
        pieces = [spectral, even, odd, across]
    else:
        links = [[(i, i + 1) for i in range(first, bands - 1, 2)] for first in (0, 1)]
        even, odd = [
            lax.ppermute(block, "lat", pairs + [(j, i) for i, j in pairs])
            for block, pairs in zip((even, odd), links)
        ]
        pieces = [lax.psum(spectral, "lat")]

    def synthesis(*refs):
        synthesis_kernel(refs[: len(pieces)], *refs[len(pieces) :])

    synth = pl.pallas_call(
        synthesis,
        out_shape=struct((bands * sectors, group, 128)),
        in_specs=[VMEM] * (len(pieces) + 2),
        out_specs=VMEM,
        scratch_shapes=[pltpu.VMEM((group, degrees), f32)],
        name="synthesis",
        compiler_params=LIMIT,
    )(*pieces, love_numbers.reshape(1, degrees), legendre)
    everyone = lax.all_to_all(synth, ("lat", "lon"), 0, 0, tiled=True)

    *windows, harmonics = pl.pallas_call(
        functools.partial(windows_kernel, period, slots, chips, bands),
        out_shape=[struct((taller, width))] * 4 + [struct((4 * waves, width), bf16)],
        in_specs=[SMEM] + [HBM] * 5 + [VMEM] * 5,
        out_specs=[VMEM] * 5,
        scratch_shapes=[
            pltpu.SMEM((waves,), jnp.int32),
            pltpu.VMEM((3, rows, cols), f32),
            pltpu.VMEM((rows, cols), jnp.int32),
            DMA((5,)),
        ],
        name="windows",
        compiler_params=LIMIT,
    )(me, *in_hbm(wavenumbers, *fields), *sides, even, odd)

    return pl.pallas_call(
        functools.partial(substep_kernel, sectors, bands),
        out_shape=[struct((rows, cols))] * 4,
        in_specs=[SMEM] + [VMEM] * 6,
        out_specs=[HBM] * 4,
        scratch_shapes=[
            pltpu.VMEM((taller, width), f32),
            pltpu.VMEM((taller + 16, width), f32),
            pltpu.VMEM((taller, width), f32),
            pltpu.VMEM((taller, width), f32),
            pltpu.VMEM((taller + 16, width), f32),
        ]
        + [pltpu.VMEM((rows, cols), f32)] * 4
        + [DMA((4,))],
        name="substeps",
        compiler_params=LIMIT,
    )(me, everyone, harmonics, *windows)


def solution(mesh):
    return jax.shard_map(
        shards,
        mesh=mesh,
        in_specs=(
            P("lat", "lon"),
            P("lat", "lon"),
            P("lat", "lon"),
            P("lon", "lat", None),
            P(),
            P(),
            P("lat", "lon"),
        ),
        out_specs=(P("lat", "lon"), P("lat", "lon"), P("lat", "lon"), P("lat", "lon")),
        check_vma=False,
    )
```

```python
import functools
import math

import jax
import jax.numpy as jnp
from jax import lax
from jax.experimental import pallas as pl
from jax.experimental.pallas import tpu as pltpu
from jax.sharding import PartitionSpec as P

SUBSTEPS = 4
MARGIN = 2 * SUBSTEPS
STEP = 0.3

f32 = jnp.float32
bf16 = jnp.bfloat16
VMEM = pl.BlockSpec(memory_space=pltpu.VMEM)
HBM = pl.BlockSpec(memory_space=pltpu.HBM)
SMEM = pl.BlockSpec(memory_space=pltpu.SMEM)
LIMIT = pltpu.CompilerParams(vmem_limit_bytes=24 * 2**20)


def struct(shape, dtype=f32):
    return jax.ShapeDtypeStruct(shape, dtype)


def in_hbm(*arrays):
    return [pltpu.with_memory_space_constraint(x, pltpu.HBM) for x in arrays]


def split2(x):
    hi = x.astype(bf16)
    lo = (x - hi.astype(f32)).astype(bf16)
    return hi, lo


def owner(me, sectors, core, shift):
    chips = sectors // 2
    return 2 * lax.rem(me // 2 + shift, chips) + lax.bitwise_xor(lax.rem(me, 2), core)


def harmonic_rows(period, cols, slots, me, waves_ref, harm_ref):
    waves, width = harm_ref.shape[0] // 2, harm_ref.shape[1]
    sectors = waves // (2 * slots)
    row = lax.broadcasted_iota(jnp.int32, (2 * slots, 1), 0)
    groups = []
    for core in range(2):
        for shift in range(sectors // 2):
            first = owner(me, sectors, core, shift) * slots
            group = jnp.zeros((2 * slots, 1), jnp.int32)
            for slot in range(slots):
                value = waves_ref[first + slot]
                group = jnp.where((row == slot) | (row == slots + slot), value, group)
            groups.append(group)
    wave = jnp.concatenate(groups, axis=0)
    start = wave * (me * cols)
    turns = jnp.floor(start.astype(f32) * (1.0 / period)).astype(jnp.int32)
    start = (start - turns * period).astype(f32)
    wave = wave.astype(f32)
    row = lax.broadcasted_iota(jnp.int32, (waves, 1), 0)
    sine = (lax.rem(row, 2 * slots) >= slots).astype(f32)
    offset = 4.0 * start - period * sine
    for tile in range(0, width, 128):
        lane = lax.broadcasted_iota(jnp.int32, (1, 128), 1) + tile
        lane = jnp.where(lane < cols + MARGIN, lane, lane - width).astype(f32)
        product = wave * lane
        product = product - period * jnp.floor(product * (1.0 / period))
        quarter = 4.0 * product + offset
        turn = jnp.floor(quarter * (1.0 / period) + 0.5)
        angle = (quarter - period * turn) * (0.5 * math.pi / period)
        square = angle * angle
        cosine = 1.0 + square * (
            -1.0 / 2 + square * (1.0 / 24 + square * (-1.0 / 720 + square * (1.0 / 40320)))
        )
        sine_of = angle * (
            1.0
            + square
            * (-1.0 / 6 + square * (1.0 / 120 + square * (-1.0 / 5040 + square * (1.0 / 362880))))
        )
        phase = turn - 4.0 * jnp.floor(turn * 0.25)
        odd = (phase == 1.0) | (phase == 3.0)
        value = jnp.where(odd, sine_of, cosine)
        value = jnp.where((phase == 1.0) | (phase == 2.0), -value, value)
        hi, lo = split2(value)
        harm_ref[:waves, tile : tile + 128] = hi
        harm_ref[waves:, tile : tile + 128] = lo


def transform_kernel(
    period,
    slots,
    waves_hbm,
    height_hbm,
    east_hbm,
    north_hbm,
    land_hbm,
    legendre_hbm,
    keep_ref,
    send_ref,
    even_ref,
    odd_ref,
    legendre_ref,
    waves_ref,
    height_ref,
    east_ref,
    north_ref,
    land_ref,
    harm_ref,
    field_ref,
    semaphores,
):
    rows, cols = height_ref.shape
    waves, width = harm_ref.shape[0] // 2, harm_ref.shape[1]
    copies = [
        pltpu.make_async_copy(source, target, semaphores.at[at])
        for at, (source, target) in enumerate(
            (
                (waves_hbm, waves_ref),
                (height_hbm, height_ref),
                (east_hbm, east_ref),
                (north_hbm, north_ref),
                (land_hbm, land_ref),
                (legendre_hbm, legendre_ref),
            )
        )
    ]
    for copy in copies:
        copy.start()
    copies[0].wait()
    harmonic_rows(period, cols, slots, lax.axis_index("lon"), waves_ref, harm_ref)
    copies[1].wait()
    for tile in range(0, width, 128):
        stop = min(cols, tile + 128)
        if stop <= tile:
            block = jnp.zeros((rows, 128), f32)
        elif stop == tile + 128:
            block = height_ref[:, tile : tile + 128]
        else:
            block = jnp.concatenate(
                [height_ref[:, tile:stop], jnp.zeros((rows, tile + 128 - stop), f32)], axis=1
            )
        hi, lo = split2(block)
        field_ref[:rows, tile : tile + 128] = hi
        field_ref[rows:, tile : tile + 128] = lo
    both = lax.dot_general(
        harm_ref[...], field_ref[...], (((1,), (1,)), ((), ())), preferred_element_type=f32
    )
    total = both[:waves] + both[waves:]
    total = (total[:, :rows] + total[:, rows:]) * (1.0 / math.sqrt(period))
    total = jnp.concatenate([total, jnp.zeros((waves, 128 - rows), f32)], axis=1)
    keep_ref[...] = total[: waves // 2].reshape(keep_ref.shape)
    send_ref[: waves // 2] = total[waves // 2 :]
    for copy in copies[2:5]:
        copy.wait()
    is_even = lax.rem(lax.axis_index("lat"), 2) == 0
    pieces = []
    for at, ref in enumerate((height_ref, east_ref, north_ref, land_ref)):
        pieces += [ref[:, :MARGIN].astype(f32), ref[:, cols - MARGIN :].astype(f32)]
        up, down = ref[rows - MARGIN :].astype(f32), ref[:MARGIN].astype(f32)
        even_ref[at, :, :cols] = jnp.where(is_even, up, down)
        odd_ref[at, :, :cols] = jnp.where(is_even, down, up)
        if cols < width:
            blank = jnp.zeros((MARGIN, width - cols), f32)
            even_ref[at, :, cols:] = blank
            odd_ref[at, :, cols:] = blank
    half = rows // 2
    send_ref[waves // 2 :] = jnp.concatenate(
        [piece[:half] for piece in pieces] + [piece[half:] for piece in pieces], axis=1
    )
    copies[5].wait()


def mix_kernel(keep_ref, recv_ref, own_ref, *send_refs):
    chips, group, _ = keep_ref.shape
    own_ref[...] = keep_ref[0] + recv_ref[:group]
    for shift, ref in enumerate(send_refs, 1):
        ref[:group] = keep_ref[shift] + recv_ref[shift * group : (shift + 1) * group]
        if ref.shape[0] > group:
            ref[group:] = recv_ref[chips * group :]


def analysis_kernel(part_refs, core_ref, legendre_ref, spectral_ref, even_ref, odd_ref):
    slots, rows, degrees = legendre_ref.shape
    chips, half = len(part_refs), rows // 2
    left, right = side_tiles(lax.axis_index("lon"), 2 * slots, chips, core_ref, part_refs[1], part_refs[-1])
    lanes = lax.broadcasted_iota(jnp.int32, left.shape, 1)
    both = jnp.where(lax.rem(lanes, 2 * MARGIN) < MARGIN, right, left)
    up, down = pltpu.roll(both[half - MARGIN :], 64, 1), both[:MARGIN]
    is_even = lax.rem(lax.axis_index("lat"), 2) == 0
    ahead = even_ref.shape[1] - 128
    even_ref[:, ahead:] = jnp.where(is_even, up, down)
    odd_ref[:, ahead:] = jnp.where(is_even, down, up)
    fourier = part_refs[0][...]
    for ref in part_refs[1:]:
        fourier = fourier + ref[: 2 * slots]
    columns = fourier.T
    for slot in range(slots):
        even = [
            jnp.broadcast_to(columns[o : o + 8, slot : slot + 1], (8, 128))
            for o in range(0, rows, 8)
        ]
        odd = [
            jnp.broadcast_to(columns[o : o + 8, slots + slot : slots + slot + 1], (8, 128))
            for o in range(0, rows, 8)
        ]
        for tile in range(0, degrees, 128):
            first = jnp.zeros((8, 128), f32)
            second = jnp.zeros((8, 128), f32)
            for at, o in enumerate(range(0, rows, 8)):
                block = legendre_ref[slot, o : o + 8, tile : tile + 128]
                first = first + block * even[at]
                second = second + block * odd[at]
            spectral_ref[slot : slot + 1, tile : tile + 128] = jnp.sum(
                first, axis=0, keepdims=True
            )
            spectral_ref[slots + slot : slots + slot + 1, tile : tile + 128] = jnp.sum(
                second, axis=0, keepdims=True
            )
    if ahead:
        even_ref[:, :ahead] = spectral_ref[...]
        odd_ref[:, :ahead] = spectral_ref[...]

def synthesis_kernel(parts_refs, love_ref, legendre_ref, out_ref, spectral_ref):
    slots, rows, degrees = legendre_ref.shape
    total = parts_refs[0][...]
    for ref in parts_refs[1:]:
        total = total + ref[:, :degrees]
    spectral_ref[...] = total * love_ref[...]
    lanes = lax.broadcasted_iota(jnp.int32, (8, 128), 1)
    octets = range(0, rows, 8)
    sums = [jnp.zeros((8, 128), f32) for _ in octets]
    for slot in range(slots):
        first = [jnp.zeros((8, 128), f32) for _ in octets]
        second = [jnp.zeros((8, 128), f32) for _ in octets]
        for tile in range(0, degrees, 128):
            even = jnp.broadcast_to(spectral_ref[slot : slot + 1, tile : tile + 128], (8, 128))
            odd = jnp.broadcast_to(
                spectral_ref[slots + slot : slots + slot + 1, tile : tile + 128], (8, 128)
            )
            for at, o in enumerate(octets):
                block = legendre_ref[slot, o : o + 8, tile : tile + 128]
                first[at] = first[at] + block * even
                second[at] = second[at] + block * odd
        for at in range(len(octets)):
            sums[at] = jnp.where(lanes == slot, jnp.sum(first[at], axis=1, keepdims=True), sums[at])
            sums[at] = jnp.where(
                lanes == slots + slot, jnp.sum(second[at], axis=1, keepdims=True), sums[at]
            )
    column = jnp.concatenate(sums + [jnp.zeros((128 - rows, 128), f32)], axis=0)
    out_ref[...] = jnp.broadcast_to(column.T[None, : 2 * slots], out_ref.shape)


def side_tiles(me, group, chips, core_ref, west_ref, east_ref):
    first = lax.rem(me, 2) == 0
    other = core_ref[chips * group :]
    left = jnp.where(first, west_ref[group:], other)
    right = jnp.where(first, other, east_ref[group:])
    return left, right


def with_sides(tail, left, right, own, at):
    lanes = lax.broadcasted_iota(jnp.int32, tail.shape, 1)
    after = pltpu.roll(right, (own - 2 * MARGIN * at) % 128, 1)
    before = pltpu.roll(left, (-MARGIN - 2 * MARGIN * at - MARGIN) % 128, 1)
    repeat = tail.shape[1] // 128
    after = jnp.concatenate([after] * repeat, axis=1)
    before = jnp.concatenate([before] * repeat, axis=1)
    tail = jnp.where((lanes >= own) & (lanes < own + MARGIN), after, tail)
    return jnp.where(lanes >= tail.shape[1] - MARGIN, before, tail)


def windows_kernel(
    period,
    slots,
    chips,
    bands,
    waves_hbm,
    height_hbm,
    east_hbm,
    north_hbm,
    land_hbm,
    core_ref,
    west_ref,
    east_ref,
    even_rows,
    odd_rows,
    even_ref,
    odd_ref,
    surface_win,
    east_win,
    north_win,
    wet_win,
    harm_ref,
    waves_ref,
    fields,
    land,
    semaphores,
):
    rows, cols = height_hbm.shape
    width = harm_ref.shape[1]
    last = (cols // 128) * 128
    copies = [
        pltpu.make_async_copy(source, target, semaphores.at[at])
        for at, (source, target) in enumerate(
            (
                (height_hbm, fields.at[0]),
                (east_hbm, fields.at[1]),
                (north_hbm, fields.at[2]),
                (land_hbm, land),
                (waves_hbm, waves_ref),
            )
        )
    ]
    for copy in copies:
        copy.start()
    copies[4].wait()
    harmonic_rows(period, cols, slots, lax.axis_index("lon"), waves_ref, harm_ref)
    left, right = side_tiles(lax.axis_index("lon"), 2 * slots, chips, core_ref, west_ref, east_ref)
    left = jnp.concatenate([left, pltpu.roll(left, 64, 1)], axis=0)
    right = jnp.concatenate([right, pltpu.roll(right, 64, 1)], axis=0)
    band = lax.axis_index("lat")
    is_even = lax.rem(band, 2) == 0
    even, odd = even_ref[:, -128:], odd_ref[:, -128:]
    corners = (jnp.where(is_even, odd, even), jnp.where(is_even, even, odd))
    for at, target in enumerate((surface_win, east_win, north_win, wet_win)):
        even, odd = even_rows[at], odd_rows[at]
        halos = (jnp.where(is_even, odd, even), jnp.where(is_even, even, odd))
        for halo, corner, first, inside in zip(
            halos, corners, (0, MARGIN + rows), (band > 0, band < bands - 1)
        ):
            place = pl.ds(first, MARGIN)
            target[place, :last] = jnp.where(inside, halo[:, :last], 0.0)
            tail = with_sides(halo[:, last:], corner, corner, cols - last, at)
            target[place, last:] = jnp.where(inside, tail, 0.0)
    for at, target in enumerate((surface_win, east_win, north_win, wet_win)):
        copies[at].wait()
        field = fields.at[at] if at < 3 else land
        target[MARGIN : MARGIN + rows, :last] = field[:, :last].astype(f32)
        tail = jnp.concatenate(
            [field[:, last:].astype(f32), jnp.zeros((rows, width - cols), f32)], axis=1
        )
        target[MARGIN : MARGIN + rows, last:] = with_sides(tail, left, right, cols - last, at)


def substep_kernel(
    sectors,
    bands,
    synth_ref,
    harm_ref,
    surface_win,
    east_win,
    north_win,
    wet,
    loading_hbm,
    surface_hbm,
    east_hbm,
    north_hbm,
    load,
    pressure,
    surface,
    east,
    north,
    loading_out,
    surface_out,
    east_out,
    north_out,
    semaphores,
):
    rows, cols = loading_hbm.shape
    taller, width = wet.shape
    waves = harm_ref.shape[0] // 2
    me, band = lax.axis_index("lon"), lax.axis_index("lat")
    below, above = jnp.maximum(band - 1, 0), jnp.minimum(band + 1, bands - 1)
    lanes = lax.broadcasted_iota(jnp.int32, synth_ref.shape[1:], 1)
    groups = []
    for core in range(2):
        for shift in range(sectors // 2):
            sector = owner(me, sectors, core, shift)
            low = jnp.where(band > 0, synth_ref[below * sectors + sector], 0.0)
            high = jnp.where(band < bands - 1, synth_ref[above * sectors + sector], 0.0)
            group = pltpu.roll(synth_ref[band * sectors + sector], MARGIN, 1)
            group = jnp.where(lanes < MARGIN, pltpu.roll(low, (MARGIN - rows) % 128, 1), group)
            high = pltpu.roll(high, MARGIN + rows, 1)
            groups.append(jnp.where(lanes >= MARGIN + rows, high, group))
    synth = jnp.concatenate(groups, axis=0).T * (1.0 / math.sqrt(waves // 2))
    hi, lo = split2(synth[:taller])
    left = jnp.concatenate(
        [jnp.concatenate([hi, hi], axis=1), jnp.concatenate([lo, lo], axis=1)], axis=0
    )
    both = lax.dot_general(
        left, harm_ref[...], (((1,), (0,)), ((), ())), preferred_element_type=f32
    )
    load[...] = both[:taller] + both[taller:]
    copies = [
        pltpu.make_async_copy(source, target, semaphores.at[at])
        for at, (source, target) in enumerate(
            (
                (loading_out, loading_hbm),
                (surface_out, surface_hbm),
                (east_out, east_hbm),
                (north_out, north_hbm),
            )
        )
    ]
    inner = pl.ds(MARGIN, rows)
    loading_out[...] = load[inner, :cols]
    copies[0].start()
    edge = jnp.zeros((8, width), f32)
    pressure[:8] = edge
    pressure[taller + 8 :] = edge
    north[:8] = edge
    north[taller + 8 :] = edge
    for o in range(0, taller, 8):
        pressure[8 + o : 16 + o] = surface_win[o : o + 8] - load[o : o + 8]
    for substep in range(SUBSTEPS):
        final = substep == SUBSTEPS - 1
        for o in range(0, taller, 8):
            here = pressure[8 + o : 16 + o]
            damp = wet[o : o + 8]
            flow = east_win[o : o + 8] if substep == 0 else east[o : o + 8]
            flow = damp * (
                flow - STEP * (pltpu.roll(here, width - 1, 1) - pltpu.roll(here, 1, 1))
            )
            east[o : o + 8] = flow
            other = north_win[o : o + 8] if substep == 0 else north[8 + o : 16 + o]
            other = damp * (
                other - STEP * (pressure[9 + o : 17 + o] - pressure[7 + o : 15 + o])
            )
            north[8 + o : 16 + o] = other
            if final and MARGIN <= o < MARGIN + rows:
                east_out[o - MARGIN : o - MARGIN + 8] = flow[:, :cols]
                north_out[o - MARGIN : o - MARGIN + 8] = other[:, :cols]
        if final:
            copies[2].start()
            copies[3].start()
        for o in range(0, taller, 8):
            if final and not MARGIN <= o < MARGIN + rows:
                continue
            flow = east[o : o + 8]
            change = STEP * (pltpu.roll(flow, width - 1, 1) - pltpu.roll(flow, 1, 1)) + STEP * (
                north[9 + o : 17 + o] - north[7 + o : 15 + o]
            )
            level = surface_win[o : o + 8] if substep == 0 else surface[o : o + 8]
            level = level - wet[o : o + 8] * change
            if final:
                surface_out[o - MARGIN : o - MARGIN + 8] = level[:, :cols]
            else:
                surface[o : o + 8] = level
                pressure[8 + o : 16 + o] = level - load[o : o + 8]
    copies[1].start()
    for copy in copies:
        copy.wait()


def shards(height, east_flow, north_flow, legendre, love_numbers, wavenumbers, land_sea):
    rows, cols = height.shape
    slots, _, degrees = legendre.shape
    sectors, bands = lax.axis_size("lon"), lax.axis_size("lat")
    chips = sectors // 2
    waves = wavenumbers.shape[0]
    period = cols * sectors
    width = -(-(cols + 2 * MARGIN) // 128) * 128
    taller = rows + 2 * MARGIN
    group, half = 2 * slots, rows // 2
    DMA = pltpu.SemaphoreType.DMA
    fields = (height, east_flow, north_flow, land_sea)

    keep, send, even, odd, legendre = pl.pallas_call(
        functools.partial(transform_kernel, period, slots),
        out_shape=[
            struct((chips, group, 128)),
            struct((chips * group + half, 128)),
            struct((4, MARGIN, width)),
            struct((4, MARGIN, width)),
            struct(legendre.shape),
        ],
        in_specs=[HBM] * 6,
        out_specs=[VMEM] * 5,
        scratch_shapes=[
            pltpu.SMEM((waves,), jnp.int32),
            pltpu.VMEM((rows, cols), f32),
            pltpu.VMEM((rows, cols), f32),
            pltpu.VMEM((rows, cols), f32),
            pltpu.VMEM((rows, cols), jnp.int32),
            pltpu.VMEM((4 * waves, width), bf16),
            pltpu.VMEM((2 * rows, width), bf16),
            DMA((6,)),
        ],
        name="transform",
        compiler_params=LIMIT,
    )(*in_hbm(wavenumbers, *fields, legendre))
    core = lax.ppermute(send, "lon", [(i, i ^ 1) for i in range(sectors)])
    neighbours = (1, chips - 1)
    own, *outgoing = pl.pallas_call(
        mix_kernel,
        out_shape=[struct((group, 128))]
        + [
            struct((group + (half if shift in neighbours else 0), 128))
            for shift in range(1, chips)
        ],
        in_specs=[VMEM] * 2,
        out_specs=[VMEM] * chips,
        name="mix",
        compiler_params=LIMIT,
    )(keep, core)
    arrived = [
        lax.ppermute(
            block, "lon", [(i, (i + 2 * shift) % sectors) for i in range(sectors)]
        )
        for shift, block in enumerate(outgoing, 1)
    ]
    sides = (core, arrived[0], arrived[-1])

    links = [[(i, i + 1) for i in range(first, bands - 1, 2)] for first in (0, 1)]
    links = [pairs + [(j, i) for i, j in pairs] for pairs in links]
    even, odd = [lax.ppermute(block, "lat", pairs) for block, pairs in zip((even, odd), links)]

    def analysis(*refs):
        analysis_kernel(refs[:chips], *refs[chips:])

    together = bands == 4
    message = 128 + (degrees if together else 0)
    spectral, *corners = pl.pallas_call(
        analysis,
        out_shape=[struct((group, degrees))] + [struct((MARGIN, message))] * 2,
        in_specs=[VMEM] * (chips + 2),
        out_specs=[VMEM] * 3,
        name="analysis",
        compiler_params=LIMIT,
    )(own, *arrived, core, legendre)
    if together:
        *corners, across = [
            lax.ppermute(block, "lat", [(i, i ^ step) for i in range(bands)])
            for block, step in ((corners[0], 1), (corners[1], 3), (spectral, 2))
        ]
        pieces = [spectral, *corners, across]
    else:
        corners = [
            lax.ppermute(block, "lat", pairs) for block, pairs in zip(corners, links)
        ]
        pieces = [lax.psum(spectral, "lat")]

    def synthesis(*refs):
        synthesis_kernel(refs[: len(pieces)], *refs[len(pieces) :])

    synth = pl.pallas_call(
        synthesis,
        out_shape=struct((bands * sectors, group, 128)),
        in_specs=[VMEM] * (len(pieces) + 2),
        out_specs=VMEM,
        scratch_shapes=[pltpu.VMEM((group, degrees), f32)],
        name="synthesis",
        cost_estimate=pl.CostEstimate(flops=100000000000, bytes_accessed=400000000, transcendentals=0),
        compiler_params=LIMIT,
    )(*pieces, love_numbers.reshape(1, degrees), legendre)
    everyone = lax.all_to_all(synth, ("lat", "lon"), 0, 0, tiled=True)

    *windows, harmonics = pl.pallas_call(
        functools.partial(windows_kernel, period, slots, chips, bands),
        out_shape=[struct((taller, width))] * 4 + [struct((4 * waves, width), bf16)],
        in_specs=[HBM] * 5 + [VMEM] * 7,
        out_specs=[VMEM] * 5,
        scratch_shapes=[
            pltpu.SMEM((waves,), jnp.int32),
            pltpu.VMEM((3, rows, cols), f32),
            pltpu.VMEM((rows, cols), jnp.int32),
            DMA((5,)),
        ],
        name="windows",
        cost_estimate=pl.CostEstimate(flops=10**11, bytes_accessed=4 * 10**8, transcendentals=0),
        compiler_params=LIMIT,
    )(*in_hbm(wavenumbers, *fields), *sides, even, odd, *corners)

    return pl.pallas_call(
        functools.partial(substep_kernel, sectors, bands),
        out_shape=[struct((rows, cols))] * 4,
        in_specs=[VMEM] * 6,
        out_specs=[HBM] * 4,
        scratch_shapes=[
            pltpu.VMEM((taller, width), f32),
            pltpu.VMEM((taller + 16, width), f32),
            pltpu.VMEM((taller, width), f32),
            pltpu.VMEM((taller, width), f32),
            pltpu.VMEM((taller + 16, width), f32),
        ]
        + [pltpu.VMEM((rows, cols), f32)] * 4
        + [DMA((4,))],
        name="substeps",
        compiler_params=LIMIT,
    )(everyone, harmonics, *windows)


def solution(mesh):
    return jax.shard_map(
        shards,
        mesh=mesh,
        in_specs=(
            P("lat", "lon"),
            P("lat", "lon"),
            P("lat", "lon"),
            P("lon", "lat", None),
            P(),
            P(),
            P("lat", "lon"),
        ),
        out_specs=(P("lat", "lon"), P("lat", "lon"), P("lat", "lon"), P("lat", "lon")),
        check_vma=False,
    )
```

```python
import functools
import math

import jax
import jax.numpy as jnp
from jax import lax
from jax.experimental import pallas as pl
from jax.experimental.pallas import tpu as pltpu
from jax.sharding import PartitionSpec as P

SUBSTEPS = 4
MARGIN = 2 * SUBSTEPS
STEP = 0.3

f32 = jnp.float32
bf16 = jnp.bfloat16
VMEM = pl.BlockSpec(memory_space=pltpu.VMEM)
HBM = pl.BlockSpec(memory_space=pltpu.HBM)
SMEM = pl.BlockSpec(memory_space=pltpu.SMEM)
LIMIT = pltpu.CompilerParams(vmem_limit_bytes=24 * 2**20)


def struct(shape, dtype=f32):
    return jax.ShapeDtypeStruct(shape, dtype)


def in_hbm(*arrays):
    return [pltpu.with_memory_space_constraint(x, pltpu.HBM) for x in arrays]


def split2(x):
    hi = x.astype(bf16)
    lo = (x - hi.astype(f32)).astype(bf16)
    return hi, lo


def owner(me, sectors, core, shift):
    chips = sectors // 2
    return 2 * lax.rem(me // 2 + shift, chips) + lax.bitwise_xor(lax.rem(me, 2), core)


def row_groups(sectors):
    return [(core, shift) for core in range(2) for shift in range(sectors // 2)]


def harmonic_rows(period, cols, slots, me, paired, waves_ref, harm_ref):
    waves, width = harm_ref.shape[0] // 2, harm_ref.shape[1]
    sectors = waves // (2 * slots)
    order = []
    for core, shift in row_groups(sectors):
        first = owner(me, sectors, core, shift) * slots
        group = [waves_ref[first + slot] for slot in range(slots)]
        order += group + group if paired else group
    if not paired:
        order = order + order
    row = lax.broadcasted_iota(jnp.int32, (8, 1), 0)
    blocks = []
    for first in range(0, waves, 8):
        block = jnp.zeros((8, 1), jnp.int32)
        for at, value in enumerate(order[first : first + 8]):
            block = jnp.where(row == at, value, block)
        blocks.append(block)
    wave = jnp.concatenate(blocks, axis=0)
    start = wave * (me * cols)
    turns = jnp.floor(start.astype(f32) * (1.0 / period)).astype(jnp.int32)
    start = (start - turns * period).astype(f32)
    wave = wave.astype(f32)
    row = lax.broadcasted_iota(jnp.int32, (waves, 1), 0)
    if paired:
        row = lax.rem(row, 2 * slots)
    sine = (row >= (slots if paired else waves // 2)).astype(f32)
    offset = 4.0 * start - period * sine
    for tile in range(0, width, 128):
        lane = lax.broadcasted_iota(jnp.int32, (1, 128), 1) + tile
        lane = jnp.where(lane < cols + MARGIN, lane, lane - width).astype(f32)
        product = wave * lane
        product = product - period * jnp.floor(product * (1.0 / period))
        quarter = 4.0 * product + offset
        turn = jnp.floor(quarter * (1.0 / period) + 0.5)
        angle = (quarter - period * turn) * (0.5 * math.pi / period)
        square = angle * angle
        cosine = 1.0 + square * (
            -1.0 / 2 + square * (1.0 / 24 + square * (-1.0 / 720 + square * (1.0 / 40320)))
        )
        sine_of = angle * (
            1.0
            + square
            * (-1.0 / 6 + square * (1.0 / 120 + square * (-1.0 / 5040 + square * (1.0 / 362880))))
        )
        phase = turn - 4.0 * jnp.floor(turn * 0.25)
        odd = (phase == 1.0) | (phase == 3.0)
        value = jnp.where(odd, sine_of, cosine)
        value = jnp.where((phase == 1.0) | (phase == 2.0), -value, value)
        hi, lo = split2(value)
        harm_ref[:waves, tile : tile + 128] = hi
        harm_ref[waves:, tile : tile + 128] = lo


def transform_kernel(
    period,
    slots,
    waves_hbm,
    height_hbm,
    east_hbm,
    north_hbm,
    land_hbm,
    keep_ref,
    send_ref,
    waves_ref,
    height_ref,
    flow_front,
    flow_back,
    land_front,
    land_back,
    harm_ref,
    field_ref,
    semaphores,
):
    rows, cols = height_ref.shape
    waves, width = harm_ref.shape[0] // 2, harm_ref.shape[1]
    back = cols - land_back.shape[1]
    fronts, backs = pl.ds(0, 128), pl.ds(back, cols - back)
    copies = [
        pltpu.make_async_copy(source, target, semaphores.at[at])
        for at, (source, target) in enumerate(
            (
                (waves_hbm, waves_ref),
                (height_hbm, height_ref),
                (east_hbm.at[:, fronts], flow_front.at[0]),
                (east_hbm.at[:, backs], flow_back.at[0]),
                (north_hbm.at[:, fronts], flow_front.at[1]),
                (north_hbm.at[:, backs], flow_back.at[1]),
                (land_hbm.at[:, fronts], land_front),
                (land_hbm.at[:, backs], land_back),
            )
        )
    ]
    for copy in copies:
        copy.start()
    copies[0].wait()
    harmonic_rows(period, cols, slots, lax.axis_index("lon"), True, waves_ref, harm_ref)
    copies[1].wait()
    for tile in range(0, width, 128):
        stop = min(cols, tile + 128)
        if stop <= tile:
            block = jnp.zeros((rows, 128), f32)
        elif stop == tile + 128:
            block = height_ref[:, tile : tile + 128]
        else:
            block = jnp.concatenate(
                [height_ref[:, tile:stop], jnp.zeros((rows, tile + 128 - stop), f32)], axis=1
            )
        hi, lo = split2(block)
        field_ref[:rows, tile : tile + 128] = hi
        field_ref[rows:, tile : tile + 128] = lo
    both = lax.dot_general(
        harm_ref[...], field_ref[...], (((1,), (1,)), ((), ())), preferred_element_type=f32
    )
    total = both[:waves] + both[waves:]
    total = (total[:, :rows] + total[:, rows:]) * (1.0 / math.sqrt(period))
    total = jnp.concatenate([total, jnp.zeros((waves, 128 - rows), f32)], axis=1)
    keep_ref[...] = total[: waves // 2].reshape(keep_ref.shape)
    send_ref[: waves // 2] = total[waves // 2 :]
    for copy in copies[2:]:
        copy.wait()
    pieces = []
    for front, end in (
        (height_ref[:, :MARGIN], height_ref[:, cols - MARGIN :]),
        (flow_front[0, :, :MARGIN], flow_back[0, :, cols - MARGIN - back :]),
        (flow_front[1, :, :MARGIN], flow_back[1, :, cols - MARGIN - back :]),
        (land_front[:, :MARGIN].astype(f32), land_back[:, cols - MARGIN - back :].astype(f32)),
    ):
        pieces += [front, end]
    half = rows // 2
    send_ref[waves // 2 :] = jnp.concatenate(
        [piece[:half] for piece in pieces] + [piece[half:] for piece in pieces], axis=1
    )


def stage_kernel(
    after_ref,
    height_hbm,
    east_hbm,
    north_hbm,
    land_hbm,
    legendre_hbm,
    even_ref,
    odd_ref,
    legendre_ref,
    flows,
    lands,
    semaphores,
):
    rows, cols = height_hbm.shape
    width = even_ref.shape[2]
    copies = []
    for side, first in enumerate((rows - MARGIN, 0)):
        band = pl.ds(first, MARGIN)
        copies.append((height_hbm.at[band], flows.at[side, 0]))
        copies.append((east_hbm.at[band], flows.at[side, 1]))
        copies.append((north_hbm.at[band], flows.at[side, 2]))
        copies.append((land_hbm.at[band], lands.at[side]))
    copies.append((legendre_hbm, legendre_ref))
    copies = [
        pltpu.make_async_copy(source, target, semaphores.at[at])
        for at, (source, target) in enumerate(copies)
    ]
    for copy in copies:
        copy.start()
    for copy in copies[:-1]:
        copy.wait()
    is_even = lax.rem(lax.axis_index("lat"), 2) == 0
    for at in range(4):
        up, down = [lands[side].astype(f32) if at == 3 else flows[side, at] for side in range(2)]
        even_ref[at, :, :cols] = jnp.where(is_even, up, down)
        odd_ref[at, :, :cols] = jnp.where(is_even, down, up)
        if cols < width:
            blank = jnp.zeros((MARGIN, width - cols), f32)
            even_ref[at, :, cols:] = blank
            odd_ref[at, :, cols:] = blank
    copies[-1].wait()


def mix_kernel(keep_ref, recv_ref, own_ref, *send_refs):
    chips, group, _ = keep_ref.shape
    own_ref[...] = keep_ref[0] + recv_ref[:group]
    for shift, ref in enumerate(send_refs, 1):
        ref[:group] = keep_ref[shift] + recv_ref[shift * group : (shift + 1) * group]
        if ref.shape[0] > group:
            ref[group:] = recv_ref[chips * group :]


def analysis_kernel(part_refs, core_ref, legendre_ref, spectral_ref, even_ref, odd_ref):
    slots, rows, degrees = legendre_ref.shape
    chips, half = len(part_refs), rows // 2
    left, right = side_tiles(lax.axis_index("lon"), 2 * slots, chips, core_ref, part_refs[1], part_refs[-1])
    lanes = lax.broadcasted_iota(jnp.int32, left.shape, 1)
    both = jnp.where(lax.rem(lanes, 2 * MARGIN) < MARGIN, right, left)
    up, down = pltpu.roll(both[half - MARGIN :], 64, 1), both[:MARGIN]
    is_even = lax.rem(lax.axis_index("lat"), 2) == 0
    ahead = even_ref.shape[1] - 128
    even_ref[:, ahead:] = jnp.where(is_even, up, down)
    odd_ref[:, ahead:] = jnp.where(is_even, down, up)
    fourier = part_refs[0][...]
    for ref in part_refs[1:]:
        fourier = fourier + ref[: 2 * slots]
    columns = fourier.T
    for slot in range(slots):
        even = [
            jnp.broadcast_to(columns[o : o + 8, slot : slot + 1], (8, 128))
            for o in range(0, rows, 8)
        ]
        odd = [
            jnp.broadcast_to(columns[o : o + 8, slots + slot : slots + slot + 1], (8, 128))
            for o in range(0, rows, 8)
        ]
        for tile in range(0, degrees, 128):
            first = jnp.zeros((8, 128), f32)
            second = jnp.zeros((8, 128), f32)
            for at, o in enumerate(range(0, rows, 8)):
                block = legendre_ref[slot, o : o + 8, tile : tile + 128]
                first = first + block * even[at]
                second = second + block * odd[at]
            spectral_ref[slot : slot + 1, tile : tile + 128] = jnp.sum(
                first, axis=0, keepdims=True
            )
            spectral_ref[slots + slot : slots + slot + 1, tile : tile + 128] = jnp.sum(
                second, axis=0, keepdims=True
            )
    if ahead:
        even_ref[:, :ahead] = spectral_ref[...]
        odd_ref[:, :ahead] = spectral_ref[...]

def synthesis_kernel(parts_refs, love_ref, legendre_ref, out_ref, spectral_ref):
    slots, rows, degrees = legendre_ref.shape
    total = parts_refs[0][...]
    for ref in parts_refs[1:]:
        total = total + ref[:, :degrees]
    spectral_ref[...] = total * love_ref[...]
    lanes = lax.broadcasted_iota(jnp.int32, (8, 128), 1)
    octets = range(0, rows, 8)
    sums = [jnp.zeros((8, 128), f32) for _ in octets]
    for slot in range(slots):
        first = [jnp.zeros((8, 128), f32) for _ in octets]
        second = [jnp.zeros((8, 128), f32) for _ in octets]
        for tile in range(0, degrees, 128):
            even = jnp.broadcast_to(spectral_ref[slot : slot + 1, tile : tile + 128], (8, 128))
            odd = jnp.broadcast_to(
                spectral_ref[slots + slot : slots + slot + 1, tile : tile + 128], (8, 128)
            )
            for at, o in enumerate(octets):
                block = legendre_ref[slot, o : o + 8, tile : tile + 128]
                first[at] = first[at] + block * even
                second[at] = second[at] + block * odd
        for at in range(len(octets)):
            sums[at] = jnp.where(lanes == slot, jnp.sum(first[at], axis=1, keepdims=True), sums[at])
            sums[at] = jnp.where(
                lanes == slots + slot, jnp.sum(second[at], axis=1, keepdims=True), sums[at]
            )
    column = jnp.concatenate(sums + [jnp.zeros((128 - rows, 128), f32)], axis=0)
    lines = column.T[: 2 * slots]
    lines = lines[:slots] + pltpu.roll(lines[slots:], 64, 1)
    out_ref[...] = jnp.broadcast_to(lines[None], out_ref.shape)


def side_tiles(me, group, chips, core_ref, west_ref, east_ref):
    first = lax.rem(me, 2) == 0
    other = core_ref[chips * group :]
    left = jnp.where(first, west_ref[group:], other)
    right = jnp.where(first, other, east_ref[group:])
    return left, right


def with_sides(tail, left, right, own, at):
    lanes = lax.broadcasted_iota(jnp.int32, tail.shape, 1)
    after = pltpu.roll(right, (own - 2 * MARGIN * at) % 128, 1)
    before = pltpu.roll(left, (-MARGIN - 2 * MARGIN * at - MARGIN) % 128, 1)
    repeat = tail.shape[1] // 128
    after = jnp.concatenate([after] * repeat, axis=1)
    before = jnp.concatenate([before] * repeat, axis=1)
    tail = jnp.where((lanes >= own) & (lanes < own + MARGIN), after, tail)
    return jnp.where(lanes >= tail.shape[1] - MARGIN, before, tail)


def interleaved(ref, step):
    return [ref[pl.ds(at, 8, stride=step)] for at in range(step)]


def windows_kernel(
    period,
    slots,
    chips,
    bands,
    waves_hbm,
    height_hbm,
    east_hbm,
    north_hbm,
    land_hbm,
    core_ref,
    west_ref,
    east_ref,
    even_rows,
    odd_rows,
    even_ref,
    odd_ref,
    surface_win,
    east_win,
    north_win,
    wet_win,
    moved_win,
    harm_ref,
    waves_ref,
    fields,
    land,
    natural,
    semaphores,
):
    rows, cols = height_hbm.shape
    width = harm_ref.shape[1]
    taller = rows + 2 * MARGIN
    step = taller // 8
    last = (cols // 128) * 128
    copies = [
        pltpu.make_async_copy(source, target, semaphores.at[at])
        for at, (source, target) in enumerate(
            (
                (height_hbm, fields.at[0]),
                (east_hbm, fields.at[1]),
                (north_hbm, fields.at[2]),
                (land_hbm, land),
                (waves_hbm, waves_ref),
            )
        )
    ]
    for copy in copies:
        copy.start()
    copies[4].wait()
    harmonic_rows(period, cols, slots, lax.axis_index("lon"), False, waves_ref, harm_ref)
    left, right = side_tiles(
        lax.axis_index("lon"), 2 * slots, chips, core_ref, west_ref, east_ref
    )
    left = jnp.concatenate([left, pltpu.roll(left, 64, 1)], axis=0)
    right = jnp.concatenate([right, pltpu.roll(right, 64, 1)], axis=0)
    band = lax.axis_index("lat")
    is_even = lax.rem(band, 2) == 0
    even, odd = even_ref[:, -128:], odd_ref[:, -128:]
    corners = (jnp.where(is_even, odd, even), jnp.where(is_even, even, odd))
    for copy in copies[:4]:
        copy.wait()
    middle = pl.ds(MARGIN, rows)
    for at, target in ((3, wet_win), (0, surface_win), (1, east_win), (2, north_win)):
        field = fields.at[at] if at < 3 else land
        even, odd = even_rows[at], odd_rows[at]
        halos = (jnp.where(is_even, odd, even), jnp.where(is_even, even, odd))
        for tile in range(0, last, 128):
            natural[tile // 128, middle] = field[:, tile : tile + 128].astype(f32)
        tail = jnp.concatenate(
            [field[:, last:].astype(f32), jnp.zeros((rows, width - cols), f32)], axis=1
        )
        tail = with_sides(tail, left, right, cols - last, at)
        for tile in range(last, width, 128):
            natural[tile // 128, middle] = tail[:, tile - last : tile - last + 128]
        for halo, corner, first, inside in zip(
            halos, corners, (0, MARGIN + rows), (band > 0, band < bands - 1)
        ):
            halo = jnp.where(inside, halo, 0.0)
            tail = with_sides(halo[:, last:], corner, corner, cols - last, at)
            tail = jnp.where(inside, tail, 0.0)
            for tile in range(0, width, 128):
                block = tail[:, tile - last :][:, :128] if tile >= last else halo[:, tile:][:, :128]
                natural[tile // 128, pl.ds(first, MARGIN)] = block
        for tile in range(0, width, 128):
            for v, block in enumerate(interleaved(natural.at[tile // 128], step)):
                place = (slice(8 * v, 8 * v + 8), slice(tile, tile + 128))
                if at == 3:
                    block = STEP * block
                elif at > 0:
                    block = jnp.where(wet_win[place] > 0.0, block, 0.0)
                target[place] = block
        if at in (1, 3):
            shifted = east_win if at == 1 else moved_win
            for v in range(step):
                shifted[8 * v : 8 * v + 8] = pltpu.roll(target[8 * v : 8 * v + 8], 1, 1)


def substep_kernel(
    sectors,
    bands,
    synth_ref,
    harm_ref,
    surface_win,
    east_win,
    north_win,
    wet,
    moved,
    loading_hbm,
    surface_hbm,
    east_hbm,
    north_hbm,
    column,
    load,
    pressure,
    east,
    north,
    natural,
    loading_out,
    surface_out,
    east_out,
    north_out,
    semaphores,
):
    rows, cols = loading_hbm.shape
    taller, width = wet.shape
    step = taller // 8
    waves = harm_ref.shape[0] // 2
    me, band = lax.axis_index("lon"), lax.axis_index("lat")
    below, above = jnp.maximum(band - 1, 0), jnp.minimum(band + 1, bands - 1)

    def gathered(place):
        lines = [
            synth_ref[place * sectors + owner(me, sectors, core, shift)]
            for core, shift in row_groups(sectors)
        ]
        lines = jnp.concatenate(lines, axis=0)
        return lines.T

    scale = 1.0 / math.sqrt(waves // 2)
    own = gathered(band) * scale
    low = jnp.where(band > 0, gathered(below)[rows - MARGIN :], 0.0) * scale
    high = jnp.where(band < bands - 1, gathered(above), 0.0) * scale
    pieces = []
    for at in range(2):
        first = 64 * at
        column[at, :MARGIN, : waves // 2] = low[first : first + MARGIN]
        column[at, MARGIN : MARGIN + rows, : waves // 2] = own[first : first + rows]
        column[at, MARGIN + rows :, : waves // 2] = high[first : first + MARGIN]
        pieces.append(
            jnp.concatenate(interleaved(column.at[at], step), axis=0)[:, : waves // 2]
        )
    hi, lo = split2(jnp.concatenate(pieces, axis=1))
    left = jnp.concatenate(
        [jnp.concatenate([hi, hi], axis=1), jnp.concatenate([lo, lo], axis=1)], axis=0
    )
    both = lax.dot_general(
        left, harm_ref[...], (((1,), (0,)), ((), ())), preferred_element_type=f32
    )
    both = both[:taller] + both[taller:]
    load[...] = both
    pressure[...] = surface_win[...] - both
    copies = [
        pltpu.make_async_copy(source, target, semaphores.at[at])
        for at, (source, target) in enumerate(
            (
                (loading_out, loading_hbm),
                (surface_out, surface_hbm),
                (east_out, east_hbm),
                (north_out, north_hbm),
            )
        )
    ]

    def give(at, target, blocks):
        for v, block in enumerate(blocks):
            for tile in range(0, width, 128):
                natural[at, tile // 128, pl.ds(v, 8, stride=step)] = block[:, tile : tile + 128]
        for tile in range(0, cols, 128):
            stop = min(cols, tile + 128)
            target[:, tile:stop] = natural[at, tile // 128, pl.ds(MARGIN, rows), : stop - tile]
        copies[at].start()

    def block(ref, v):
        return ref[8 * v : 8 * v + 8]

    def across(ref, v):
        after = pltpu.roll(block(ref, 0), 7, 0) if v == step - 1 else block(ref, v + 1)
        before = pltpu.roll(block(ref, step - 1), 1, 0) if v == 0 else block(ref, v - 1)
        return after - before

    give(0, loading_out, [block(load, v) for v in range(step)])
    for substep in range(SUBSTEPS):
        first, final = substep == 0, substep == SUBSTEPS - 1
        for v in range(step):
            here = block(pressure, v)
            flow = block(east_win if first else east, v)
            flow = flow - block(moved, v) * (here - pltpu.roll(here, 2, 1))
            east[8 * v : 8 * v + 8] = flow
            flow = block(north_win if first else north, v)
            north[8 * v : 8 * v + 8] = flow - block(wet, v) * across(pressure, v)
        if final:
            give(2, east_out, [pltpu.roll(block(east, v), width - 1, 1) for v in range(step)])
            give(3, north_out, [block(north, v) for v in range(step)])
        levels = []
        for v in range(step):
            flow = block(east, v)
            change = pltpu.roll(flow, width - 2, 1) - flow + across(north, v)
            level = block(pressure, v) - block(wet, v) * change
            if final:
                levels.append(level + block(load, v))
            else:
                pressure[8 * v : 8 * v + 8] = level
        if final:
            give(1, surface_out, levels)
    for copy in copies:
        copy.wait()


def shards(height, east_flow, north_flow, legendre, love_numbers, wavenumbers, land_sea):
    rows, cols = height.shape
    slots, _, degrees = legendre.shape
    sectors, bands = lax.axis_size("lon"), lax.axis_size("lat")
    chips = sectors // 2
    waves = wavenumbers.shape[0]
    period = cols * sectors
    width = -(-(cols + 2 * MARGIN) // 128) * 128
    taller = rows + 2 * MARGIN
    group, half = 2 * slots, rows // 2
    back = (cols - MARGIN) // 128 * 128
    DMA = pltpu.SemaphoreType.DMA
    fields = (height, east_flow, north_flow, land_sea)

    keep, send = pl.pallas_call(
        functools.partial(transform_kernel, period, slots),
        out_shape=[struct((chips, group, 128)), struct((chips * group + half, 128))],
        in_specs=[HBM] * 5,
        out_specs=[VMEM] * 2,
        scratch_shapes=[
            pltpu.SMEM((waves,), jnp.int32),
            pltpu.VMEM((rows, cols), f32),
            pltpu.VMEM((2, rows, 128), f32),
            pltpu.VMEM((2, rows, cols - back), f32),
            pltpu.VMEM((rows, 128), jnp.int32),
            pltpu.VMEM((rows, cols - back), jnp.int32),
            pltpu.VMEM((4 * waves, width), bf16),
            pltpu.VMEM((2 * rows, width), bf16),
            DMA((8,)),
        ],
        name="transform",
        compiler_params=LIMIT,
    )(*in_hbm(wavenumbers, *fields))
    core = lax.ppermute(send, "lon", [(i, i ^ 1) for i in range(sectors)])
    neighbours = (1, chips - 1)
    own, *outgoing = pl.pallas_call(
        mix_kernel,
        out_shape=[struct((group, 128))]
        + [
            struct((group + (half if shift in neighbours else 0), 128))
            for shift in range(1, chips)
        ],
        in_specs=[VMEM] * 2,
        out_specs=[VMEM] * chips,
        name="mix",
        compiler_params=LIMIT,
    )(keep, core)
    arrived = [
        lax.ppermute(
            block, "lon", [(i, (i + 2 * shift) % sectors) for i in range(sectors)]
        )
        for shift, block in enumerate(outgoing, 1)
    ]
    sides = (core, arrived[0], arrived[-1])

    even, odd, legendre = pl.pallas_call(
        stage_kernel,
        out_shape=[struct((4, MARGIN, width))] * 2 + [struct(legendre.shape)],
        in_specs=[VMEM] + [HBM] * 5,
        out_specs=[VMEM] * 3,
        scratch_shapes=[
            pltpu.VMEM((2, 3, MARGIN, cols), f32),
            pltpu.VMEM((2, MARGIN, cols), jnp.int32),
            DMA((9,)),
        ],
        name="stage",
        compiler_params=LIMIT,
    )(own, *in_hbm(*fields, legendre))
    links = [[(i, i + 1) for i in range(first, bands - 1, 2)] for first in (0, 1)]
    links = [pairs + [(j, i) for i, j in pairs] for pairs in links]
    even, odd = [lax.ppermute(block, "lat", pairs) for block, pairs in zip((even, odd), links)]

    def analysis(*refs):
        analysis_kernel(refs[:chips], *refs[chips:])

    together = bands == 4
    message = 128 + (degrees if together else 0)
    spectral, *corners = pl.pallas_call(
        analysis,
        out_shape=[struct((group, degrees))] + [struct((MARGIN, message))] * 2,
        in_specs=[VMEM] * (chips + 2),
        out_specs=[VMEM] * 3,
        name="analysis",
        compiler_params=LIMIT,
    )(own, *arrived, core, legendre)
    if together:
        *corners, across = [
            lax.ppermute(block, "lat", [(i, i ^ step) for i in range(bands)])
            for block, step in ((corners[0], 1), (corners[1], 3), (spectral, 2))
        ]
        pieces = [spectral, *corners, across]
    else:
        corners = [
            lax.ppermute(block, "lat", pairs) for block, pairs in zip(corners, links)
        ]
        pieces = [lax.psum(spectral, "lat")]

    def synthesis(*refs):
        synthesis_kernel(refs[: len(pieces)], *refs[len(pieces) :])

    synth = pl.pallas_call(
        synthesis,
        out_shape=struct((bands * sectors, slots, 128)),
        in_specs=[VMEM] * (len(pieces) + 2),
        out_specs=VMEM,
        scratch_shapes=[pltpu.VMEM((group, degrees), f32)],
        name="synthesis",
        cost_estimate=pl.CostEstimate(flops=100000000000, bytes_accessed=400000000, transcendentals=0),
        compiler_params=LIMIT,
    )(*pieces, love_numbers.reshape(1, degrees), legendre)
    everyone = lax.all_to_all(synth, ("lat", "lon"), 0, 0, tiled=True)

    *windows, harmonics = pl.pallas_call(
        functools.partial(windows_kernel, period, slots, chips, bands),
        out_shape=[struct((taller, width))] * 5 + [struct((4 * waves, width), bf16)],
        in_specs=[HBM] * 5 + [VMEM] * 7,
        out_specs=[VMEM] * 6,
        scratch_shapes=[
            pltpu.SMEM((waves,), jnp.int32),
            pltpu.VMEM((3, rows, cols), f32),
            pltpu.VMEM((rows, cols), jnp.int32),
            pltpu.VMEM((width // 128, taller, 128), f32),
            DMA((5,)),
        ],
        name="windows",
        cost_estimate=pl.CostEstimate(flops=10**11, bytes_accessed=4 * 10**8, transcendentals=0),
        compiler_params=LIMIT,
    )(*in_hbm(wavenumbers, *fields), *sides, even, odd, *corners)

    return pl.pallas_call(
        functools.partial(substep_kernel, sectors, bands),
        out_shape=[struct((rows, cols))] * 4,
        in_specs=[VMEM] * 7,
        out_specs=[HBM] * 4,
        scratch_shapes=[
            pltpu.VMEM((2, taller, 128), f32),
            pltpu.VMEM((taller, width), f32),
            pltpu.VMEM((taller, width), f32),
            pltpu.VMEM((taller, width), f32),
            pltpu.VMEM((taller, width), f32),
            pltpu.VMEM((4, width // 128, taller, 128), f32),
        ]
        + [pltpu.VMEM((rows, cols), f32)] * 4
        + [DMA((4,))],
        name="substeps",
        compiler_params=LIMIT,
    )(everyone, harmonics, *windows)


def solution(mesh):
    return jax.shard_map(
        shards,
        mesh=mesh,
        in_specs=(
            P("lat", "lon"),
            P("lat", "lon"),
            P("lat", "lon"),
            P("lon", "lat", None),
            P(),
            P(),
            P("lat", "lon"),
        ),
        out_specs=(P("lat", "lon"), P("lat", "lon"), P("lat", "lon"), P("lat", "lon")),
        check_vma=False,
    )
```

```python
import functools
import math

import jax
import jax.numpy as jnp
from jax import lax
from jax.experimental import pallas as pl
from jax.experimental.pallas import tpu as pltpu
from jax.sharding import PartitionSpec as P

SUBSTEPS = 4
MARGIN = 2 * SUBSTEPS
STEP = 0.3

f32 = jnp.float32
bf16 = jnp.bfloat16
VMEM = pl.BlockSpec(memory_space=pltpu.VMEM)
HBM = pl.BlockSpec(memory_space=pltpu.HBM)
SMEM = pl.BlockSpec(memory_space=pltpu.SMEM)
LIMIT = pltpu.CompilerParams(vmem_limit_bytes=24 * 2**20)


def struct(shape, dtype=f32):
    return jax.ShapeDtypeStruct(shape, dtype)


def in_hbm(*arrays):
    return [pltpu.with_memory_space_constraint(x, pltpu.HBM) for x in arrays]


def split2(x):
    hi = x.astype(bf16)
    lo = (x - hi.astype(f32)).astype(bf16)
    return hi, lo


def owner(me, sectors, core, shift):
    chips = sectors // 2
    crossed = core if shift == 0 else 1 - core
    return 2 * lax.rem(me // 2 + shift, chips) + lax.bitwise_xor(lax.rem(me, 2), crossed)


def row_groups(sectors):
    return [(core, shift) for core in range(2) for shift in range(sectors // 2)]


def harmonic_rows(period, cols, slots, me, paired, waves_ref, harm_ref):
    waves, width = harm_ref.shape[0] // 2, harm_ref.shape[1]
    sectors = waves // (2 * slots)
    order = []
    for core, shift in row_groups(sectors):
        first = owner(me, sectors, core, shift) * slots
        group = [waves_ref[first + slot] for slot in range(slots)]
        order += group + group if paired else group
    if not paired:
        order = order + order
    row = lax.broadcasted_iota(jnp.int32, (8, 1), 0)
    blocks = []
    for first in range(0, waves, 8):
        block = jnp.zeros((8, 1), jnp.int32)
        for at, value in enumerate(order[first : first + 8]):
            block = jnp.where(row == at, value, block)
        blocks.append(block)
    wave = jnp.concatenate(blocks, axis=0)
    start = wave * (me * cols)
    turns = jnp.floor(start.astype(f32) * (1.0 / period)).astype(jnp.int32)
    start = (start - turns * period).astype(f32)
    wave = wave.astype(f32)
    row = lax.broadcasted_iota(jnp.int32, (waves, 1), 0)
    if paired:
        row = lax.rem(row, 2 * slots)
    sine = (row >= (slots if paired else waves // 2)).astype(f32)
    offset = 4.0 * start - period * sine
    for tile in range(0, width, 128):
        lane = lax.broadcasted_iota(jnp.int32, (1, 128), 1) + tile
        lane = jnp.where(lane < cols + MARGIN, lane, lane - width).astype(f32)
        product = wave * lane
        product = product - period * jnp.floor(product * (1.0 / period))
        quarter = 4.0 * product + offset
        turn = jnp.floor(quarter * (1.0 / period) + 0.5)
        angle = (quarter - period * turn) * (0.5 * math.pi / period)
        square = angle * angle
        cosine = 1.0 + square * (
            -1.0 / 2 + square * (1.0 / 24 + square * (-1.0 / 720 + square * (1.0 / 40320)))
        )
        sine_of = angle * (
            1.0
            + square
            * (-1.0 / 6 + square * (1.0 / 120 + square * (-1.0 / 5040 + square * (1.0 / 362880))))
        )
        phase = turn - 4.0 * jnp.floor(turn * 0.25)
        odd = (phase == 1.0) | (phase == 3.0)
        value = jnp.where(odd, sine_of, cosine)
        value = jnp.where((phase == 1.0) | (phase == 2.0), -value, value)
        hi, lo = split2(value)
        harm_ref[:waves, tile : tile + 128] = hi
        harm_ref[waves:, tile : tile + 128] = lo


def transform_kernel(
    period,
    slots,
    waves_hbm,
    height_hbm,
    east_hbm,
    north_hbm,
    land_hbm,
    keep_ref,
    send_ref,
    tile_ref,
    waves_ref,
    height_ref,
    flow_front,
    flow_back,
    land_front,
    land_back,
    harm_ref,
    field_ref,
    semaphores,
):
    rows, cols = height_ref.shape
    waves, width = harm_ref.shape[0] // 2, harm_ref.shape[1]
    back = cols - land_back.shape[1]
    fronts, backs = pl.ds(0, 128), pl.ds(back, cols - back)
    copies = [
        pltpu.make_async_copy(source, target, semaphores.at[at])
        for at, (source, target) in enumerate(
            (
                (waves_hbm, waves_ref),
                (height_hbm, height_ref),
                (east_hbm.at[:, fronts], flow_front.at[0]),
                (east_hbm.at[:, backs], flow_back.at[0]),
                (north_hbm.at[:, fronts], flow_front.at[1]),
                (north_hbm.at[:, backs], flow_back.at[1]),
                (land_hbm.at[:, fronts], land_front),
                (land_hbm.at[:, backs], land_back),
            )
        )
    ]
    for copy in copies:
        copy.start()
    copies[0].wait()
    harmonic_rows(period, cols, slots, lax.axis_index("lon"), True, waves_ref, harm_ref)
    copies[1].wait()
    for tile in range(0, width, 128):
        stop = min(cols, tile + 128)
        if stop <= tile:
            block = jnp.zeros((rows, 128), f32)
        elif stop == tile + 128:
            block = height_ref[:, tile : tile + 128]
        else:
            block = jnp.concatenate(
                [height_ref[:, tile:stop], jnp.zeros((rows, tile + 128 - stop), f32)], axis=1
            )
        hi, lo = split2(block)
        field_ref[:rows, tile : tile + 128] = hi
        field_ref[rows:, tile : tile + 128] = lo
    rows_by_rows = (((1,), (1,)), ((), ()))
    high = lax.dot_general(
        harm_ref[...], field_ref[:rows], rows_by_rows, preferred_element_type=f32
    )
    low = lax.dot_general(
        harm_ref[:waves], field_ref[rows:], rows_by_rows, preferred_element_type=f32
    )
    total = (high[:waves] + high[waves:] + low) * (1.0 / math.sqrt(period))
    total = jnp.concatenate([total, jnp.zeros((waves, 128 - rows), f32)], axis=1)
    keep_ref[...] = total[: waves // 2].reshape(keep_ref.shape)
    send_ref[: waves // 2] = total[waves // 2 :]
    for copy in copies[2:]:
        copy.wait()
    pieces = []
    for front, end in (
        (height_ref[:, :MARGIN], height_ref[:, cols - MARGIN :]),
        (flow_front[0, :, :MARGIN], flow_back[0, :, cols - MARGIN - back :]),
        (flow_front[1, :, :MARGIN], flow_back[1, :, cols - MARGIN - back :]),
        (land_front[:, :MARGIN].astype(f32), land_back[:, cols - MARGIN - back :].astype(f32)),
    ):
        pieces += [front, end]
    half = rows // 2
    tile = jnp.concatenate(
        [piece[:half] for piece in pieces] + [piece[half:] for piece in pieces], axis=1
    )
    send_ref[waves // 2 :] = tile
    tile_ref[...] = tile


def stage_kernel(
    after_ref,
    height_hbm,
    east_hbm,
    north_hbm,
    land_hbm,
    legendre_hbm,
    even_ref,
    odd_ref,
    legendre_ref,
    flows,
    lands,
    semaphores,
):
    rows, cols = height_hbm.shape
    width = even_ref.shape[2]
    copies = []
    for side, first in enumerate((rows - MARGIN, 0)):
        band = pl.ds(first, MARGIN)
        copies.append((height_hbm.at[band], flows.at[side, 0]))
        copies.append((east_hbm.at[band], flows.at[side, 1]))
        copies.append((north_hbm.at[band], flows.at[side, 2]))
        copies.append((land_hbm.at[band], lands.at[side]))
    copies.append((legendre_hbm, legendre_ref))
    copies = [
        pltpu.make_async_copy(source, target, semaphores.at[at])
        for at, (source, target) in enumerate(copies)
    ]
    for copy in copies:
        copy.start()
    for copy in copies[:-1]:
        copy.wait()
    is_even = lax.rem(lax.axis_index("lat"), 2) == 0
    for at in range(4):
        up, down = [lands[side].astype(f32) if at == 3 else flows[side, at] for side in range(2)]
        even_ref[at, :, :cols] = jnp.where(is_even, up, down)
        odd_ref[at, :, :cols] = jnp.where(is_even, down, up)
        if cols < width:
            blank = jnp.zeros((MARGIN, width - cols), f32)
            even_ref[at, :, cols:] = blank
            odd_ref[at, :, cols:] = blank
    copies[-1].wait()


def mix_kernel(keep_ref, tile_ref, recv_ref, own_ref, *send_refs):
    chips, group, _ = keep_ref.shape
    own_ref[...] = keep_ref[0] + recv_ref[:group]
    for shift, ref in enumerate(send_refs, 1):
        ref[:group] = keep_ref[shift] + recv_ref[shift * group : (shift + 1) * group]
        if ref.shape[0] > group:
            ref[group:] = tile_ref[...]


def analysis_kernel(part_refs, core_ref, legendre_ref, spectral_ref, even_ref, odd_ref):
    slots, rows, degrees = legendre_ref.shape
    chips, half = len(part_refs), rows // 2
    left, right = side_tiles(lax.axis_index("lon"), 2 * slots, chips, core_ref, part_refs[1], part_refs[-1])
    lanes = lax.broadcasted_iota(jnp.int32, left.shape, 1)
    both = jnp.where(lax.rem(lanes, 2 * MARGIN) < MARGIN, right, left)
    up, down = pltpu.roll(both[half - MARGIN :], 64, 1), both[:MARGIN]
    is_even = lax.rem(lax.axis_index("lat"), 2) == 0
    ahead = even_ref.shape[1] - 128
    even_ref[:, ahead:] = jnp.where(is_even, up, down)
    odd_ref[:, ahead:] = jnp.where(is_even, down, up)
    fourier = part_refs[0][...]
    for ref in part_refs[1:]:
        fourier = fourier + ref[: 2 * slots]
    columns = fourier.T
    for slot in range(slots):
        even = [
            jnp.broadcast_to(columns[o : o + 8, slot : slot + 1], (8, 128))
            for o in range(0, rows, 8)
        ]
        odd = [
            jnp.broadcast_to(columns[o : o + 8, slots + slot : slots + slot + 1], (8, 128))
            for o in range(0, rows, 8)
        ]
        for tile in range(0, degrees, 128):
            first = jnp.zeros((8, 128), f32)
            second = jnp.zeros((8, 128), f32)
            for at, o in enumerate(range(0, rows, 8)):
                block = legendre_ref[slot, o : o + 8, tile : tile + 128]
                first = first + block * even[at]
                second = second + block * odd[at]
            spectral_ref[slot : slot + 1, tile : tile + 128] = jnp.sum(
                first, axis=0, keepdims=True
            )
            spectral_ref[slots + slot : slots + slot + 1, tile : tile + 128] = jnp.sum(
                second, axis=0, keepdims=True
            )
    if ahead:
        even_ref[:, :ahead] = spectral_ref[...]
        odd_ref[:, :ahead] = spectral_ref[...]

def synthesis_kernel(parts_refs, love_ref, legendre_ref, out_ref, spectral_ref):
    slots, rows, degrees = legendre_ref.shape
    total = parts_refs[0][...]
    for ref in parts_refs[1:]:
        total = total + ref[:, :degrees]
    spectral_ref[...] = total * love_ref[...]
    lanes = lax.broadcasted_iota(jnp.int32, (8, 128), 1)
    octets = range(0, rows, 8)
    sums = [jnp.zeros((8, 128), f32) for _ in octets]
    for slot in range(slots):
        first = [jnp.zeros((8, 128), f32) for _ in octets]
        second = [jnp.zeros((8, 128), f32) for _ in octets]
        for tile in range(0, degrees, 128):
            even = jnp.broadcast_to(spectral_ref[slot : slot + 1, tile : tile + 128], (8, 128))
            odd = jnp.broadcast_to(
                spectral_ref[slots + slot : slots + slot + 1, tile : tile + 128], (8, 128)
            )
            for at, o in enumerate(octets):
                block = legendre_ref[slot, o : o + 8, tile : tile + 128]
                first[at] = first[at] + block * even
                second[at] = second[at] + block * odd
        for at in range(len(octets)):
            sums[at] = jnp.where(lanes == slot, jnp.sum(first[at], axis=1, keepdims=True), sums[at])
            sums[at] = jnp.where(
                lanes == slots + slot, jnp.sum(second[at], axis=1, keepdims=True), sums[at]
            )
    column = jnp.concatenate(sums + [jnp.zeros((128 - rows, 128), f32)], axis=0)
    lines = column.T[: 2 * slots]
    lines = lines[:slots] + pltpu.roll(lines[slots:], 64, 1)
    out_ref[...] = jnp.broadcast_to(lines[None], out_ref.shape)


def side_tiles(me, group, chips, core_ref, west_ref, east_ref):
    first = lax.rem(me, 2) == 0
    other = core_ref[chips * group :]
    left = jnp.where(first, west_ref[group:], other)
    right = jnp.where(first, other, east_ref[group:])
    return left, right


def with_sides(tail, left, right, own, at):
    lanes = lax.broadcasted_iota(jnp.int32, tail.shape, 1)
    after = pltpu.roll(right, (own - 2 * MARGIN * at) % 128, 1)
    before = pltpu.roll(left, (-MARGIN - 2 * MARGIN * at - MARGIN) % 128, 1)
    repeat = tail.shape[1] // 128
    after = jnp.concatenate([after] * repeat, axis=1)
    before = jnp.concatenate([before] * repeat, axis=1)
    tail = jnp.where((lanes >= own) & (lanes < own + MARGIN), after, tail)
    return jnp.where(lanes >= tail.shape[1] - MARGIN, before, tail)


def interleaved(ref, step):
    return [ref[pl.ds(at, 8, stride=step)] for at in range(step)]


def windows_kernel(
    period,
    slots,
    chips,
    bands,
    waves_hbm,
    height_hbm,
    east_hbm,
    north_hbm,
    land_hbm,
    core_ref,
    west_ref,
    east_ref,
    even_rows,
    odd_rows,
    even_ref,
    odd_ref,
    surface_win,
    east_win,
    north_win,
    wet_win,
    moved_win,
    harm_ref,
    waves_ref,
    fields,
    land,
    natural,
    semaphores,
):
    rows, cols = height_hbm.shape
    width = harm_ref.shape[1]
    taller = rows + 2 * MARGIN
    step = taller // 8
    last = (cols // 128) * 128
    copies = [
        pltpu.make_async_copy(source, target, semaphores.at[at])
        for at, (source, target) in enumerate(
            (
                (height_hbm, fields.at[0]),
                (east_hbm, fields.at[1]),
                (north_hbm, fields.at[2]),
                (land_hbm, land),
                (waves_hbm, waves_ref),
            )
        )
    ]
    for copy in copies:
        copy.start()
    copies[4].wait()
    harmonic_rows(period, cols, slots, lax.axis_index("lon"), False, waves_ref, harm_ref)
    left, right = side_tiles(
        lax.axis_index("lon"), 2 * slots, chips, core_ref, west_ref, east_ref
    )
    left = jnp.concatenate([left, pltpu.roll(left, 64, 1)], axis=0)
    right = jnp.concatenate([right, pltpu.roll(right, 64, 1)], axis=0)
    band = lax.axis_index("lat")
    is_even = lax.rem(band, 2) == 0
    even, odd = even_ref[:, -128:], odd_ref[:, -128:]
    corners = (jnp.where(is_even, odd, even), jnp.where(is_even, even, odd))
    for copy in copies[:4]:
        copy.wait()
    middle = pl.ds(MARGIN, rows)
    for at, target in ((3, wet_win), (0, surface_win), (1, east_win), (2, north_win)):
        field = fields.at[at] if at < 3 else land
        even, odd = even_rows[at], odd_rows[at]
        halos = (jnp.where(is_even, odd, even), jnp.where(is_even, even, odd))
        for tile in range(0, last, 128):
            natural[tile // 128, middle] = field[:, tile : tile + 128].astype(f32)
        tail = jnp.concatenate(
            [field[:, last:].astype(f32), jnp.zeros((rows, width - cols), f32)], axis=1
        )
        tail = with_sides(tail, left, right, cols - last, at)
        for tile in range(last, width, 128):
            natural[tile // 128, middle] = tail[:, tile - last : tile - last + 128]
        for halo, corner, first, inside in zip(
            halos, corners, (0, MARGIN + rows), (band > 0, band < bands - 1)
        ):
            halo = jnp.where(inside, halo, 0.0)
            tail = with_sides(halo[:, last:], corner, corner, cols - last, at)
            tail = jnp.where(inside, tail, 0.0)
            for tile in range(0, width, 128):
                block = tail[:, tile - last :][:, :128] if tile >= last else halo[:, tile:][:, :128]
                natural[tile // 128, pl.ds(first, MARGIN)] = block
        for tile in range(0, width, 128):
            for v, block in enumerate(interleaved(natural.at[tile // 128], step)):
                place = (slice(8 * v, 8 * v + 8), slice(tile, tile + 128))
                if at == 3:
                    block = STEP * block
                elif at > 0:
                    block = jnp.where(wet_win[place] > 0.0, block, 0.0)
                target[place] = block
        if at in (1, 3):
            shifted = east_win if at == 1 else moved_win
            for v in range(step):
                shifted[8 * v : 8 * v + 8] = pltpu.roll(target[8 * v : 8 * v + 8], 1, 1)


def substep_kernel(
    sectors,
    bands,
    synth_ref,
    harm_ref,
    surface_win,
    east_win,
    north_win,
    wet,
    moved,
    loading_hbm,
    surface_hbm,
    east_hbm,
    north_hbm,
    column,
    load,
    pressure,
    east,
    north,
    natural,
    loading_out,
    surface_out,
    east_out,
    north_out,
    semaphores,
):
    rows, cols = loading_hbm.shape
    taller, width = wet.shape
    step = taller // 8
    waves = harm_ref.shape[0] // 2
    me, band = lax.axis_index("lon"), lax.axis_index("lat")
    below, above = jnp.maximum(band - 1, 0), jnp.minimum(band + 1, bands - 1)

    def gathered(place):
        lines = [
            synth_ref[place * sectors + owner(me, sectors, core, shift)]
            for core, shift in row_groups(sectors)
        ]
        lines = jnp.concatenate(lines, axis=0)
        return lines.T

    scale = 1.0 / math.sqrt(waves // 2)
    own = gathered(band) * scale
    low = jnp.where(band > 0, gathered(below)[rows - MARGIN :], 0.0) * scale
    high = jnp.where(band < bands - 1, gathered(above), 0.0) * scale
    pieces = []
    for at in range(2):
        first = 64 * at
        column[at, :MARGIN, : waves // 2] = low[first : first + MARGIN]
        column[at, MARGIN : MARGIN + rows, : waves // 2] = own[first : first + rows]
        column[at, MARGIN + rows :, : waves // 2] = high[first : first + MARGIN]
        pieces.append(
            jnp.concatenate(interleaved(column.at[at], step), axis=0)[:, : waves // 2]
        )
    hi, lo = split2(jnp.concatenate(pieces, axis=1))
    left = jnp.concatenate(
        [jnp.concatenate([hi, hi], axis=1), jnp.concatenate([lo, lo], axis=1)], axis=0
    )
    both = lax.dot_general(
        left, harm_ref[...], (((1,), (0,)), ((), ())), preferred_element_type=f32
    )
    both = both[:taller] + both[taller:]
    load[...] = both
    pressure[...] = surface_win[...] - both
    copies = [
        pltpu.make_async_copy(source, target, semaphores.at[at])
        for at, (source, target) in enumerate(
            (
                (loading_out, loading_hbm),
                (surface_out, surface_hbm),
                (east_out, east_hbm),
                (north_out, north_hbm),
            )
        )
    ]

    def give(at, target, blocks):
        for v, block in enumerate(blocks):
            for tile in range(0, width, 128):
                natural[at, tile // 128, pl.ds(v, 8, stride=step)] = block[:, tile : tile + 128]
        for tile in range(0, cols, 128):
            stop = min(cols, tile + 128)
            target[:, tile:stop] = natural[at, tile // 128, pl.ds(MARGIN, rows), : stop - tile]
        copies[at].start()

    def block(ref, v):
        return ref[8 * v : 8 * v + 8]

    def across(ref, v):
        after = pltpu.roll(block(ref, 0), 7, 0) if v == step - 1 else block(ref, v + 1)
        before = pltpu.roll(block(ref, step - 1), 1, 0) if v == 0 else block(ref, v - 1)
        return after - before

    give(0, loading_out, [block(load, v) for v in range(step)])
    for substep in range(SUBSTEPS):
        first, final = substep == 0, substep == SUBSTEPS - 1
        for v in range(step):
            here = block(pressure, v)
            flow = block(east_win if first else east, v)
            flow = flow - block(moved, v) * (here - pltpu.roll(here, 2, 1))
            east[8 * v : 8 * v + 8] = flow
            flow = block(north_win if first else north, v)
            north[8 * v : 8 * v + 8] = flow - block(wet, v) * across(pressure, v)
        if final:
            give(2, east_out, [pltpu.roll(block(east, v), width - 1, 1) for v in range(step)])
            give(3, north_out, [block(north, v) for v in range(step)])
        levels = []
        for v in range(step):
            flow = block(east, v)
            change = pltpu.roll(flow, width - 2, 1) - flow + across(north, v)
            level = block(pressure, v) - block(wet, v) * change
            if final:
                levels.append(level + block(load, v))
            else:
                pressure[8 * v : 8 * v + 8] = level
        if final:
            give(1, surface_out, levels)
    for copy in copies:
        copy.wait()


def shards(height, east_flow, north_flow, legendre, love_numbers, wavenumbers, land_sea):
    rows, cols = height.shape
    slots, _, degrees = legendre.shape
    sectors, bands = lax.axis_size("lon"), lax.axis_size("lat")
    chips = sectors // 2
    waves = wavenumbers.shape[0]
    period = cols * sectors
    width = -(-(cols + 2 * MARGIN) // 128) * 128
    taller = rows + 2 * MARGIN
    group, half = 2 * slots, rows // 2
    back = (cols - MARGIN) // 128 * 128
    DMA = pltpu.SemaphoreType.DMA
    fields = (height, east_flow, north_flow, land_sea)

    keep, send, tile = pl.pallas_call(
        functools.partial(transform_kernel, period, slots),
        out_shape=[
            struct((chips, group, 128)),
            struct((chips * group + half, 128)),
            struct((half, 128)),
        ],
        in_specs=[HBM] * 5,
        out_specs=[VMEM] * 3,
        scratch_shapes=[
            pltpu.SMEM((waves,), jnp.int32),
            pltpu.VMEM((rows, cols), f32),
            pltpu.VMEM((2, rows, 128), f32),
            pltpu.VMEM((2, rows, cols - back), f32),
            pltpu.VMEM((rows, 128), jnp.int32),
            pltpu.VMEM((rows, cols - back), jnp.int32),
            pltpu.VMEM((4 * waves, width), bf16),
            pltpu.VMEM((2 * rows, width), bf16),
            DMA((8,)),
        ],
        name="transform",
        compiler_params=LIMIT,
    )(*in_hbm(wavenumbers, *fields))
    core = lax.ppermute(send, "lon", [(i, i ^ 1) for i in range(sectors)])
    neighbours = (1, chips - 1)
    own, *outgoing = pl.pallas_call(
        mix_kernel,
        out_shape=[struct((group, 128))]
        + [
            struct((group + (half if shift in neighbours else 0), 128))
            for shift in range(1, chips)
        ],
        in_specs=[VMEM] * 3,
        out_specs=[VMEM] * chips,
        name="mix",
        compiler_params=LIMIT,
    )(keep, tile, core)
    arrived = []
    for shift, block in enumerate(outgoing, 1):
        across = [(i, 2 * ((i // 2 + shift) % chips) + 1 - i % 2) for i in range(sectors)]
        arrived.append(lax.ppermute(block, "lon", across))
    sides = (core, arrived[0], arrived[-1])

    even, odd, legendre = pl.pallas_call(
        stage_kernel,
        out_shape=[struct((4, MARGIN, width))] * 2 + [struct(legendre.shape)],
        in_specs=[VMEM] + [HBM] * 5,
        out_specs=[VMEM] * 3,
        scratch_shapes=[
            pltpu.VMEM((2, 3, MARGIN, cols), f32),
            pltpu.VMEM((2, MARGIN, cols), jnp.int32),
            DMA((9,)),
        ],
        name="stage",
        compiler_params=LIMIT,
    )(own, *in_hbm(*fields, legendre))
    links = [[(i, (i + 1) % bands) for i in range(first, bands, 2)] for first in (0, 1)]
    links = [pairs + [(j, i) for i, j in pairs] for pairs in links]
    even, odd = [lax.ppermute(block, "lat", pairs) for block, pairs in zip((even, odd), links)]

    def analysis(*refs):
        analysis_kernel(refs[:chips], *refs[chips:])

    together = bands == 4
    message = 128 + (degrees if together else 0)
    spectral, *corners = pl.pallas_call(
        analysis,
        out_shape=[struct((group, degrees))] + [struct((MARGIN, message))] * 2,
        in_specs=[VMEM] * (chips + 2),
        out_specs=[VMEM] * 3,
        name="analysis",
        compiler_params=LIMIT,
    )(own, *arrived, core, legendre)
    if together:
        *corners, across = [
            lax.ppermute(block, "lat", [(i, i ^ step) for i in range(bands)])
            for block, step in ((corners[0], 1), (corners[1], 3), (spectral, 2))
        ]
        pieces = [spectral, *corners, across]
    else:
        corners = [
            lax.ppermute(block, "lat", pairs) for block, pairs in zip(corners, links)
        ]
        pieces = [lax.psum(spectral, "lat")]

    def synthesis(*refs):
        synthesis_kernel(refs[: len(pieces)], *refs[len(pieces) :])

    synth = pl.pallas_call(
        synthesis,
        out_shape=struct((bands * sectors, slots, 128)),
        in_specs=[VMEM] * (len(pieces) + 2),
        out_specs=VMEM,
        scratch_shapes=[pltpu.VMEM((group, degrees), f32)],
        name="synthesis",
        cost_estimate=pl.CostEstimate(flops=100000000000, bytes_accessed=400000000, transcendentals=0),
        compiler_params=LIMIT,
    )(*pieces, love_numbers.reshape(1, degrees), legendre)
    everyone = lax.all_to_all(synth, ("lat", "lon"), 0, 0, tiled=True)

    *windows, harmonics = pl.pallas_call(
        functools.partial(windows_kernel, period, slots, chips, bands),
        out_shape=[struct((taller, width))] * 5 + [struct((4 * waves, width), bf16)],
        in_specs=[HBM] * 5 + [VMEM] * 7,
        out_specs=[VMEM] * 6,
        scratch_shapes=[
            pltpu.SMEM((waves,), jnp.int32),
            pltpu.VMEM((3, rows, cols), f32),
            pltpu.VMEM((rows, cols), jnp.int32),
            pltpu.VMEM((width // 128, taller, 128), f32),
            DMA((5,)),
        ],
        name="windows",
        cost_estimate=pl.CostEstimate(flops=10**11, bytes_accessed=4 * 10**8, transcendentals=0),
        compiler_params=LIMIT,
    )(*in_hbm(wavenumbers, *fields), *sides, even, odd, *corners)

    return pl.pallas_call(
        functools.partial(substep_kernel, sectors, bands),
        out_shape=[struct((rows, cols))] * 4,
        in_specs=[VMEM] * 7,
        out_specs=[HBM] * 4,
        scratch_shapes=[
            pltpu.VMEM((2, taller, 128), f32),
            pltpu.VMEM((taller, width), f32),
            pltpu.VMEM((taller, width), f32),
            pltpu.VMEM((taller, width), f32),
            pltpu.VMEM((taller, width), f32),
            pltpu.VMEM((4, width // 128, taller, 128), f32),
        ]
        + [pltpu.VMEM((rows, cols), f32)] * 4
        + [DMA((4,))],
        name="substeps",
        compiler_params=LIMIT,
    )(everyone, harmonics, *windows)


def solution(mesh):
    return jax.shard_map(
        shards,
        mesh=mesh,
        in_specs=(
            P("lat", "lon"),
            P("lat", "lon"),
            P("lat", "lon"),
            P("lon", "lat", None),
            P(),
            P(),
            P("lat", "lon"),
        ),
        out_specs=(P("lat", "lon"), P("lat", "lon"), P("lat", "lon"), P("lat", "lon")),
        check_vma=False,
    )
```

```python
import functools
import math

import jax
import jax.numpy as jnp
from jax import lax
from jax.experimental import pallas as pl
from jax.experimental.pallas import tpu as pltpu
from jax.sharding import PartitionSpec as P

SUBSTEPS = 4
MARGIN = 2 * SUBSTEPS
STEP = 0.3

f32 = jnp.float32
bf16 = jnp.bfloat16
VMEM = pl.BlockSpec(memory_space=pltpu.VMEM)
HBM = pl.BlockSpec(memory_space=pltpu.HBM)
SMEM = pl.BlockSpec(memory_space=pltpu.SMEM)
LIMIT = pltpu.CompilerParams(vmem_limit_bytes=24 * 2**20)


def struct(shape, dtype=f32):
    return jax.ShapeDtypeStruct(shape, dtype)


def in_hbm(*arrays):
    return [pltpu.with_memory_space_constraint(x, pltpu.HBM) for x in arrays]


def split2(x):
    hi = x.astype(bf16)
    lo = (x - hi.astype(f32)).astype(bf16)
    return hi, lo


def owner(me, sectors, core, shift):
    chips = sectors // 2
    crossed = core if shift == 0 else 1 - core
    return 2 * lax.rem(me // 2 + shift, chips) + lax.bitwise_xor(lax.rem(me, 2), crossed)


def row_groups(sectors):
    return [(core, shift) for core in range(2) for shift in range(sectors // 2)]


def harmonic_rows(period, cols, slots, me, paired, waves_ref, harm_ref):
    waves, width = harm_ref.shape[0] // 2, harm_ref.shape[1]
    sectors = waves // (2 * slots)
    order = []
    for core, shift in row_groups(sectors):
        first = owner(me, sectors, core, shift) * slots
        group = [waves_ref[first + slot] for slot in range(slots)]
        order += group + group if paired else group
    if not paired:
        order = order + order
    row = lax.broadcasted_iota(jnp.int32, (8, 1), 0)
    blocks = []
    for first in range(0, waves, 8):
        block = jnp.zeros((8, 1), jnp.int32)
        for at, value in enumerate(order[first : first + 8]):
            block = jnp.where(row == at, value, block)
        blocks.append(block)
    wave = jnp.concatenate(blocks, axis=0)
    start = wave * (me * cols)
    turns = jnp.floor(start.astype(f32) * (1.0 / period)).astype(jnp.int32)
    start = (start - turns * period).astype(f32)
    wave = wave.astype(f32)
    row = lax.broadcasted_iota(jnp.int32, (waves, 1), 0)
    if paired:
        row = lax.rem(row, 2 * slots)
    sine = (row >= (slots if paired else waves // 2)).astype(f32)
    offset = 4.0 * start - period * sine
    for tile in range(0, width, 128):
        lane = lax.broadcasted_iota(jnp.int32, (1, 128), 1) + tile
        lane = jnp.where(lane < cols + MARGIN, lane, lane - width).astype(f32)
        product = wave * lane
        product = product - period * jnp.floor(product * (1.0 / period))
        quarter = 4.0 * product + offset
        turn = jnp.floor(quarter * (1.0 / period) + 0.5)
        angle = (quarter - period * turn) * (0.5 * math.pi / period)
        square = angle * angle
        cosine = 1.0 + square * (
            -1.0 / 2 + square * (1.0 / 24 + square * (-1.0 / 720 + square * (1.0 / 40320)))
        )
        sine_of = angle * (
            1.0
            + square
            * (-1.0 / 6 + square * (1.0 / 120 + square * (-1.0 / 5040 + square * (1.0 / 362880))))
        )
        phase = turn - 4.0 * jnp.floor(turn * 0.25)
        odd = (phase == 1.0) | (phase == 3.0)
        value = jnp.where(odd, sine_of, cosine)
        value = jnp.where((phase == 1.0) | (phase == 2.0), -value, value)
        hi, lo = split2(value)
        harm_ref[:waves, tile : tile + 128] = hi
        harm_ref[waves:, tile : tile + 128] = lo


def transform_kernel(
    period,
    slots,
    waves_hbm,
    height_hbm,
    east_hbm,
    north_hbm,
    land_hbm,
    keep_ref,
    send_ref,
    tile_ref,
    waves_ref,
    height_ref,
    flow_front,
    flow_back,
    land_front,
    land_back,
    harm_ref,
    field_ref,
    semaphores,
):
    rows, cols = height_ref.shape
    waves, width = harm_ref.shape[0] // 2, harm_ref.shape[1]
    back = cols - land_back.shape[1]
    fronts, backs = pl.ds(0, 128), pl.ds(back, cols - back)
    copies = [
        pltpu.make_async_copy(source, target, semaphores.at[at])
        for at, (source, target) in enumerate(
            (
                (waves_hbm, waves_ref),
                (height_hbm, height_ref),
                (east_hbm.at[:, fronts], flow_front.at[0]),
                (east_hbm.at[:, backs], flow_back.at[0]),
                (north_hbm.at[:, fronts], flow_front.at[1]),
                (north_hbm.at[:, backs], flow_back.at[1]),
                (land_hbm.at[:, fronts], land_front),
                (land_hbm.at[:, backs], land_back),
            )
        )
    ]
    for copy in copies:
        copy.start()
    copies[0].wait()
    harmonic_rows(period, cols, slots, lax.axis_index("lon"), True, waves_ref, harm_ref)
    copies[1].wait()
    for tile in range(0, width, 128):
        stop = min(cols, tile + 128)
        if stop <= tile:
            block = jnp.zeros((rows, 128), f32)
        elif stop == tile + 128:
            block = height_ref[:, tile : tile + 128]
        else:
            block = jnp.concatenate(
                [height_ref[:, tile:stop], jnp.zeros((rows, tile + 128 - stop), f32)], axis=1
            )
        hi, lo = split2(block)
        field_ref[:rows, tile : tile + 128] = hi
        field_ref[rows:, tile : tile + 128] = lo
    rows_by_rows = (((1,), (1,)), ((), ()))
    high = lax.dot_general(
        harm_ref[...], field_ref[:rows], rows_by_rows, preferred_element_type=f32
    )
    low = lax.dot_general(
        harm_ref[:waves], field_ref[rows:], rows_by_rows, preferred_element_type=f32
    )
    total = (high[:waves] + high[waves:] + low) * (1.0 / math.sqrt(period))
    total = jnp.concatenate([total, jnp.zeros((waves, 128 - rows), f32)], axis=1)
    keep_ref[...] = total[: waves // 2].reshape(keep_ref.shape)
    send_ref[: waves // 2] = total[waves // 2 :]
    for copy in copies[2:]:
        copy.wait()
    pieces = []
    for front, end in (
        (height_ref[:, :MARGIN], height_ref[:, cols - MARGIN :]),
        (flow_front[0, :, :MARGIN], flow_back[0, :, cols - MARGIN - back :]),
        (flow_front[1, :, :MARGIN], flow_back[1, :, cols - MARGIN - back :]),
        (land_front[:, :MARGIN].astype(f32), land_back[:, cols - MARGIN - back :].astype(f32)),
    ):
        pieces += [front, end]
    half = rows // 2
    tile = jnp.concatenate(
        [piece[:half] for piece in pieces] + [piece[half:] for piece in pieces], axis=1
    )
    send_ref[waves // 2 :] = tile
    tile_ref[...] = tile


def stage_kernel(
    after_ref,
    height_hbm,
    east_hbm,
    north_hbm,
    land_hbm,
    legendre_hbm,
    even_ref,
    odd_ref,
    legendre_ref,
    flows,
    lands,
    semaphores,
):
    rows, cols = height_hbm.shape
    width = even_ref.shape[2]
    copies = []
    for side, first in enumerate((rows - MARGIN, 0)):
        band = pl.ds(first, MARGIN)
        copies.append((height_hbm.at[band], flows.at[side, 0]))
        copies.append((east_hbm.at[band], flows.at[side, 1]))
        copies.append((north_hbm.at[band], flows.at[side, 2]))
        copies.append((land_hbm.at[band], lands.at[side]))
    copies.append((legendre_hbm, legendre_ref))
    copies = [
        pltpu.make_async_copy(source, target, semaphores.at[at])
        for at, (source, target) in enumerate(copies)
    ]
    for copy in copies:
        copy.start()
    for copy in copies[:-1]:
        copy.wait()
    is_even = lax.rem(lax.axis_index("lat"), 2) == 0
    for at in range(4):
        up, down = [lands[side].astype(f32) if at == 3 else flows[side, at] for side in range(2)]
        even_ref[at, :, :cols] = jnp.where(is_even, up, down)
        odd_ref[at, :, :cols] = jnp.where(is_even, down, up)
        if cols < width:
            blank = jnp.zeros((MARGIN, width - cols), f32)
            even_ref[at, :, cols:] = blank
            odd_ref[at, :, cols:] = blank
    copies[-1].wait()


def mix_kernel(keep_ref, tile_ref, recv_ref, own_ref, *send_refs):
    chips, group, _ = keep_ref.shape
    own_ref[...] = keep_ref[0] + recv_ref[:group]
    for shift, ref in enumerate(send_refs, 1):
        ref[:group] = keep_ref[shift] + recv_ref[shift * group : (shift + 1) * group]
        if ref.shape[0] > group:
            ref[group:] = tile_ref[...]


def analysis_kernel(part_refs, core_ref, legendre_ref, spectral_ref, even_ref, odd_ref):
    slots, rows, degrees = legendre_ref.shape
    chips, half = len(part_refs), rows // 2
    left, right = side_tiles(lax.axis_index("lon"), 2 * slots, chips, core_ref, part_refs[1], part_refs[-1])
    lanes = lax.broadcasted_iota(jnp.int32, left.shape, 1)
    both = jnp.where(lax.rem(lanes, 2 * MARGIN) < MARGIN, right, left)
    up, down = pltpu.roll(both[half - MARGIN :], 64, 1), both[:MARGIN]
    is_even = lax.rem(lax.axis_index("lat"), 2) == 0
    ahead = even_ref.shape[1] - 128
    even_ref[:, ahead:] = jnp.where(is_even, up, down)
    odd_ref[:, ahead:] = jnp.where(is_even, down, up)
    fourier = part_refs[0][...]
    for ref in part_refs[1:]:
        fourier = fourier + ref[: 2 * slots]
    columns = fourier.T
    for slot in range(slots):
        even = [
            jnp.broadcast_to(columns[o : o + 8, slot : slot + 1], (8, 128))
            for o in range(0, rows, 8)
        ]
        odd = [
            jnp.broadcast_to(columns[o : o + 8, slots + slot : slots + slot + 1], (8, 128))
            for o in range(0, rows, 8)
        ]
        for tile in range(0, degrees, 128):
            first = jnp.zeros((8, 128), f32)
            second = jnp.zeros((8, 128), f32)
            for at, o in enumerate(range(0, rows, 8)):
                block = legendre_ref[slot, o : o + 8, tile : tile + 128]
                first = first + block * even[at]
                second = second + block * odd[at]
            spectral_ref[slot : slot + 1, tile : tile + 128] = jnp.sum(
                first, axis=0, keepdims=True
            )
            spectral_ref[slots + slot : slots + slot + 1, tile : tile + 128] = jnp.sum(
                second, axis=0, keepdims=True
            )
    if ahead:
        even_ref[:, :ahead] = spectral_ref[...]
        odd_ref[:, :ahead] = spectral_ref[...]

def synthesis_kernel(parts_refs, love_ref, legendre_ref, out_ref, spectral_ref):
    slots, rows, degrees = legendre_ref.shape
    total = parts_refs[0][...]
    for ref in parts_refs[1:]:
        total = total + ref[:, :degrees]
    spectral_ref[...] = total * love_ref[...]
    lanes = lax.broadcasted_iota(jnp.int32, (8, 128), 1)
    octets = range(0, rows, 8)
    sums = [jnp.zeros((8, 128), f32) for _ in octets]
    for slot in range(slots):
        first = [jnp.zeros((8, 128), f32) for _ in octets]
        second = [jnp.zeros((8, 128), f32) for _ in octets]
        for tile in range(0, degrees, 128):
            even = jnp.broadcast_to(spectral_ref[slot : slot + 1, tile : tile + 128], (8, 128))
            odd = jnp.broadcast_to(
                spectral_ref[slots + slot : slots + slot + 1, tile : tile + 128], (8, 128)
            )
            for at, o in enumerate(octets):
                block = legendre_ref[slot, o : o + 8, tile : tile + 128]
                first[at] = first[at] + block * even
                second[at] = second[at] + block * odd
        for at in range(len(octets)):
            sums[at] = jnp.where(lanes == slot, jnp.sum(first[at], axis=1, keepdims=True), sums[at])
            sums[at] = jnp.where(
                lanes == slots + slot, jnp.sum(second[at], axis=1, keepdims=True), sums[at]
            )
    column = jnp.concatenate(sums + [jnp.zeros((128 - rows, 128), f32)], axis=0)
    lines = column.T[: 2 * slots]
    lines = lines[:slots] + pltpu.roll(lines[slots:], 64, 1)
    out_ref[...] = jnp.broadcast_to(lines[None], out_ref.shape)


def side_tiles(me, group, chips, core_ref, west_ref, east_ref):
    first = lax.rem(me, 2) == 0
    other = core_ref[chips * group :]
    left = jnp.where(first, west_ref[group:], other)
    right = jnp.where(first, other, east_ref[group:])
    return left, right


def with_sides(tail, left, right, own, at):
    lanes = lax.broadcasted_iota(jnp.int32, tail.shape, 1)
    after = pltpu.roll(right, (own - 2 * MARGIN * at) % 128, 1)
    before = pltpu.roll(left, (-MARGIN - 2 * MARGIN * at - MARGIN) % 128, 1)
    repeat = tail.shape[1] // 128
    after = jnp.concatenate([after] * repeat, axis=1)
    before = jnp.concatenate([before] * repeat, axis=1)
    tail = jnp.where((lanes >= own) & (lanes < own + MARGIN), after, tail)
    return jnp.where(lanes >= tail.shape[1] - MARGIN, before, tail)


def interleaved(ref, step):
    return [ref[pl.ds(at, 8, stride=step)] for at in range(step)]


def windows_kernel(
    period,
    slots,
    chips,
    bands,
    waves_hbm,
    height_hbm,
    east_hbm,
    north_hbm,
    land_hbm,
    core_ref,
    west_ref,
    east_ref,
    even_rows,
    odd_rows,
    even_ref,
    odd_ref,
    surface_win,
    east_win,
    north_win,
    wet_win,
    moved_win,
    harm_ref,
    waves_ref,
    fields,
    land,
    natural,
    semaphores,
):
    rows, cols = height_hbm.shape
    width = harm_ref.shape[1]
    taller = rows + 2 * MARGIN
    step = taller // 8
    last = (cols // 128) * 128
    copies = [
        pltpu.make_async_copy(source, target, semaphores.at[at])
        for at, (source, target) in enumerate(
            (
                (height_hbm, fields.at[0]),
                (east_hbm, fields.at[1]),
                (north_hbm, fields.at[2]),
                (land_hbm, land),
                (waves_hbm, waves_ref),
            )
        )
    ]
    for copy in copies:
        copy.start()
    copies[4].wait()
    harmonic_rows(period, cols, slots, lax.axis_index("lon"), False, waves_ref, harm_ref)
    left, right = side_tiles(
        lax.axis_index("lon"), 2 * slots, chips, core_ref, west_ref, east_ref
    )
    left = jnp.concatenate([left, pltpu.roll(left, 64, 1)], axis=0)
    right = jnp.concatenate([right, pltpu.roll(right, 64, 1)], axis=0)
    band = lax.axis_index("lat")
    is_even = lax.rem(band, 2) == 0
    even, odd = even_ref[:, -128:], odd_ref[:, -128:]
    corners = (jnp.where(is_even, odd, even), jnp.where(is_even, even, odd))
    for copy in copies[:4]:
        copy.wait()
    middle = pl.ds(MARGIN, rows)
    for at, target in ((3, wet_win), (0, surface_win), (1, east_win), (2, north_win)):
        field = fields.at[at] if at < 3 else land
        even, odd = even_rows[at], odd_rows[at]
        halos = (jnp.where(is_even, odd, even), jnp.where(is_even, even, odd))
        for tile in range(0, last, 128):
            natural[tile // 128, middle] = field[:, tile : tile + 128].astype(f32)
        tail = jnp.concatenate(
            [field[:, last:].astype(f32), jnp.zeros((rows, width - cols), f32)], axis=1
        )
        tail = with_sides(tail, left, right, cols - last, at)
        for tile in range(last, width, 128):
            natural[tile // 128, middle] = tail[:, tile - last : tile - last + 128]
        for halo, corner, first, inside in zip(
            halos, corners, (0, MARGIN + rows), (band > 0, band < bands - 1)
        ):
            halo = jnp.where(inside, halo, 0.0)
            tail = with_sides(halo[:, last:], corner, corner, cols - last, at)
            tail = jnp.where(inside, tail, 0.0)
            for tile in range(0, width, 128):
                block = tail[:, tile - last :][:, :128] if tile >= last else halo[:, tile:][:, :128]
                natural[tile // 128, pl.ds(first, MARGIN)] = block
        for tile in range(0, width, 128):
            for v, block in enumerate(interleaved(natural.at[tile // 128], step)):
                place = (slice(8 * v, 8 * v + 8), slice(tile, tile + 128))
                if at == 3:
                    block = STEP * block
                elif at > 0:
                    block = jnp.where(wet_win[place] > 0.0, block, 0.0)
                target[place] = block
        if at in (1, 3):
            shifted = east_win if at == 1 else moved_win
            for v in range(step):
                shifted[8 * v : 8 * v + 8] = pltpu.roll(target[8 * v : 8 * v + 8], 1, 1)


def substep_kernel(
    sectors,
    bands,
    synth_ref,
    harm_ref,
    surface_win,
    east_win,
    north_win,
    wet,
    moved,
    loading_hbm,
    surface_hbm,
    east_hbm,
    north_hbm,
    column,
    load,
    pressure,
    east,
    north,
    natural,
    loading_out,
    surface_out,
    east_out,
    north_out,
    semaphores,
):
    rows, cols = loading_hbm.shape
    taller, width = wet.shape
    step = taller // 8
    waves = harm_ref.shape[0] // 2
    me, band = lax.axis_index("lon"), lax.axis_index("lat")
    below, above = jnp.maximum(band - 1, 0), jnp.minimum(band + 1, bands - 1)

    def gathered(place):
        lines = [
            synth_ref[place * sectors + owner(me, sectors, core, shift)]
            for core, shift in row_groups(sectors)
        ]
        lines = jnp.concatenate(lines, axis=0)
        return lines.T

    scale = 1.0 / math.sqrt(waves // 2)
    own = gathered(band) * scale
    low = jnp.where(band > 0, gathered(below)[rows - MARGIN :], 0.0) * scale
    high = jnp.where(band < bands - 1, gathered(above), 0.0) * scale
    pieces = []
    for at in range(2):
        first = 64 * at
        column[at, :MARGIN, : waves // 2] = low[first : first + MARGIN]
        column[at, MARGIN : MARGIN + rows, : waves // 2] = own[first : first + rows]
        column[at, MARGIN + rows :, : waves // 2] = high[first : first + MARGIN]
        pieces.append(
            jnp.concatenate(interleaved(column.at[at], step), axis=0)[:, : waves // 2]
        )
    hi, lo = split2(jnp.concatenate(pieces, axis=1))
    left = jnp.concatenate(
        [jnp.concatenate([hi, hi], axis=1), jnp.concatenate([lo, lo], axis=1)], axis=0
    )
    both = lax.dot_general(
        left, harm_ref[...], (((1,), (0,)), ((), ())), preferred_element_type=f32
    )
    both = both[:taller] + both[taller:]
    load[...] = both
    pressure[...] = surface_win[...] - both
    copies = [
        pltpu.make_async_copy(source, target, semaphores.at[at])
        for at, (source, target) in enumerate(
            (
                (loading_out, loading_hbm),
                (surface_out, surface_hbm),
                (east_out, east_hbm),
                (north_out, north_hbm),
            )
        )
    ]

    def give(at, target, blocks):
        for v, block in enumerate(blocks):
            for tile in range(0, width, 128):
                natural[at, tile // 128, pl.ds(v, 8, stride=step)] = block[:, tile : tile + 128]
        for tile in range(0, cols, 128):
            stop = min(cols, tile + 128)
            target[:, tile:stop] = natural[at, tile // 128, pl.ds(MARGIN, rows), : stop - tile]
        copies[at].start()

    def block(ref, v):
        return ref[8 * v : 8 * v + 8]

    def across(ref, v):
        after = pltpu.roll(block(ref, 0), 7, 0) if v == step - 1 else block(ref, v + 1)
        before = pltpu.roll(block(ref, step - 1), 1, 0) if v == 0 else block(ref, v - 1)
        return after - before

    give(0, loading_out, [block(load, v) for v in range(step)])
    for substep in range(SUBSTEPS):
        first, final = substep == 0, substep == SUBSTEPS - 1
        for v in range(step):
            here = block(pressure, v)
            flow = block(east_win if first else east, v)
            flow = flow - block(moved, v) * (here - pltpu.roll(here, 2, 1))
            east[8 * v : 8 * v + 8] = flow
            flow = block(north_win if first else north, v)
            north[8 * v : 8 * v + 8] = flow - block(wet, v) * across(pressure, v)
        if final:
            give(2, east_out, [pltpu.roll(block(east, v), width - 1, 1) for v in range(step)])
            give(3, north_out, [block(north, v) for v in range(step)])
        levels = []
        for v in range(step):
            flow = block(east, v)
            change = pltpu.roll(flow, width - 2, 1) - flow + across(north, v)
            level = block(pressure, v) - block(wet, v) * change
            if final:
                levels.append(level + block(load, v))
            else:
                pressure[8 * v : 8 * v + 8] = level
        if final:
            give(1, surface_out, levels)
    for copy in copies:
        copy.wait()


def shards(height, east_flow, north_flow, legendre, love_numbers, wavenumbers, land_sea):
    rows, cols = height.shape
    slots, _, degrees = legendre.shape
    sectors, bands = lax.axis_size("lon"), lax.axis_size("lat")
    chips = sectors // 2
    waves = wavenumbers.shape[0]
    period = cols * sectors
    width = -(-(cols + 2 * MARGIN) // 128) * 128
    taller = rows + 2 * MARGIN
    group, half = 2 * slots, rows // 2
    back = (cols - MARGIN) // 128 * 128
    DMA = pltpu.SemaphoreType.DMA
    fields = (height, east_flow, north_flow, land_sea)

    keep, send, tile = pl.pallas_call(
        functools.partial(transform_kernel, period, slots),
        out_shape=[
            struct((chips, group, 128)),
            struct((chips * group + half, 128)),
            struct((half, 128)),
        ],
        in_specs=[HBM] * 5,
        out_specs=[VMEM] * 3,
        scratch_shapes=[
            pltpu.SMEM((waves,), jnp.int32),
            pltpu.VMEM((rows, cols), f32),
            pltpu.VMEM((2, rows, 128), f32),
            pltpu.VMEM((2, rows, cols - back), f32),
            pltpu.VMEM((rows, 128), jnp.int32),
            pltpu.VMEM((rows, cols - back), jnp.int32),
            pltpu.VMEM((4 * waves, width), bf16),
            pltpu.VMEM((2 * rows, width), bf16),
            DMA((8,)),
        ],
        name="transform",
        compiler_params=LIMIT,
    )(*in_hbm(wavenumbers, *fields))
    core = lax.ppermute(send, "lon", [(i, i ^ 1) for i in range(sectors)])
    neighbours = (1, chips - 1)
    own, *outgoing = pl.pallas_call(
        mix_kernel,
        out_shape=[struct((group, 128))]
        + [
            struct((group + (half if shift in neighbours else 0), 128))
            for shift in range(1, chips)
        ],
        in_specs=[VMEM] * 3,
        out_specs=[VMEM] * chips,
        name="mix",
        compiler_params=LIMIT,
    )(keep, tile, core)
    arrived = []
    for shift, block in enumerate(outgoing, 1):
        across = [(i, 2 * ((i // 2 + shift) % chips) + 1 - i % 2) for i in range(sectors)]
        arrived.append(lax.ppermute(block, "lon", across))
    sides = (core, arrived[0], arrived[-1])

    even, odd, legendre = pl.pallas_call(
        stage_kernel,
        out_shape=[struct((4, MARGIN, width))] * 2 + [struct(legendre.shape)],
        in_specs=[VMEM] + [HBM] * 5,
        out_specs=[VMEM] * 3,
        scratch_shapes=[
            pltpu.VMEM((2, 3, MARGIN, cols), f32),
            pltpu.VMEM((2, MARGIN, cols), jnp.int32),
            DMA((9,)),
        ],
        name="stage",
        compiler_params=LIMIT,
    )(own, *in_hbm(*fields, legendre))
    links = [[(i, (i + 1) % bands) for i in range(first, bands, 2)] for first in (0, 1)]
    links = [pairs + [(j, i) for i, j in pairs] for pairs in links]
    even, odd = [lax.ppermute(block, "lat", pairs) for block, pairs in zip((even, odd), links)]

    def analysis(*refs):
        analysis_kernel(refs[:chips], *refs[chips:])

    together = bands == 4
    message = 128 + (degrees if together else 0)
    spectral, *corners = pl.pallas_call(
        analysis,
        out_shape=[struct((group, degrees))] + [struct((MARGIN, message))] * 2,
        in_specs=[VMEM] * (chips + 2),
        out_specs=[VMEM] * 3,
        name="analysis",
        compiler_params=LIMIT,
    )(own, *arrived, core, legendre)
    if together:
        *corners, across = [
            lax.ppermute(block, "lat", [(i, i ^ step) for i in range(bands)])
            for block, step in ((corners[0], 1), (corners[1], 3), (spectral, 2))
        ]
        pieces = [spectral, corners[1], corners[0], across]
    else:
        corners = [
            lax.ppermute(block, "lat", pairs) for block, pairs in zip(corners, links)
        ]
        pieces = [lax.psum(spectral, "lat")]

    def synthesis(*refs):
        synthesis_kernel(refs[: len(pieces)], *refs[len(pieces) :])

    synth = pl.pallas_call(
        synthesis,
        out_shape=struct((bands * sectors, slots, 128)),
        in_specs=[VMEM] * (len(pieces) + 2),
        out_specs=VMEM,
        scratch_shapes=[pltpu.VMEM((group, degrees), f32)],
        name="synthesis",
        cost_estimate=pl.CostEstimate(flops=100000000000, bytes_accessed=400000000, transcendentals=0),
        compiler_params=LIMIT,
    )(*pieces, love_numbers.reshape(1, degrees), legendre)
    everyone = lax.all_to_all(synth, ("lat", "lon"), 0, 0, tiled=True)

    *windows, harmonics = pl.pallas_call(
        functools.partial(windows_kernel, period, slots, chips, bands),
        out_shape=[struct((taller, width))] * 5 + [struct((4 * waves, width), bf16)],
        in_specs=[HBM] * 5 + [VMEM] * 7,
        out_specs=[VMEM] * 6,
        scratch_shapes=[
            pltpu.SMEM((waves,), jnp.int32),
            pltpu.VMEM((3, rows, cols), f32),
            pltpu.VMEM((rows, cols), jnp.int32),
            pltpu.VMEM((width // 128, taller, 128), f32),
            DMA((5,)),
        ],
        name="windows",
        cost_estimate=pl.CostEstimate(flops=10**11, bytes_accessed=4 * 10**8, transcendentals=0),
        compiler_params=LIMIT,
    )(*in_hbm(wavenumbers, *fields), *sides, even, odd, *corners)

    return pl.pallas_call(
        functools.partial(substep_kernel, sectors, bands),
        out_shape=[struct((rows, cols))] * 4,
        in_specs=[VMEM] * 7,
        out_specs=[HBM] * 4,
        scratch_shapes=[
            pltpu.VMEM((2, taller, 128), f32),
            pltpu.VMEM((taller, width), f32),
            pltpu.VMEM((taller, width), f32),
            pltpu.VMEM((taller, width), f32),
            pltpu.VMEM((taller, width), f32),
            pltpu.VMEM((4, width // 128, taller, 128), f32),
        ]
        + [pltpu.VMEM((rows, cols), f32)] * 4
        + [DMA((4,))],
        name="substeps",
        compiler_params=LIMIT,
    )(everyone, harmonics, *windows)


def solution(mesh):
    return jax.shard_map(
        shards,
        mesh=mesh,
        in_specs=(
            P("lat", "lon"),
            P("lat", "lon"),
            P("lat", "lon"),
            P("lon", "lat", None),
            P(),
            P(),
            P("lat", "lon"),
        ),
        out_specs=(P("lat", "lon"), P("lat", "lon"), P("lat", "lon"), P("lat", "lon")),
        check_vma=False,
    )
```

```python
import functools
import math

import jax
import jax.numpy as jnp
from jax import lax
from jax.experimental import pallas as pl
from jax.experimental.pallas import tpu as pltpu
from jax.sharding import PartitionSpec as P

SUBSTEPS = 4
MARGIN = 2 * SUBSTEPS
STEP = 0.3

f32 = jnp.float32
bf16 = jnp.bfloat16
VMEM = pl.BlockSpec(memory_space=pltpu.VMEM)
HBM = pl.BlockSpec(memory_space=pltpu.HBM)
SMEM = pl.BlockSpec(memory_space=pltpu.SMEM)
LIMIT = pltpu.CompilerParams(vmem_limit_bytes=24 * 2**20)


def struct(shape, dtype=f32):
    return jax.ShapeDtypeStruct(shape, dtype)


def in_hbm(*arrays):
    return [pltpu.with_memory_space_constraint(x, pltpu.HBM) for x in arrays]


def split2(x):
    hi = x.astype(bf16)
    lo = (x - hi.astype(f32)).astype(bf16)
    return hi, lo


def chip_at(chip, shift, chips):
    return chip ^ shift if chips == 4 else (chip + shift) % chips


def owner(me, sectors, core, shift):
    crossed = core if shift == 0 else 1 - core
    chip = chip_at(me // 2, shift, sectors // 2)
    return 2 * chip + lax.bitwise_xor(lax.rem(me, 2), crossed)


def row_groups(sectors):
    return [(core, shift) for core in range(2) for shift in range(sectors // 2)]


def harmonic_rows(period, cols, slots, me, paired, waves_ref, harm_ref):
    waves, width = harm_ref.shape[0] // 2, harm_ref.shape[1]
    sectors = waves // (2 * slots)
    order = []
    for core, shift in row_groups(sectors):
        first = owner(me, sectors, core, shift) * slots
        group = [waves_ref[first + slot] for slot in range(slots)]
        order += group + group if paired else group
    if not paired:
        order = order + order
    row = lax.broadcasted_iota(jnp.int32, (8, 1), 0)
    blocks = []
    for first in range(0, waves, 8):
        block = jnp.zeros((8, 1), jnp.int32)
        for at, value in enumerate(order[first : first + 8]):
            block = jnp.where(row == at, value, block)
        blocks.append(block)
    wave = jnp.concatenate(blocks, axis=0)
    start = wave * (me * cols)
    turns = jnp.floor(start.astype(f32) * (1.0 / period)).astype(jnp.int32)
    start = (start - turns * period).astype(f32)
    wave = wave.astype(f32)
    row = lax.broadcasted_iota(jnp.int32, (waves, 1), 0)
    if paired:
        row = lax.rem(row, 2 * slots)
    sine = (row >= (slots if paired else waves // 2)).astype(f32)
    offset = 4.0 * start - period * sine
    for tile in range(0, width, 128):
        lane = lax.broadcasted_iota(jnp.int32, (1, 128), 1) + tile
        lane = jnp.where(lane < cols + MARGIN, lane, lane - width).astype(f32)
        product = wave * lane
        product = product - period * jnp.floor(product * (1.0 / period))
        quarter = 4.0 * product + offset
        turn = jnp.floor(quarter * (1.0 / period) + 0.5)
        angle = (quarter - period * turn) * (0.5 * math.pi / period)
        square = angle * angle
        cosine = 1.0 + square * (
            -1.0 / 2 + square * (1.0 / 24 + square * (-1.0 / 720 + square * (1.0 / 40320)))
        )
        sine_of = angle * (
            1.0
            + square
            * (-1.0 / 6 + square * (1.0 / 120 + square * (-1.0 / 5040 + square * (1.0 / 362880))))
        )
        phase = turn - 4.0 * jnp.floor(turn * 0.25)
        odd = (phase == 1.0) | (phase == 3.0)
        value = jnp.where(odd, sine_of, cosine)
        value = jnp.where((phase == 1.0) | (phase == 2.0), -value, value)
        hi, lo = split2(value)
        harm_ref[:waves, tile : tile + 128] = hi
        harm_ref[waves:, tile : tile + 128] = lo


def transform_kernel(
    period,
    slots,
    waves_hbm,
    height_hbm,
    east_hbm,
    north_hbm,
    land_hbm,
    keep_ref,
    send_ref,
    tile_ref,
    waves_ref,
    height_ref,
    flow_front,
    flow_back,
    land_front,
    land_back,
    harm_ref,
    field_ref,
    semaphores,
):
    rows, cols = height_ref.shape
    waves, width = harm_ref.shape[0] // 2, harm_ref.shape[1]
    back = cols - land_back.shape[1]
    fronts, backs = pl.ds(0, 128), pl.ds(back, cols - back)
    copies = [
        pltpu.make_async_copy(source, target, semaphores.at[at])
        for at, (source, target) in enumerate(
            (
                (waves_hbm, waves_ref),
                (height_hbm, height_ref),
                (east_hbm.at[:, fronts], flow_front.at[0]),
                (east_hbm.at[:, backs], flow_back.at[0]),
                (north_hbm.at[:, fronts], flow_front.at[1]),
                (north_hbm.at[:, backs], flow_back.at[1]),
                (land_hbm.at[:, fronts], land_front),
                (land_hbm.at[:, backs], land_back),
            )
        )
    ]
    for copy in copies:
        copy.start()
    copies[0].wait()
    harmonic_rows(period, cols, slots, lax.axis_index("lon"), True, waves_ref, harm_ref)
    copies[1].wait()
    for tile in range(0, width, 128):
        stop = min(cols, tile + 128)
        if stop <= tile:
            block = jnp.zeros((rows, 128), f32)
        elif stop == tile + 128:
            block = height_ref[:, tile : tile + 128]
        else:
            block = jnp.concatenate(
                [height_ref[:, tile:stop], jnp.zeros((rows, tile + 128 - stop), f32)], axis=1
            )
        hi, lo = split2(block)
        field_ref[:rows, tile : tile + 128] = hi
        field_ref[rows:, tile : tile + 128] = lo
    rows_by_rows = (((1,), (1,)), ((), ()))
    high = lax.dot_general(
        harm_ref[...], field_ref[:rows], rows_by_rows, preferred_element_type=f32
    )
    low = lax.dot_general(
        harm_ref[:waves], field_ref[rows:], rows_by_rows, preferred_element_type=f32
    )
    total = (high[:waves] + high[waves:] + low) * (1.0 / math.sqrt(period))
    total = jnp.concatenate([total, jnp.zeros((waves, 128 - rows), f32)], axis=1)
    keep_ref[...] = total[: waves // 2].reshape(keep_ref.shape)
    send_ref[: waves // 2] = total[waves // 2 :]
    for copy in copies[2:]:
        copy.wait()
    pieces = []
    for front, end in (
        (height_ref[:, :MARGIN], height_ref[:, cols - MARGIN :]),
        (flow_front[0, :, :MARGIN], flow_back[0, :, cols - MARGIN - back :]),
        (flow_front[1, :, :MARGIN], flow_back[1, :, cols - MARGIN - back :]),
        (land_front[:, :MARGIN].astype(f32), land_back[:, cols - MARGIN - back :].astype(f32)),
    ):
        pieces += [front, end]
    half = rows // 2
    tile = jnp.concatenate(
        [piece[:half] for piece in pieces] + [piece[half:] for piece in pieces], axis=1
    )
    send_ref[waves // 2 :] = tile
    tile_ref[...] = tile


def stage_kernel(
    after_ref,
    height_hbm,
    east_hbm,
    north_hbm,
    land_hbm,
    legendre_hbm,
    even_ref,
    odd_ref,
    legendre_ref,
    flows,
    lands,
    semaphores,
):
    rows, cols = height_hbm.shape
    width = even_ref.shape[2]
    copies = []
    for side, first in enumerate((rows - MARGIN, 0)):
        band = pl.ds(first, MARGIN)
        copies.append((height_hbm.at[band], flows.at[side, 0]))
        copies.append((east_hbm.at[band], flows.at[side, 1]))
        copies.append((north_hbm.at[band], flows.at[side, 2]))
        copies.append((land_hbm.at[band], lands.at[side]))
    copies.append((legendre_hbm, legendre_ref))
    copies = [
        pltpu.make_async_copy(source, target, semaphores.at[at])
        for at, (source, target) in enumerate(copies)
    ]
    for copy in copies:
        copy.start()
    for copy in copies[:-1]:
        copy.wait()
    is_even = lax.rem(lax.axis_index("lat"), 2) == 0
    for at in range(4):
        up, down = [lands[side].astype(f32) if at == 3 else flows[side, at] for side in range(2)]
        even_ref[at, :, :cols] = jnp.where(is_even, up, down)
        odd_ref[at, :, :cols] = jnp.where(is_even, down, up)
        if cols < width:
            blank = jnp.zeros((MARGIN, width - cols), f32)
            even_ref[at, :, cols:] = blank
            odd_ref[at, :, cols:] = blank
    copies[-1].wait()


def mix_kernel(keep_ref, tile_ref, recv_ref, own_ref, *send_refs):
    chips, group, _ = keep_ref.shape
    own_ref[...] = keep_ref[0] + recv_ref[:group]
    for shift, ref in enumerate(send_refs, 1):
        ref[:group] = keep_ref[shift] + recv_ref[shift * group : (shift + 1) * group]
        if ref.shape[0] > group:
            ref[group:] = tile_ref[...]


def analysis_kernel(part_refs, core_ref, legendre_ref, spectral_ref, even_ref, odd_ref):
    slots, rows, degrees = legendre_ref.shape
    chips, half = len(part_refs), rows // 2
    left, right = side_tiles(lax.axis_index("lon"), 2 * slots, chips, core_ref, part_refs[1], part_refs[-1])
    lanes = lax.broadcasted_iota(jnp.int32, left.shape, 1)
    both = jnp.where(lax.rem(lanes, 2 * MARGIN) < MARGIN, right, left)
    up, down = pltpu.roll(both[half - MARGIN :], 64, 1), both[:MARGIN]
    is_even = lax.rem(lax.axis_index("lat"), 2) == 0
    ahead = even_ref.shape[1] - 128
    even_ref[:, ahead:] = jnp.where(is_even, up, down)
    odd_ref[:, ahead:] = jnp.where(is_even, down, up)
    fourier = part_refs[0][...]
    for ref in part_refs[1:]:
        fourier = fourier + ref[: 2 * slots]
    columns = fourier.T
    for slot in range(slots):
        even = [
            jnp.broadcast_to(columns[o : o + 8, slot : slot + 1], (8, 128))
            for o in range(0, rows, 8)
        ]
        odd = [
            jnp.broadcast_to(columns[o : o + 8, slots + slot : slots + slot + 1], (8, 128))
            for o in range(0, rows, 8)
        ]
        for tile in range(0, degrees, 128):
            first = jnp.zeros((8, 128), f32)
            second = jnp.zeros((8, 128), f32)
            for at, o in enumerate(range(0, rows, 8)):
                block = legendre_ref[slot, o : o + 8, tile : tile + 128]
                first = first + block * even[at]
                second = second + block * odd[at]
            spectral_ref[slot : slot + 1, tile : tile + 128] = jnp.sum(
                first, axis=0, keepdims=True
            )
            spectral_ref[slots + slot : slots + slot + 1, tile : tile + 128] = jnp.sum(
                second, axis=0, keepdims=True
            )
    if ahead:
        even_ref[:, :ahead] = spectral_ref[...]
        odd_ref[:, :ahead] = spectral_ref[...]

def synthesis_kernel(parts_refs, love_ref, legendre_ref, out_ref, spectral_ref):
    slots, rows, degrees = legendre_ref.shape
    total = parts_refs[0][...]
    for ref in parts_refs[1:]:
        total = total + ref[:, :degrees]
    spectral_ref[...] = total * love_ref[...]
    lanes = lax.broadcasted_iota(jnp.int32, (8, 128), 1)
    octets = range(0, rows, 8)
    sums = [jnp.zeros((8, 128), f32) for _ in octets]
    for slot in range(slots):
        first = [jnp.zeros((8, 128), f32) for _ in octets]
        second = [jnp.zeros((8, 128), f32) for _ in octets]
        for tile in range(0, degrees, 128):
            even = jnp.broadcast_to(spectral_ref[slot : slot + 1, tile : tile + 128], (8, 128))
            odd = jnp.broadcast_to(
                spectral_ref[slots + slot : slots + slot + 1, tile : tile + 128], (8, 128)
            )
            for at, o in enumerate(octets):
                block = legendre_ref[slot, o : o + 8, tile : tile + 128]
                first[at] = first[at] + block * even
                second[at] = second[at] + block * odd
        for at in range(len(octets)):
            sums[at] = jnp.where(lanes == slot, jnp.sum(first[at], axis=1, keepdims=True), sums[at])
            sums[at] = jnp.where(
                lanes == slots + slot, jnp.sum(second[at], axis=1, keepdims=True), sums[at]
            )
    column = jnp.concatenate(sums + [jnp.zeros((128 - rows, 128), f32)], axis=0)
    lines = column.T[: 2 * slots]
    lines = lines[:slots] + pltpu.roll(lines[slots:], 64, 1)
    out_ref[...] = jnp.broadcast_to(lines[None], out_ref.shape)


def side_tiles(me, group, chips, core_ref, west_ref, east_ref):
    first = lax.rem(me, 2) == 0
    other = core_ref[chips * group :]
    west, east = west_ref[group:], east_ref[group:]
    if chips == 4:
        even = lax.rem(me // 2, 2) == 0
        west, east = jnp.where(even, east, west), jnp.where(even, west, east)
    left = jnp.where(first, west, other)
    right = jnp.where(first, other, east)
    return left, right


def with_sides(tail, left, right, own, at):
    lanes = lax.broadcasted_iota(jnp.int32, tail.shape, 1)
    after = pltpu.roll(right, (own - 2 * MARGIN * at) % 128, 1)
    before = pltpu.roll(left, (-MARGIN - 2 * MARGIN * at - MARGIN) % 128, 1)
    repeat = tail.shape[1] // 128
    after = jnp.concatenate([after] * repeat, axis=1)
    before = jnp.concatenate([before] * repeat, axis=1)
    tail = jnp.where((lanes >= own) & (lanes < own + MARGIN), after, tail)
    return jnp.where(lanes >= tail.shape[1] - MARGIN, before, tail)


def interleaved(ref, step):
    return [ref[pl.ds(at, 8, stride=step)] for at in range(step)]


def windows_kernel(
    period,
    slots,
    chips,
    bands,
    waves_hbm,
    height_hbm,
    east_hbm,
    north_hbm,
    land_hbm,
    core_ref,
    west_ref,
    east_ref,
    even_rows,
    odd_rows,
    even_ref,
    odd_ref,
    surface_win,
    east_win,
    north_win,
    wet_win,
    moved_win,
    harm_ref,
    waves_ref,
    fields,
    land,
    natural,
    semaphores,
):
    rows, cols = height_hbm.shape
    width = harm_ref.shape[1]
    taller = rows + 2 * MARGIN
    step = taller // 8
    last = (cols // 128) * 128
    copies = [
        pltpu.make_async_copy(source, target, semaphores.at[at])
        for at, (source, target) in enumerate(
            (
                (height_hbm, fields.at[0]),
                (east_hbm, fields.at[1]),
                (north_hbm, fields.at[2]),
                (land_hbm, land),
                (waves_hbm, waves_ref),
            )
        )
    ]
    for copy in copies:
        copy.start()
    copies[4].wait()
    harmonic_rows(period, cols, slots, lax.axis_index("lon"), False, waves_ref, harm_ref)
    left, right = side_tiles(
        lax.axis_index("lon"), 2 * slots, chips, core_ref, west_ref, east_ref
    )
    left = jnp.concatenate([left, pltpu.roll(left, 64, 1)], axis=0)
    right = jnp.concatenate([right, pltpu.roll(right, 64, 1)], axis=0)
    band = lax.axis_index("lat")
    is_even = lax.rem(band, 2) == 0
    even, odd = even_ref[:, -128:], odd_ref[:, -128:]
    corners = (jnp.where(is_even, odd, even), jnp.where(is_even, even, odd))
    for copy in copies[:4]:
        copy.wait()
    middle = pl.ds(MARGIN, rows)
    for at, target in ((3, wet_win), (0, surface_win), (1, east_win), (2, north_win)):
        field = fields.at[at] if at < 3 else land
        even, odd = even_rows[at], odd_rows[at]
        halos = (jnp.where(is_even, odd, even), jnp.where(is_even, even, odd))
        for tile in range(0, last, 128):
            natural[tile // 128, middle] = field[:, tile : tile + 128].astype(f32)
        tail = jnp.concatenate(
            [field[:, last:].astype(f32), jnp.zeros((rows, width - cols), f32)], axis=1
        )
        tail = with_sides(tail, left, right, cols - last, at)
        for tile in range(last, width, 128):
            natural[tile // 128, middle] = tail[:, tile - last : tile - last + 128]
        for halo, corner, first, inside in zip(
            halos, corners, (0, MARGIN + rows), (band > 0, band < bands - 1)
        ):
            halo = jnp.where(inside, halo, 0.0)
            tail = with_sides(halo[:, last:], corner, corner, cols - last, at)
            tail = jnp.where(inside, tail, 0.0)
            for tile in range(0, width, 128):
                block = tail[:, tile - last :][:, :128] if tile >= last else halo[:, tile:][:, :128]
                natural[tile // 128, pl.ds(first, MARGIN)] = block
        for tile in range(0, width, 128):
            for v, block in enumerate(interleaved(natural.at[tile // 128], step)):
                place = (slice(8 * v, 8 * v + 8), slice(tile, tile + 128))
                if at == 3:
                    block = STEP * block
                elif at > 0:
                    block = jnp.where(wet_win[place] > 0.0, block, 0.0)
                target[place] = block
        if at in (1, 3):
            shifted = east_win if at == 1 else moved_win
            for v in range(step):
                shifted[8 * v : 8 * v + 8] = pltpu.roll(target[8 * v : 8 * v + 8], 1, 1)


def substep_kernel(
    sectors,
    bands,
    synth_ref,
    harm_ref,
    surface_win,
    east_win,
    north_win,
    wet,
    moved,
    loading_hbm,
    surface_hbm,
    east_hbm,
    north_hbm,
    column,
    load,
    pressure,
    east,
    north,
    natural,
    loading_out,
    surface_out,
    east_out,
    north_out,
    semaphores,
):
    rows, cols = loading_hbm.shape
    taller, width = wet.shape
    step = taller // 8
    waves = harm_ref.shape[0] // 2
    me, band = lax.axis_index("lon"), lax.axis_index("lat")
    below, above = jnp.maximum(band - 1, 0), jnp.minimum(band + 1, bands - 1)

    def gathered(place):
        lines = [
            synth_ref[place * sectors + owner(me, sectors, core, shift)]
            for core, shift in row_groups(sectors)
        ]
        lines = jnp.concatenate(lines, axis=0)
        return lines.T

    scale = 1.0 / math.sqrt(waves // 2)
    own = gathered(band) * scale
    low = jnp.where(band > 0, gathered(below)[rows - MARGIN :], 0.0) * scale
    high = jnp.where(band < bands - 1, gathered(above), 0.0) * scale
    pieces = []
    for at in range(2):
        first = 64 * at
        column[at, :MARGIN, : waves // 2] = low[first : first + MARGIN]
        column[at, MARGIN : MARGIN + rows, : waves // 2] = own[first : first + rows]
        column[at, MARGIN + rows :, : waves // 2] = high[first : first + MARGIN]
        pieces.append(
            jnp.concatenate(interleaved(column.at[at], step), axis=0)[:, : waves // 2]
        )
    hi, lo = split2(jnp.concatenate(pieces, axis=1))
    columns = (((1,), (0,)), ((), ()))
    both = lax.dot_general(
        jnp.concatenate([hi, hi], axis=1), harm_ref[...], columns, preferred_element_type=f32
    )
    both = both + lax.dot_general(lo, harm_ref[:waves], columns, preferred_element_type=f32)
    load[...] = both
    pressure[...] = surface_win[...] - both
    copies = [
        pltpu.make_async_copy(source, target, semaphores.at[at])
        for at, (source, target) in enumerate(
            (
                (loading_out, loading_hbm),
                (surface_out, surface_hbm),
                (east_out, east_hbm),
                (north_out, north_hbm),
            )
        )
    ]

    def give(at, target, blocks):
        for v, block in enumerate(blocks):
            for tile in range(0, width, 128):
                natural[at, tile // 128, pl.ds(v, 8, stride=step)] = block[:, tile : tile + 128]
        for tile in range(0, cols, 128):
            stop = min(cols, tile + 128)
            target[:, tile:stop] = natural[at, tile // 128, pl.ds(MARGIN, rows), : stop - tile]
        copies[at].start()

    def block(ref, v):
        return ref[8 * v : 8 * v + 8]

    def across(ref, v):
        after = pltpu.roll(block(ref, 0), 7, 0) if v == step - 1 else block(ref, v + 1)
        before = pltpu.roll(block(ref, step - 1), 1, 0) if v == 0 else block(ref, v - 1)
        return after - before

    give(0, loading_out, [block(load, v) for v in range(step)])
    for substep in range(SUBSTEPS):
        first, final = substep == 0, substep == SUBSTEPS - 1
        for v in range(step):
            here = block(pressure, v)
            flow = block(east_win if first else east, v)
            flow = flow - block(moved, v) * (here - pltpu.roll(here, 2, 1))
            east[8 * v : 8 * v + 8] = flow
            flow = block(north_win if first else north, v)
            north[8 * v : 8 * v + 8] = flow - block(wet, v) * across(pressure, v)
        if final:
            give(2, east_out, [pltpu.roll(block(east, v), width - 1, 1) for v in range(step)])
            give(3, north_out, [block(north, v) for v in range(step)])
        levels = []
        for v in range(step):
            flow = block(east, v)
            change = pltpu.roll(flow, width - 2, 1) - flow + across(north, v)
            level = block(pressure, v) - block(wet, v) * change
            if final:
                levels.append(level + block(load, v))
            else:
                pressure[8 * v : 8 * v + 8] = level
        if final:
            give(1, surface_out, levels)
    for copy in copies:
        copy.wait()


def shards(height, east_flow, north_flow, legendre, love_numbers, wavenumbers, land_sea):
    rows, cols = height.shape
    slots, _, degrees = legendre.shape
    sectors, bands = lax.axis_size("lon"), lax.axis_size("lat")
    chips = sectors // 2
    waves = wavenumbers.shape[0]
    period = cols * sectors
    width = -(-(cols + 2 * MARGIN) // 128) * 128
    taller = rows + 2 * MARGIN
    group, half = 2 * slots, rows // 2
    back = (cols - MARGIN) // 128 * 128
    DMA = pltpu.SemaphoreType.DMA
    fields = (height, east_flow, north_flow, land_sea)

    keep, send, tile = pl.pallas_call(
        functools.partial(transform_kernel, period, slots),
        out_shape=[
            struct((chips, group, 128)),
            struct((chips * group + half, 128)),
            struct((half, 128)),
        ],
        in_specs=[HBM] * 5,
        out_specs=[VMEM] * 3,
        scratch_shapes=[
            pltpu.SMEM((waves,), jnp.int32),
            pltpu.VMEM((rows, cols), f32),
            pltpu.VMEM((2, rows, 128), f32),
            pltpu.VMEM((2, rows, cols - back), f32),
            pltpu.VMEM((rows, 128), jnp.int32),
            pltpu.VMEM((rows, cols - back), jnp.int32),
            pltpu.VMEM((4 * waves, width), bf16),
            pltpu.VMEM((2 * rows, width), bf16),
            DMA((8,)),
        ],
        name="transform",
        compiler_params=LIMIT,
    )(*in_hbm(wavenumbers, *fields))
    core = lax.ppermute(send, "lon", [(i, i ^ 1) for i in range(sectors)])
    neighbours = (1, chips - 1)
    own, *outgoing = pl.pallas_call(
        mix_kernel,
        out_shape=[struct((group, 128))]
        + [
            struct((group + (half if shift in neighbours else 0), 128))
            for shift in range(1, chips)
        ],
        in_specs=[VMEM] * 3,
        out_specs=[VMEM] * chips,
        name="mix",
        compiler_params=LIMIT,
    )(keep, tile, core)
    arrived = []
    for shift, block in enumerate(outgoing, 1):
        across = [
            (i, 2 * chip_at(i // 2, shift, chips) + 1 - i % 2) for i in range(sectors)
        ]
        arrived.append(lax.ppermute(block, "lon", across))
    sides = (core, arrived[0], arrived[-1])

    even, odd, legendre = pl.pallas_call(
        stage_kernel,
        out_shape=[struct((4, MARGIN, width))] * 2 + [struct(legendre.shape)],
        in_specs=[VMEM] + [HBM] * 5,
        out_specs=[VMEM] * 3,
        scratch_shapes=[
            pltpu.VMEM((2, 3, MARGIN, cols), f32),
            pltpu.VMEM((2, MARGIN, cols), jnp.int32),
            DMA((9,)),
        ],
        name="stage",
        compiler_params=LIMIT,
    )(own, *in_hbm(*fields, legendre))
    links = [[(i, (i + 1) % bands) for i in range(first, bands, 2)] for first in (0, 1)]
    links = [pairs + [(j, i) for i, j in pairs] for pairs in links]
    even, odd = [lax.ppermute(block, "lat", pairs) for block, pairs in zip((even, odd), links)]

    def analysis(*refs):
        analysis_kernel(refs[:chips], *refs[chips:])

    together = bands == 4
    message = 128 + (degrees if together else 0)
    spectral, *corners = pl.pallas_call(
        analysis,
        out_shape=[struct((group, degrees))] + [struct((MARGIN, message))] * 2,
        in_specs=[VMEM] * (chips + 2),
        out_specs=[VMEM] * 3,
        name="analysis",
        compiler_params=LIMIT,
    )(own, *arrived, core, legendre)
    if together:
        *corners, across = [
            lax.ppermute(block, "lat", [(i, i ^ step) for i in range(bands)])
            for block, step in ((corners[0], 1), (corners[1], 3), (spectral, 2))
        ]
        pieces = [spectral, corners[1], corners[0], across]
    else:
        corners = [
            lax.ppermute(block, "lat", pairs) for block, pairs in zip(corners, links)
        ]
        pieces = [lax.psum(spectral, "lat")]

    def synthesis(*refs):
        synthesis_kernel(refs[: len(pieces)], *refs[len(pieces) :])

    synth = pl.pallas_call(
        synthesis,
        out_shape=struct((bands * sectors, slots, 128)),
        in_specs=[VMEM] * (len(pieces) + 2),
        out_specs=VMEM,
        scratch_shapes=[pltpu.VMEM((group, degrees), f32)],
        name="synthesis",
        cost_estimate=pl.CostEstimate(flops=100000000000, bytes_accessed=400000000, transcendentals=0),
        compiler_params=LIMIT,
    )(*pieces, love_numbers.reshape(1, degrees), legendre)
    everyone = lax.all_to_all(synth, ("lat", "lon"), 0, 0, tiled=True)

    *windows, harmonics = pl.pallas_call(
        functools.partial(windows_kernel, period, slots, chips, bands),
        out_shape=[struct((taller, width))] * 5 + [struct((4 * waves, width), bf16)],
        in_specs=[HBM] * 5 + [VMEM] * 7,
        out_specs=[VMEM] * 6,
        scratch_shapes=[
            pltpu.SMEM((waves,), jnp.int32),
            pltpu.VMEM((3, rows, cols), f32),
            pltpu.VMEM((rows, cols), jnp.int32),
            pltpu.VMEM((width // 128, taller, 128), f32),
            DMA((5,)),
        ],
        name="windows",
        cost_estimate=pl.CostEstimate(flops=10**11, bytes_accessed=4 * 10**8, transcendentals=0),
        compiler_params=LIMIT,
    )(*in_hbm(wavenumbers, *fields), *sides, even, odd, *corners)

    return pl.pallas_call(
        functools.partial(substep_kernel, sectors, bands),
        out_shape=[struct((rows, cols))] * 4,
        in_specs=[VMEM] * 7,
        out_specs=[HBM] * 4,
        scratch_shapes=[
            pltpu.VMEM((2, taller, 128), f32),
            pltpu.VMEM((taller, width), f32),
            pltpu.VMEM((taller, width), f32),
            pltpu.VMEM((taller, width), f32),
            pltpu.VMEM((taller, width), f32),
            pltpu.VMEM((4, width // 128, taller, 128), f32),
        ]
        + [pltpu.VMEM((rows, cols), f32)] * 4
        + [DMA((4,))],
        name="substeps",
        compiler_params=LIMIT,
    )(everyone, harmonics, *windows)


def solution(mesh):
    return jax.shard_map(
        shards,
        mesh=mesh,
        in_specs=(
            P("lat", "lon"),
            P("lat", "lon"),
            P("lat", "lon"),
            P("lon", "lat", None),
            P(),
            P(),
            P("lat", "lon"),
        ),
        out_specs=(P("lat", "lon"), P("lat", "lon"), P("lat", "lon"), P("lat", "lon")),
        check_vma=False,
    )
```

```python
import functools
import math

import jax
import jax.numpy as jnp
from jax import lax
from jax.experimental import pallas as pl
from jax.experimental.pallas import tpu as pltpu
from jax.sharding import PartitionSpec as P

SUBSTEPS = 4
MARGIN = 2 * SUBSTEPS
STEP = 0.3

f32 = jnp.float32
bf16 = jnp.bfloat16
VMEM = pl.BlockSpec(memory_space=pltpu.VMEM)
HBM = pl.BlockSpec(memory_space=pltpu.HBM)
SMEM = pl.BlockSpec(memory_space=pltpu.SMEM)
LIMIT = pltpu.CompilerParams(vmem_limit_bytes=24 * 2**20)


def struct(shape, dtype=f32):
    return jax.ShapeDtypeStruct(shape, dtype)


def in_hbm(*arrays):
    return [pltpu.with_memory_space_constraint(x, pltpu.HBM) for x in arrays]


def split2(x):
    hi = x.astype(bf16)
    lo = (x - hi.astype(f32)).astype(bf16)
    return hi, lo


def chip_at(chip, shift, chips):
    return chip ^ shift if chips == 4 else (chip + shift) % chips


def owner(me, sectors, core, shift):
    crossed = core if shift == 0 else 1 - core
    chip = chip_at(me // 2, shift, sectors // 2)
    return 2 * chip + lax.bitwise_xor(lax.rem(me, 2), crossed)


def row_groups(sectors):
    return [(core, shift) for core in range(2) for shift in range(sectors // 2)]


def harmonic_rows(period, cols, slots, me, paired, waves_ref, harm_ref):
    waves, width = harm_ref.shape[0] // 2, harm_ref.shape[1]
    sectors = waves // (2 * slots)
    order = []
    for core, shift in row_groups(sectors):
        first = owner(me, sectors, core, shift) * slots
        group = [waves_ref[first + slot] for slot in range(slots)]
        order += group + group if paired else group
    if not paired:
        order = order + order
    row = lax.broadcasted_iota(jnp.int32, (8, 1), 0)
    blocks = []
    for first in range(0, waves, 8):
        block = jnp.zeros((8, 1), jnp.int32)
        for at, value in enumerate(order[first : first + 8]):
            block = jnp.where(row == at, value, block)
        blocks.append(block)
    wave = jnp.concatenate(blocks, axis=0)
    start = wave * (me * cols)
    turns = jnp.floor(start.astype(f32) * (1.0 / period)).astype(jnp.int32)
    start = (start - turns * period).astype(f32)
    wave = wave.astype(f32)
    row = lax.broadcasted_iota(jnp.int32, (waves, 1), 0)
    if paired:
        row = lax.rem(row, 2 * slots)
    sine = (row >= (slots if paired else waves // 2)).astype(f32)
    offset = 4.0 * start - period * sine
    for tile in range(0, width, 128):
        lane = lax.broadcasted_iota(jnp.int32, (1, 128), 1) + tile
        lane = jnp.where(lane < cols + MARGIN, lane, lane - width).astype(f32)
        product = wave * lane
        product = product - period * jnp.floor(product * (1.0 / period))
        quarter = 4.0 * product + offset
        turn = jnp.floor(quarter * (1.0 / period) + 0.5)
        angle = (quarter - period * turn) * (0.5 * math.pi / period)
        square = angle * angle
        cosine = 1.0 + square * (
            -1.0 / 2 + square * (1.0 / 24 + square * (-1.0 / 720 + square * (1.0 / 40320)))
        )
        sine_of = angle * (
            1.0
            + square
            * (-1.0 / 6 + square * (1.0 / 120 + square * (-1.0 / 5040 + square * (1.0 / 362880))))
        )
        phase = turn - 4.0 * jnp.floor(turn * 0.25)
        odd = (phase == 1.0) | (phase == 3.0)
        value = jnp.where(odd, sine_of, cosine)
        value = jnp.where((phase == 1.0) | (phase == 2.0), -value, value)
        hi, lo = split2(value)
        harm_ref[:waves, tile : tile + 128] = hi
        harm_ref[waves:, tile : tile + 128] = lo


def transform_kernel(
    period,
    slots,
    waves_hbm,
    height_hbm,
    east_hbm,
    north_hbm,
    land_hbm,
    keep_ref,
    send_ref,
    tile_ref,
    waves_ref,
    height_ref,
    flow_front,
    flow_back,
    land_front,
    land_back,
    harm_ref,
    field_ref,
    semaphores,
):
    rows, cols = height_ref.shape
    waves, width = harm_ref.shape[0] // 2, harm_ref.shape[1]
    back = cols - land_back.shape[1]
    fronts, backs = pl.ds(0, 128), pl.ds(back, cols - back)
    copies = [
        pltpu.make_async_copy(source, target, semaphores.at[at])
        for at, (source, target) in enumerate(
            (
                (waves_hbm, waves_ref),
                (height_hbm, height_ref),
                (east_hbm.at[:, fronts], flow_front.at[0]),
                (east_hbm.at[:, backs], flow_back.at[0]),
                (north_hbm.at[:, fronts], flow_front.at[1]),
                (north_hbm.at[:, backs], flow_back.at[1]),
                (land_hbm.at[:, fronts], land_front),
                (land_hbm.at[:, backs], land_back),
            )
        )
    ]
    for copy in copies:
        copy.start()
    copies[0].wait()
    harmonic_rows(period, cols, slots, lax.axis_index("lon"), True, waves_ref, harm_ref)
    for copy in copies[1:]:
        copy.wait()
    for tile in range(0, width, 128):
        stop = min(cols, tile + 128)
        if stop <= tile:
            block = jnp.zeros((rows, 128), f32)
        elif stop == tile + 128:
            block = height_ref[:, tile : tile + 128]
        else:
            block = jnp.concatenate(
                [height_ref[:, tile:stop], jnp.zeros((rows, tile + 128 - stop), f32)], axis=1
            )
        hi, lo = split2(block)
        field_ref[:rows, tile : tile + 128] = hi
        field_ref[rows:, tile : tile + 128] = lo
    rows_by_rows = (((1,), (1,)), ((), ()))
    high = lax.dot_general(
        harm_ref[...], field_ref[:rows], rows_by_rows, preferred_element_type=f32
    )
    low = lax.dot_general(
        harm_ref[:waves], field_ref[rows:], rows_by_rows, preferred_element_type=f32
    )
    total = (high[:waves] + high[waves:] + low) * (1.0 / math.sqrt(period))
    total = jnp.concatenate([total, jnp.zeros((waves, 128 - rows), f32)], axis=1)
    keep_ref[...] = total[: waves // 2].reshape(keep_ref.shape)
    send_ref[: waves // 2] = total[waves // 2 :]
    pieces = []
    for front, end in (
        (height_ref[:, :MARGIN], height_ref[:, cols - MARGIN :]),
        (flow_front[0, :, :MARGIN], flow_back[0, :, cols - MARGIN - back :]),
        (flow_front[1, :, :MARGIN], flow_back[1, :, cols - MARGIN - back :]),
        (land_front[:, :MARGIN].astype(f32), land_back[:, cols - MARGIN - back :].astype(f32)),
    ):
        pieces += [front, end]
    half = rows // 2
    tile = jnp.concatenate(
        [piece[:half] for piece in pieces] + [piece[half:] for piece in pieces], axis=1
    )
    send_ref[waves // 2 :] = tile
    tile_ref[...] = tile


def stage_kernel(
    after_ref,
    height_hbm,
    east_hbm,
    north_hbm,
    land_hbm,
    legendre_hbm,
    even_ref,
    odd_ref,
    legendre_ref,
    flows,
    lands,
    semaphores,
):
    rows, cols = height_hbm.shape
    width = even_ref.shape[2]
    copies = []
    for side, first in enumerate((rows - MARGIN, 0)):
        band = pl.ds(first, MARGIN)
        copies.append((height_hbm.at[band], flows.at[side, 0]))
        copies.append((east_hbm.at[band], flows.at[side, 1]))
        copies.append((north_hbm.at[band], flows.at[side, 2]))
        copies.append((land_hbm.at[band], lands.at[side]))
    copies.append((legendre_hbm, legendre_ref))
    copies = [
        pltpu.make_async_copy(source, target, semaphores.at[at])
        for at, (source, target) in enumerate(copies)
    ]
    for copy in copies:
        copy.start()
    for copy in copies[:-1]:
        copy.wait()
    is_even = lax.rem(lax.axis_index("lat"), 2) == 0
    for at in range(4):
        up, down = [lands[side].astype(f32) if at == 3 else flows[side, at] for side in range(2)]
        even_ref[at, :, :cols] = jnp.where(is_even, up, down)
        odd_ref[at, :, :cols] = jnp.where(is_even, down, up)
        if cols < width:
            blank = jnp.zeros((MARGIN, width - cols), f32)
            even_ref[at, :, cols:] = blank
            odd_ref[at, :, cols:] = blank
    copies[-1].wait()


def mix_kernel(keep_ref, tile_ref, recv_ref, own_ref, *send_refs):
    chips, group, _ = keep_ref.shape
    own_ref[...] = keep_ref[0] + recv_ref[:group]
    for shift, ref in enumerate(send_refs, 1):
        ref[:group] = keep_ref[shift] + recv_ref[shift * group : (shift + 1) * group]
        if ref.shape[0] > group:
            ref[group:] = tile_ref[...]


def analysis_kernel(part_refs, core_ref, legendre_ref, spectral_ref, even_ref, odd_ref):
    slots, rows, degrees = legendre_ref.shape
    chips, half = len(part_refs), rows // 2
    left, right = side_tiles(lax.axis_index("lon"), 2 * slots, chips, core_ref, part_refs[1], part_refs[-1])
    lanes = lax.broadcasted_iota(jnp.int32, left.shape, 1)
    both = jnp.where(lax.rem(lanes, 2 * MARGIN) < MARGIN, right, left)
    up, down = pltpu.roll(both[half - MARGIN :], 64, 1), both[:MARGIN]
    is_even = lax.rem(lax.axis_index("lat"), 2) == 0
    ahead = even_ref.shape[1] - 128
    even_ref[:, ahead:] = jnp.where(is_even, up, down)
    odd_ref[:, ahead:] = jnp.where(is_even, down, up)
    fourier = part_refs[0][...]
    for ref in part_refs[1:]:
        fourier = fourier + ref[: 2 * slots]
    columns = fourier.T
    for slot in range(slots):
        even = [
            jnp.broadcast_to(columns[o : o + 8, slot : slot + 1], (8, 128))
            for o in range(0, rows, 8)
        ]
        odd = [
            jnp.broadcast_to(columns[o : o + 8, slots + slot : slots + slot + 1], (8, 128))
            for o in range(0, rows, 8)
        ]
        for tile in range(0, degrees, 128):
            first = jnp.zeros((8, 128), f32)
            second = jnp.zeros((8, 128), f32)
            for at, o in enumerate(range(0, rows, 8)):
                block = legendre_ref[slot, o : o + 8, tile : tile + 128]
                first = first + block * even[at]
                second = second + block * odd[at]
            spectral_ref[slot : slot + 1, tile : tile + 128] = jnp.sum(
                first, axis=0, keepdims=True
            )
            spectral_ref[slots + slot : slots + slot + 1, tile : tile + 128] = jnp.sum(
                second, axis=0, keepdims=True
            )
    if ahead:
        even_ref[:, :ahead] = spectral_ref[...]
        odd_ref[:, :ahead] = spectral_ref[...]

def synthesis_kernel(parts_refs, love_ref, legendre_ref, out_ref, spectral_ref):
    slots, rows, degrees = legendre_ref.shape
    total = parts_refs[0][...]
    for ref in parts_refs[1:]:
        total = total + ref[:, :degrees]
    spectral_ref[...] = total * love_ref[...]
    lanes = lax.broadcasted_iota(jnp.int32, (8, 128), 1)
    octets = range(0, rows, 8)
    sums = [jnp.zeros((8, 128), f32) for _ in octets]
    for slot in range(slots):
        first = [jnp.zeros((8, 128), f32) for _ in octets]
        second = [jnp.zeros((8, 128), f32) for _ in octets]
        for tile in range(0, degrees, 128):
            even = jnp.broadcast_to(spectral_ref[slot : slot + 1, tile : tile + 128], (8, 128))
            odd = jnp.broadcast_to(
                spectral_ref[slots + slot : slots + slot + 1, tile : tile + 128], (8, 128)
            )
            for at, o in enumerate(octets):
                block = legendre_ref[slot, o : o + 8, tile : tile + 128]
                first[at] = first[at] + block * even
                second[at] = second[at] + block * odd
        for at in range(len(octets)):
            sums[at] = jnp.where(lanes == slot, jnp.sum(first[at], axis=1, keepdims=True), sums[at])
            sums[at] = jnp.where(
                lanes == slots + slot, jnp.sum(second[at], axis=1, keepdims=True), sums[at]
            )
    column = jnp.concatenate(sums + [jnp.zeros((128 - rows, 128), f32)], axis=0)
    lines = column.T[: 2 * slots]
    lines = lines[:slots] + pltpu.roll(lines[slots:], 64, 1)
    out_ref[...] = jnp.broadcast_to(lines[None], out_ref.shape)


def side_tiles(me, group, chips, core_ref, west_ref, east_ref):
    first = lax.rem(me, 2) == 0
    other = core_ref[chips * group :]
    west, east = west_ref[group:], east_ref[group:]
    if chips == 4:
        even = lax.rem(me // 2, 2) == 0
        west, east = jnp.where(even, east, west), jnp.where(even, west, east)
    left = jnp.where(first, west, other)
    right = jnp.where(first, other, east)
    return left, right


def with_sides(tail, left, right, own, at):
    lanes = lax.broadcasted_iota(jnp.int32, tail.shape, 1)
    after = pltpu.roll(right, (own - 2 * MARGIN * at) % 128, 1)
    before = pltpu.roll(left, (-MARGIN - 2 * MARGIN * at - MARGIN) % 128, 1)
    repeat = tail.shape[1] // 128
    after = jnp.concatenate([after] * repeat, axis=1)
    before = jnp.concatenate([before] * repeat, axis=1)
    tail = jnp.where((lanes >= own) & (lanes < own + MARGIN), after, tail)
    return jnp.where(lanes >= tail.shape[1] - MARGIN, before, tail)


def interleaved(ref, step):
    return [ref[pl.ds(at, 8, stride=step)] for at in range(step)]


def windows_kernel(
    period,
    slots,
    chips,
    bands,
    waves_hbm,
    height_hbm,
    east_hbm,
    north_hbm,
    land_hbm,
    core_ref,
    west_ref,
    east_ref,
    even_rows,
    odd_rows,
    even_ref,
    odd_ref,
    surface_win,
    east_win,
    north_win,
    wet_win,
    moved_win,
    harm_ref,
    waves_ref,
    fields,
    land,
    natural,
    semaphores,
):
    rows, cols = height_hbm.shape
    width = harm_ref.shape[1]
    taller = rows + 2 * MARGIN
    step = taller // 8
    last = (cols // 128) * 128
    copies = [
        pltpu.make_async_copy(source, target, semaphores.at[at])
        for at, (source, target) in enumerate(
            (
                (height_hbm, fields.at[0]),
                (east_hbm, fields.at[1]),
                (north_hbm, fields.at[2]),
                (land_hbm, land),
                (waves_hbm, waves_ref),
            )
        )
    ]
    for copy in copies:
        copy.start()
    copies[4].wait()
    harmonic_rows(period, cols, slots, lax.axis_index("lon"), False, waves_ref, harm_ref)
    left, right = side_tiles(
        lax.axis_index("lon"), 2 * slots, chips, core_ref, west_ref, east_ref
    )
    left = jnp.concatenate([left, pltpu.roll(left, 64, 1)], axis=0)
    right = jnp.concatenate([right, pltpu.roll(right, 64, 1)], axis=0)
    band = lax.axis_index("lat")
    is_even = lax.rem(band, 2) == 0
    even, odd = even_ref[:, -128:], odd_ref[:, -128:]
    corners = (jnp.where(is_even, odd, even), jnp.where(is_even, even, odd))
    for copy in copies[:4]:
        copy.wait()
    middle = pl.ds(MARGIN, rows)
    for at, target in ((3, wet_win), (0, surface_win), (1, east_win), (2, north_win)):
        field = fields.at[at] if at < 3 else land
        even, odd = even_rows[at], odd_rows[at]
        halos = (jnp.where(is_even, odd, even), jnp.where(is_even, even, odd))
        for tile in range(0, last, 128):
            natural[tile // 128, middle] = field[:, tile : tile + 128].astype(f32)
        tail = jnp.concatenate(
            [field[:, last:].astype(f32), jnp.zeros((rows, width - cols), f32)], axis=1
        )
        tail = with_sides(tail, left, right, cols - last, at)
        for tile in range(last, width, 128):
            natural[tile // 128, middle] = tail[:, tile - last : tile - last + 128]
        for halo, corner, first, inside in zip(
            halos, corners, (0, MARGIN + rows), (band > 0, band < bands - 1)
        ):
            halo = jnp.where(inside, halo, 0.0)
            tail = with_sides(halo[:, last:], corner, corner, cols - last, at)
            tail = jnp.where(inside, tail, 0.0)
            for tile in range(0, width, 128):
                block = tail[:, tile - last :][:, :128] if tile >= last else halo[:, tile:][:, :128]
                natural[tile // 128, pl.ds(first, MARGIN)] = block
        for tile in range(0, width, 128):
            for v, block in enumerate(interleaved(natural.at[tile // 128], step)):
                place = (slice(8 * v, 8 * v + 8), slice(tile, tile + 128))
                if at == 3:
                    block = STEP * block
                elif at > 0:
                    block = jnp.where(wet_win[place] > 0.0, block, 0.0)
                target[place] = block
        if at in (1, 3):
            shifted = east_win if at == 1 else moved_win
            for v in range(step):
                shifted[8 * v : 8 * v + 8] = pltpu.roll(target[8 * v : 8 * v + 8], 1, 1)


def substep_kernel(
    sectors,
    bands,
    synth_ref,
    harm_ref,
    surface_win,
    east_win,
    north_win,
    wet,
    moved,
    loading_hbm,
    surface_hbm,
    east_hbm,
    north_hbm,
    column,
    load,
    pressure,
    east,
    north,
    natural,
    loading_out,
    surface_out,
    east_out,
    north_out,
    semaphores,
):
    rows, cols = loading_hbm.shape
    taller, width = wet.shape
    step = taller // 8
    waves = harm_ref.shape[0] // 2
    me, band = lax.axis_index("lon"), lax.axis_index("lat")
    below, above = jnp.maximum(band - 1, 0), jnp.minimum(band + 1, bands - 1)

    def gathered(place):
        lines = [
            synth_ref[place * sectors + owner(me, sectors, core, shift)]
            for core, shift in row_groups(sectors)
        ]
        lines = jnp.concatenate(lines, axis=0)
        return lines.T

    scale = 1.0 / math.sqrt(waves // 2)
    own = gathered(band) * scale
    low = jnp.where(band > 0, gathered(below)[rows - MARGIN :], 0.0) * scale
    high = jnp.where(band < bands - 1, gathered(above), 0.0) * scale
    pieces = []
    for at in range(2):
        first = 64 * at
        column[at, :MARGIN, : waves // 2] = low[first : first + MARGIN]
        column[at, MARGIN : MARGIN + rows, : waves // 2] = own[first : first + rows]
        column[at, MARGIN + rows :, : waves // 2] = high[first : first + MARGIN]
        pieces.append(
            jnp.concatenate(interleaved(column.at[at], step), axis=0)[:, : waves // 2]
        )
    hi, lo = split2(jnp.concatenate(pieces, axis=1))
    columns = (((1,), (0,)), ((), ()))
    both = lax.dot_general(
        jnp.concatenate([hi, hi], axis=1), harm_ref[...], columns, preferred_element_type=f32
    )
    both = both + lax.dot_general(lo, harm_ref[:waves], columns, preferred_element_type=f32)
    load[...] = both
    pressure[...] = surface_win[...] - both
    copies = [
        pltpu.make_async_copy(source, target, semaphores.at[at])
        for at, (source, target) in enumerate(
            (
                (loading_out, loading_hbm),
                (surface_out, surface_hbm),
                (east_out, east_hbm),
                (north_out, north_hbm),
            )
        )
    ]

    def give(at, target, blocks):
        for v, block in enumerate(blocks):
            for tile in range(0, width, 128):
                natural[at, tile // 128, pl.ds(v, 8, stride=step)] = block[:, tile : tile + 128]
        for tile in range(0, cols, 128):
            stop = min(cols, tile + 128)
            target[:, tile:stop] = natural[at, tile // 128, pl.ds(MARGIN, rows), : stop - tile]
        copies[at].start()

    def block(ref, v):
        return ref[8 * v : 8 * v + 8]

    def across(ref, v):
        after = pltpu.roll(block(ref, 0), 7, 0) if v == step - 1 else block(ref, v + 1)
        before = pltpu.roll(block(ref, step - 1), 1, 0) if v == 0 else block(ref, v - 1)
        return after - before

    give(0, loading_out, [block(load, v) for v in range(step)])
    for substep in range(SUBSTEPS):
        first, final = substep == 0, substep == SUBSTEPS - 1
        for v in range(step):
            here = block(pressure, v)
            flow = block(east_win if first else east, v)
            flow = flow - block(moved, v) * (here - pltpu.roll(here, 2, 1))
            east[8 * v : 8 * v + 8] = flow
            flow = block(north_win if first else north, v)
            north[8 * v : 8 * v + 8] = flow - block(wet, v) * across(pressure, v)
        if final:
            give(2, east_out, [pltpu.roll(block(east, v), width - 1, 1) for v in range(step)])
            give(3, north_out, [block(north, v) for v in range(step)])
        levels = []
        for v in range(step):
            flow = block(east, v)
            change = pltpu.roll(flow, width - 2, 1) - flow + across(north, v)
            level = block(pressure, v) - block(wet, v) * change
            if final:
                levels.append(level + block(load, v))
            else:
                pressure[8 * v : 8 * v + 8] = level
        if final:
            give(1, surface_out, levels)
    for copy in copies:
        copy.wait()


def shards(height, east_flow, north_flow, legendre, love_numbers, wavenumbers, land_sea):
    rows, cols = height.shape
    slots, _, degrees = legendre.shape
    sectors, bands = lax.axis_size("lon"), lax.axis_size("lat")
    chips = sectors // 2
    waves = wavenumbers.shape[0]
    period = cols * sectors
    width = -(-(cols + 2 * MARGIN) // 128) * 128
    taller = rows + 2 * MARGIN
    group, half = 2 * slots, rows // 2
    back = (cols - MARGIN) // 128 * 128
    DMA = pltpu.SemaphoreType.DMA
    fields = (height, east_flow, north_flow, land_sea)

    keep, send, tile = pl.pallas_call(
        functools.partial(transform_kernel, period, slots),
        out_shape=[
            struct((chips, group, 128)),
            struct((chips * group + half, 128)),
            struct((half, 128)),
        ],
        in_specs=[HBM] * 5,
        out_specs=[VMEM] * 3,
        scratch_shapes=[
            pltpu.SMEM((waves,), jnp.int32),
            pltpu.VMEM((rows, cols), f32),
            pltpu.VMEM((2, rows, 128), f32),
            pltpu.VMEM((2, rows, cols - back), f32),
            pltpu.VMEM((rows, 128), jnp.int32),
            pltpu.VMEM((rows, cols - back), jnp.int32),
            pltpu.VMEM((4 * waves, width), bf16),
            pltpu.VMEM((2 * rows, width), bf16),
            DMA((8,)),
        ],
        name="transform",
        compiler_params=LIMIT,
    )(*in_hbm(wavenumbers, *fields))
    core = lax.ppermute(send, "lon", [(i, i ^ 1) for i in range(sectors)])
    neighbours = (1, chips - 1)
    own, *outgoing = pl.pallas_call(
        mix_kernel,
        out_shape=[struct((group, 128))]
        + [
            struct((group + (half if shift in neighbours else 0), 128))
            for shift in range(1, chips)
        ],
        in_specs=[VMEM] * 3,
        out_specs=[VMEM] * chips,
        name="mix",
        compiler_params=LIMIT,
    )(keep, tile, core)
    arrived = []
    for shift, block in enumerate(outgoing, 1):
        across = [
            (i, 2 * chip_at(i // 2, shift, chips) + 1 - i % 2) for i in range(sectors)
        ]
        arrived.append(lax.ppermute(block, "lon", across))
    sides = (core, arrived[0], arrived[-1])

    even, odd, legendre = pl.pallas_call(
        stage_kernel,
        out_shape=[struct((4, MARGIN, width))] * 2 + [struct(legendre.shape)],
        in_specs=[VMEM] + [HBM] * 5,
        out_specs=[VMEM] * 3,
        scratch_shapes=[
            pltpu.VMEM((2, 3, MARGIN, cols), f32),
            pltpu.VMEM((2, MARGIN, cols), jnp.int32),
            DMA((9,)),
        ],
        name="stage",
        compiler_params=LIMIT,
    )(own, *in_hbm(*fields, legendre))
    links = [[(i, (i + 1) % bands) for i in range(first, bands, 2)] for first in (0, 1)]
    links = [pairs + [(j, i) for i, j in pairs] for pairs in links]
    even, odd = [lax.ppermute(block, "lat", pairs) for block, pairs in zip((even, odd), links)]

    def analysis(*refs):
        analysis_kernel(refs[:chips], *refs[chips:])

    together = bands == 4
    message = 128 + (degrees if together else 0)
    spectral, *corners = pl.pallas_call(
        analysis,
        out_shape=[struct((group, degrees))] + [struct((MARGIN, message))] * 2,
        in_specs=[VMEM] * (chips + 2),
        out_specs=[VMEM] * 3,
        name="analysis",
        compiler_params=LIMIT,
    )(own, *arrived, core, legendre)
    if together:
        *corners, across = [
            lax.ppermute(block, "lat", [(i, i ^ step) for i in range(bands)])
            for block, step in ((corners[0], 1), (corners[1], 3), (spectral, 2))
        ]
        pieces = [spectral, corners[1], corners[0], across]
    else:
        corners = [
            lax.ppermute(block, "lat", pairs) for block, pairs in zip(corners, links)
        ]
        pieces = [lax.psum(spectral, "lat")]

    def synthesis(*refs):
        synthesis_kernel(refs[: len(pieces)], *refs[len(pieces) :])

    synth = pl.pallas_call(
        synthesis,
        out_shape=struct((bands * sectors, slots, 128)),
        in_specs=[VMEM] * (len(pieces) + 2),
        out_specs=VMEM,
        scratch_shapes=[pltpu.VMEM((group, degrees), f32)],
        name="synthesis",
        cost_estimate=pl.CostEstimate(flops=100000000000, bytes_accessed=400000000, transcendentals=0),
        compiler_params=LIMIT,
    )(*pieces, love_numbers.reshape(1, degrees), legendre)
    everyone = lax.all_to_all(synth, ("lat", "lon"), 0, 0, tiled=True)

    *windows, harmonics = pl.pallas_call(
        functools.partial(windows_kernel, period, slots, chips, bands),
        out_shape=[struct((taller, width))] * 5 + [struct((4 * waves, width), bf16)],
        in_specs=[HBM] * 5 + [VMEM] * 7,
        out_specs=[VMEM] * 6,
        scratch_shapes=[
            pltpu.SMEM((waves,), jnp.int32),
            pltpu.VMEM((3, rows, cols), f32),
            pltpu.VMEM((rows, cols), jnp.int32),
            pltpu.VMEM((width // 128, taller, 128), f32),
            DMA((5,)),
        ],
        name="windows",
        cost_estimate=pl.CostEstimate(flops=10**11, bytes_accessed=4 * 10**8, transcendentals=0),
        compiler_params=LIMIT,
    )(*in_hbm(wavenumbers, *fields), *sides, even, odd, *corners)

    return pl.pallas_call(
        functools.partial(substep_kernel, sectors, bands),
        out_shape=[struct((rows, cols))] * 4,
        in_specs=[VMEM] * 7,
        out_specs=[HBM] * 4,
        scratch_shapes=[
            pltpu.VMEM((2, taller, 128), f32),
            pltpu.VMEM((taller, width), f32),
            pltpu.VMEM((taller, width), f32),
            pltpu.VMEM((taller, width), f32),
            pltpu.VMEM((taller, width), f32),
            pltpu.VMEM((4, width // 128, taller, 128), f32),
        ]
        + [pltpu.VMEM((rows, cols), f32)] * 4
        + [DMA((4,))],
        name="substeps",
        compiler_params=LIMIT,
    )(everyone, harmonics, *windows)


def solution(mesh):
    return jax.shard_map(
        shards,
        mesh=mesh,
        in_specs=(
            P("lat", "lon"),
            P("lat", "lon"),
            P("lat", "lon"),
            P("lon", "lat", None),
            P(),
            P(),
            P("lat", "lon"),
        ),
        out_specs=(P("lat", "lon"), P("lat", "lon"), P("lat", "lon"), P("lat", "lon")),
        check_vma=False,
    )
```

```python
import functools
import math

import jax
import jax.numpy as jnp
from jax import lax
from jax.experimental import pallas as pl
from jax.experimental.pallas import tpu as pltpu
from jax.sharding import PartitionSpec as P

SUBSTEPS = 4
MARGIN = 2 * SUBSTEPS
STEP = 0.3

f32 = jnp.float32
bf16 = jnp.bfloat16
VMEM = pl.BlockSpec(memory_space=pltpu.VMEM)
HBM = pl.BlockSpec(memory_space=pltpu.HBM)
SMEM = pl.BlockSpec(memory_space=pltpu.SMEM)
LIMIT = pltpu.CompilerParams(vmem_limit_bytes=24 * 2**20)


def struct(shape, dtype=f32):
    return jax.ShapeDtypeStruct(shape, dtype)


def in_hbm(*arrays):
    return [pltpu.with_memory_space_constraint(x, pltpu.HBM) for x in arrays]


def split2(x):
    hi = x.astype(bf16)
    lo = (x - hi.astype(f32)).astype(bf16)
    return hi, lo


def chip_at(chip, shift, chips):
    return chip ^ shift if chips == 4 else (chip + shift) % chips


def owner(me, sectors, core, shift):
    crossed = core if shift == 0 else 1 - core
    chip = chip_at(me // 2, shift, sectors // 2)
    return 2 * chip + lax.bitwise_xor(lax.rem(me, 2), crossed)


def row_groups(sectors):
    return [(core, shift) for core in range(2) for shift in range(sectors // 2)]


def harmonic_rows(period, cols, slots, me, paired, waves_ref, harm_ref):
    waves, width = harm_ref.shape[0] // 2, harm_ref.shape[1]
    sectors = waves // (2 * slots)
    order = []
    for core, shift in row_groups(sectors):
        first = owner(me, sectors, core, shift) * slots
        group = [waves_ref[first + slot] for slot in range(slots)]
        order += group
    row = lax.broadcasted_iota(jnp.int32, (8, 1), 0)
    blocks = []
    for first in range(0, waves // 2, 8):
        block = jnp.zeros((8, 1), jnp.int32)
        for at, value in enumerate(order[first : first + 8]):
            block = jnp.where(row == at, value, block)
        blocks.append(block)
    wave = jnp.concatenate(blocks, axis=0)
    start = wave * (me * cols)
    turns = jnp.floor(start.astype(f32) * (1.0 / period)).astype(jnp.int32)
    start = (start - turns * period).astype(f32)
    wave = wave.astype(f32)
    for tile in range(0, width, 128):
        lane = lax.broadcasted_iota(jnp.int32, (1, 128), 1) + tile
        lane = jnp.where(lane < cols + MARGIN, lane, lane - width).astype(f32)
        product = wave * lane
        product = product - period * jnp.floor(product * (1.0 / period))
        quarter = 4.0 * (product + start)
        turn = jnp.floor(quarter * (1.0 / period) + 0.5)
        angle = (quarter - period * turn) * (0.5 * math.pi / period)
        square = angle * angle
        cosine = 1.0 + square * (
            -1.0 / 2 + square * (1.0 / 24 + square * (-1.0 / 720 + square * (1.0 / 40320)))
        )
        sine_of = angle * (
            1.0
            + square
            * (-1.0 / 6 + square * (1.0 / 120 + square * (-1.0 / 5040 + square * (1.0 / 362880))))
        )
        phase = turn - 4.0 * jnp.floor(turn * 0.25)
        odd = (phase == 1.0) | (phase == 3.0)
        cosines = jnp.where(odd, sine_of, cosine)
        cosines = jnp.where((phase == 1.0) | (phase == 2.0), -cosines, cosines)
        sines = jnp.where(odd, cosine, sine_of)
        sines = jnp.where(phase >= 2.0, -sines, sines)
        if paired:
            parts = []
            for first in range(0, waves // 2, slots):
                parts += [cosines[first : first + slots], sines[first : first + slots]]
        else:
            parts = [cosines, sines]
        value = jnp.concatenate(parts, axis=0)
        hi, lo = split2(value)
        harm_ref[:waves, tile : tile + 128] = hi
        harm_ref[waves:, tile : tile + 128] = lo


def transform_kernel(
    period,
    slots,
    waves_hbm,
    height_hbm,
    east_hbm,
    north_hbm,
    land_hbm,
    keep_ref,
    send_ref,
    tile_ref,
    waves_ref,
    height_ref,
    flow_front,
    flow_back,
    land_front,
    land_back,
    harm_ref,
    field_ref,
    semaphores,
):
    rows, cols = height_ref.shape
    waves, width = harm_ref.shape[0] // 2, harm_ref.shape[1]
    back = cols - land_back.shape[1]
    fronts, backs = pl.ds(0, 128), pl.ds(back, cols - back)
    copies = [
        pltpu.make_async_copy(source, target, semaphores.at[at])
        for at, (source, target) in enumerate(
            (
                (waves_hbm, waves_ref),
                (height_hbm, height_ref),
                (east_hbm.at[:, fronts], flow_front.at[0]),
                (east_hbm.at[:, backs], flow_back.at[0]),
                (north_hbm.at[:, fronts], flow_front.at[1]),
                (north_hbm.at[:, backs], flow_back.at[1]),
                (land_hbm.at[:, fronts], land_front),
                (land_hbm.at[:, backs], land_back),
            )
        )
    ]
    for copy in copies:
        copy.start()
    copies[0].wait()
    harmonic_rows(period, cols, slots, lax.axis_index("lon"), True, waves_ref, harm_ref)
    for copy in copies[1:]:
        copy.wait()
    for tile in range(0, width, 128):
        stop = min(cols, tile + 128)
        if stop <= tile:
            block = jnp.zeros((rows, 128), f32)
        elif stop == tile + 128:
            block = height_ref[:, tile : tile + 128]
        else:
            block = jnp.concatenate(
                [height_ref[:, tile:stop], jnp.zeros((rows, tile + 128 - stop), f32)], axis=1
            )
        hi, lo = split2(block)
        field_ref[:rows, tile : tile + 128] = hi
        field_ref[rows:, tile : tile + 128] = lo
    rows_by_rows = (((1,), (1,)), ((), ()))
    high = lax.dot_general(
        harm_ref[...], field_ref[:rows], rows_by_rows, preferred_element_type=f32
    )
    low = lax.dot_general(
        harm_ref[:waves], field_ref[rows:], rows_by_rows, preferred_element_type=f32
    )
    total = (high[:waves] + high[waves:] + low) * (1.0 / math.sqrt(period))
    total = jnp.concatenate([total, jnp.zeros((waves, 128 - rows), f32)], axis=1)
    keep_ref[...] = total[: waves // 2].reshape(keep_ref.shape)
    send_ref[: waves // 2] = total[waves // 2 :]
    pieces = []
    for front, end in (
        (height_ref[:, :MARGIN], height_ref[:, cols - MARGIN :]),
        (flow_front[0, :, :MARGIN], flow_back[0, :, cols - MARGIN - back :]),
        (flow_front[1, :, :MARGIN], flow_back[1, :, cols - MARGIN - back :]),
        (land_front[:, :MARGIN].astype(f32), land_back[:, cols - MARGIN - back :].astype(f32)),
    ):
        pieces += [front, end]
    half = rows // 2
    tile = jnp.concatenate(
        [piece[:half] for piece in pieces] + [piece[half:] for piece in pieces], axis=1
    )
    send_ref[waves // 2 :] = tile
    tile_ref[...] = tile


def stage_kernel(
    after_ref,
    height_hbm,
    east_hbm,
    north_hbm,
    land_hbm,
    legendre_hbm,
    even_ref,
    odd_ref,
    legendre_ref,
    flows,
    lands,
    semaphores,
):
    rows, cols = height_hbm.shape
    width = even_ref.shape[2]
    copies = []
    for side, first in enumerate((rows - MARGIN, 0)):
        band = pl.ds(first, MARGIN)
        copies.append((height_hbm.at[band], flows.at[side, 0]))
        copies.append((east_hbm.at[band], flows.at[side, 1]))
        copies.append((north_hbm.at[band], flows.at[side, 2]))
        copies.append((land_hbm.at[band], lands.at[side]))
    copies.append((legendre_hbm, legendre_ref))
    copies = [
        pltpu.make_async_copy(source, target, semaphores.at[at])
        for at, (source, target) in enumerate(copies)
    ]
    for copy in copies:
        copy.start()
    for copy in copies[:-1]:
        copy.wait()
    is_even = lax.rem(lax.axis_index("lat"), 2) == 0
    for at in range(4):
        up, down = [lands[side].astype(f32) if at == 3 else flows[side, at] for side in range(2)]
        even_ref[at, :, :cols] = jnp.where(is_even, up, down)
        odd_ref[at, :, :cols] = jnp.where(is_even, down, up)
        if cols < width:
            blank = jnp.zeros((MARGIN, width - cols), f32)
            even_ref[at, :, cols:] = blank
            odd_ref[at, :, cols:] = blank
    copies[-1].wait()


def mix_kernel(keep_ref, tile_ref, recv_ref, own_ref, *send_refs):
    chips, group, _ = keep_ref.shape
    own_ref[...] = keep_ref[0] + recv_ref[:group]
    for shift, ref in enumerate(send_refs, 1):
        ref[:group] = keep_ref[shift] + recv_ref[shift * group : (shift + 1) * group]
        if ref.shape[0] > group:
            ref[group:] = tile_ref[...]


def analysis_kernel(part_refs, core_ref, legendre_ref, spectral_ref, even_ref, odd_ref):
    slots, rows, degrees = legendre_ref.shape
    chips, half = len(part_refs), rows // 2
    left, right = side_tiles(lax.axis_index("lon"), 2 * slots, chips, core_ref, part_refs[1], part_refs[-1])
    lanes = lax.broadcasted_iota(jnp.int32, left.shape, 1)
    both = jnp.where(lax.rem(lanes, 2 * MARGIN) < MARGIN, right, left)
    up, down = pltpu.roll(both[half - MARGIN :], 64, 1), both[:MARGIN]
    is_even = lax.rem(lax.axis_index("lat"), 2) == 0
    ahead = even_ref.shape[1] - 128
    even_ref[:, ahead:] = jnp.where(is_even, up, down)
    odd_ref[:, ahead:] = jnp.where(is_even, down, up)
    fourier = part_refs[0][...]
    for ref in part_refs[1:]:
        fourier = fourier + ref[: 2 * slots]
    columns = fourier.T
    for slot in range(slots):
        even = [
            jnp.broadcast_to(columns[o : o + 8, slot : slot + 1], (8, 128))
            for o in range(0, rows, 8)
        ]
        odd = [
            jnp.broadcast_to(columns[o : o + 8, slots + slot : slots + slot + 1], (8, 128))
            for o in range(0, rows, 8)
        ]
        for tile in range(0, degrees, 128):
            first = jnp.zeros((8, 128), f32)
            second = jnp.zeros((8, 128), f32)
            for at, o in enumerate(range(0, rows, 8)):
                block = legendre_ref[slot, o : o + 8, tile : tile + 128]
                first = first + block * even[at]
                second = second + block * odd[at]
            spectral_ref[slot : slot + 1, tile : tile + 128] = jnp.sum(
                first, axis=0, keepdims=True
            )
            spectral_ref[slots + slot : slots + slot + 1, tile : tile + 128] = jnp.sum(
                second, axis=0, keepdims=True
            )
    if ahead:
        even_ref[:, :ahead] = spectral_ref[...]
        odd_ref[:, :ahead] = spectral_ref[...]

def synthesis_kernel(parts_refs, love_ref, legendre_ref, out_ref, spectral_ref):
    slots, rows, degrees = legendre_ref.shape
    total = parts_refs[0][...]
    for ref in parts_refs[1:]:
        total = total + ref[:, :degrees]
    spectral_ref[...] = total * love_ref[...]
    lanes = lax.broadcasted_iota(jnp.int32, (8, 128), 1)
    octets = range(0, rows, 8)
    sums = [jnp.zeros((8, 128), f32) for _ in octets]
    for slot in range(slots):
        first = [jnp.zeros((8, 128), f32) for _ in octets]
        second = [jnp.zeros((8, 128), f32) for _ in octets]
        for tile in range(0, degrees, 128):
            even = jnp.broadcast_to(spectral_ref[slot : slot + 1, tile : tile + 128], (8, 128))
            odd = jnp.broadcast_to(
                spectral_ref[slots + slot : slots + slot + 1, tile : tile + 128], (8, 128)
            )
            for at, o in enumerate(octets):
                block = legendre_ref[slot, o : o + 8, tile : tile + 128]
                first[at] = first[at] + block * even
                second[at] = second[at] + block * odd
        for at in range(len(octets)):
            sums[at] = jnp.where(lanes == slot, jnp.sum(first[at], axis=1, keepdims=True), sums[at])
            sums[at] = jnp.where(
                lanes == slots + slot, jnp.sum(second[at], axis=1, keepdims=True), sums[at]
            )
    column = jnp.concatenate(sums + [jnp.zeros((128 - rows, 128), f32)], axis=0)
    lines = column.T[: 2 * slots]
    lines = lines[:slots] + pltpu.roll(lines[slots:], 64, 1)
    out_ref[...] = jnp.broadcast_to(lines[None], out_ref.shape)


def side_tiles(me, group, chips, core_ref, west_ref, east_ref):
    first = lax.rem(me, 2) == 0
    other = core_ref[chips * group :]
    west, east = west_ref[group:], east_ref[group:]
    if chips == 4:
        even = lax.rem(me // 2, 2) == 0
        west, east = jnp.where(even, east, west), jnp.where(even, west, east)
    left = jnp.where(first, west, other)
    right = jnp.where(first, other, east)
    return left, right


def with_sides(tail, left, right, own, at):
    lanes = lax.broadcasted_iota(jnp.int32, tail.shape, 1)
    after = pltpu.roll(right, (own - 2 * MARGIN * at) % 128, 1)
    before = pltpu.roll(left, (-MARGIN - 2 * MARGIN * at - MARGIN) % 128, 1)
    repeat = tail.shape[1] // 128
    after = jnp.concatenate([after] * repeat, axis=1)
    before = jnp.concatenate([before] * repeat, axis=1)
    tail = jnp.where((lanes >= own) & (lanes < own + MARGIN), after, tail)
    return jnp.where(lanes >= tail.shape[1] - MARGIN, before, tail)


def interleaved(ref, step):
    return [ref[pl.ds(at, 8, stride=step)] for at in range(step)]


def windows_kernel(
    period,
    slots,
    chips,
    bands,
    waves_hbm,
    height_hbm,
    east_hbm,
    north_hbm,
    land_hbm,
    core_ref,
    west_ref,
    east_ref,
    even_rows,
    odd_rows,
    even_ref,
    odd_ref,
    surface_win,
    east_win,
    north_win,
    wet_win,
    moved_win,
    harm_ref,
    waves_ref,
    fields,
    land,
    natural,
    semaphores,
):
    rows, cols = height_hbm.shape
    width = harm_ref.shape[1]
    taller = rows + 2 * MARGIN
    step = taller // 8
    last = (cols // 128) * 128
    copies = [
        pltpu.make_async_copy(source, target, semaphores.at[at])
        for at, (source, target) in enumerate(
            (
                (height_hbm, fields.at[0]),
                (east_hbm, fields.at[1]),
                (north_hbm, fields.at[2]),
                (land_hbm, land),
                (waves_hbm, waves_ref),
            )
        )
    ]
    for copy in copies:
        copy.start()
    copies[4].wait()
    harmonic_rows(period, cols, slots, lax.axis_index("lon"), False, waves_ref, harm_ref)
    left, right = side_tiles(
        lax.axis_index("lon"), 2 * slots, chips, core_ref, west_ref, east_ref
    )
    left = jnp.concatenate([left, pltpu.roll(left, 64, 1)], axis=0)
    right = jnp.concatenate([right, pltpu.roll(right, 64, 1)], axis=0)
    band = lax.axis_index("lat")
    is_even = lax.rem(band, 2) == 0
    even, odd = even_ref[:, -128:], odd_ref[:, -128:]
    corners = (jnp.where(is_even, odd, even), jnp.where(is_even, even, odd))
    for copy in copies[:4]:
        copy.wait()
    middle = pl.ds(MARGIN, rows)
    for at, target in ((3, wet_win), (0, surface_win), (1, east_win), (2, north_win)):
        field = fields.at[at] if at < 3 else land
        even, odd = even_rows[at], odd_rows[at]
        halos = (jnp.where(is_even, odd, even), jnp.where(is_even, even, odd))
        for tile in range(0, last, 128):
            natural[tile // 128, middle] = field[:, tile : tile + 128].astype(f32)
        tail = jnp.concatenate(
            [field[:, last:].astype(f32), jnp.zeros((rows, width - cols), f32)], axis=1
        )
        tail = with_sides(tail, left, right, cols - last, at)
        for tile in range(last, width, 128):
            natural[tile // 128, middle] = tail[:, tile - last : tile - last + 128]
        for halo, corner, first, inside in zip(
            halos, corners, (0, MARGIN + rows), (band > 0, band < bands - 1)
        ):
            halo = jnp.where(inside, halo, 0.0)
            tail = with_sides(halo[:, last:], corner, corner, cols - last, at)
            tail = jnp.where(inside, tail, 0.0)
            for tile in range(0, width, 128):
                block = tail[:, tile - last :][:, :128] if tile >= last else halo[:, tile:][:, :128]
                natural[tile // 128, pl.ds(first, MARGIN)] = block
        for tile in range(0, width, 128):
            for v, block in enumerate(interleaved(natural.at[tile // 128], step)):
                place = (slice(8 * v, 8 * v + 8), slice(tile, tile + 128))
                if at == 3:
                    block = STEP * block
                elif at > 0:
                    block = jnp.where(wet_win[place] > 0.0, block, 0.0)
                target[place] = block
        if at in (1, 3):
            shifted = east_win if at == 1 else moved_win
            for v in range(step):
                shifted[8 * v : 8 * v + 8] = pltpu.roll(target[8 * v : 8 * v + 8], 1, 1)


def substep_kernel(
    sectors,
    bands,
    synth_ref,
    harm_ref,
    surface_win,
    east_win,
    north_win,
    wet,
    moved,
    loading_hbm,
    surface_hbm,
    east_hbm,
    north_hbm,
    column,
    load,
    pressure,
    east,
    north,
    natural,
    loading_out,
    surface_out,
    east_out,
    north_out,
    semaphores,
):
    rows, cols = loading_hbm.shape
    taller, width = wet.shape
    step = taller // 8
    waves = harm_ref.shape[0] // 2
    me, band = lax.axis_index("lon"), lax.axis_index("lat")
    below, above = jnp.maximum(band - 1, 0), jnp.minimum(band + 1, bands - 1)

    def gathered(place):
        lines = [
            synth_ref[place * sectors + owner(me, sectors, core, shift)]
            for core, shift in row_groups(sectors)
        ]
        lines = jnp.concatenate(lines, axis=0)
        return lines.T

    scale = 1.0 / math.sqrt(waves // 2)
    own = gathered(band) * scale
    low = jnp.where(band > 0, gathered(below)[rows - MARGIN :], 0.0) * scale
    high = jnp.where(band < bands - 1, gathered(above), 0.0) * scale
    pieces = []
    for at in range(2):
        first = 64 * at
        column[at, :MARGIN, : waves // 2] = low[first : first + MARGIN]
        column[at, MARGIN : MARGIN + rows, : waves // 2] = own[first : first + rows]
        column[at, MARGIN + rows :, : waves // 2] = high[first : first + MARGIN]
        pieces.append(
            jnp.concatenate(interleaved(column.at[at], step), axis=0)[:, : waves // 2]
        )
    hi, lo = split2(jnp.concatenate(pieces, axis=1))
    columns = (((1,), (0,)), ((), ()))
    both = lax.dot_general(
        jnp.concatenate([hi, hi], axis=1), harm_ref[...], columns, preferred_element_type=f32
    )
    both = both + lax.dot_general(lo, harm_ref[:waves], columns, preferred_element_type=f32)
    load[...] = both
    pressure[...] = surface_win[...] - both
    copies = [
        pltpu.make_async_copy(source, target, semaphores.at[at])
        for at, (source, target) in enumerate(
            (
                (loading_out, loading_hbm),
                (surface_out, surface_hbm),
                (east_out, east_hbm),
                (north_out, north_hbm),
            )
        )
    ]

    def give(at, target, blocks):
        for v, block in enumerate(blocks):
            for tile in range(0, width, 128):
                natural[at, tile // 128, pl.ds(v, 8, stride=step)] = block[:, tile : tile + 128]
        for tile in range(0, cols, 128):
            stop = min(cols, tile + 128)
            target[:, tile:stop] = natural[at, tile // 128, pl.ds(MARGIN, rows), : stop - tile]
        copies[at].start()

    def block(ref, v):
        return ref[8 * v : 8 * v + 8]

    def across(ref, v):
        after = pltpu.roll(block(ref, 0), 7, 0) if v == step - 1 else block(ref, v + 1)
        before = pltpu.roll(block(ref, step - 1), 1, 0) if v == 0 else block(ref, v - 1)
        return after - before

    give(0, loading_out, [block(load, v) for v in range(step)])
    for substep in range(SUBSTEPS):
        first, final = substep == 0, substep == SUBSTEPS - 1
        for v in range(step):
            here = block(pressure, v)
            flow = block(east_win if first else east, v)
            flow = flow - block(moved, v) * (here - pltpu.roll(here, 2, 1))
            east[8 * v : 8 * v + 8] = flow
            flow = block(north_win if first else north, v)
            north[8 * v : 8 * v + 8] = flow - block(wet, v) * across(pressure, v)
        if final:
            give(2, east_out, [pltpu.roll(block(east, v), width - 1, 1) for v in range(step)])
            give(3, north_out, [block(north, v) for v in range(step)])
        levels = []
        for v in range(step):
            flow = block(east, v)
            change = pltpu.roll(flow, width - 2, 1) - flow + across(north, v)
            level = block(pressure, v) - block(wet, v) * change
            if final:
                levels.append(level + block(load, v))
            else:
                pressure[8 * v : 8 * v + 8] = level
        if final:
            give(1, surface_out, levels)
    for copy in copies:
        copy.wait()


def shards(height, east_flow, north_flow, legendre, love_numbers, wavenumbers, land_sea):
    rows, cols = height.shape
    slots, _, degrees = legendre.shape
    sectors, bands = lax.axis_size("lon"), lax.axis_size("lat")
    chips = sectors // 2
    waves = wavenumbers.shape[0]
    period = cols * sectors
    width = -(-(cols + 2 * MARGIN) // 128) * 128
    taller = rows + 2 * MARGIN
    group, half = 2 * slots, rows // 2
    back = (cols - MARGIN) // 128 * 128
    DMA = pltpu.SemaphoreType.DMA
    fields = (height, east_flow, north_flow, land_sea)

    keep, send, tile = pl.pallas_call(
        functools.partial(transform_kernel, period, slots),
        out_shape=[
            struct((chips, group, 128)),
            struct((chips * group + half, 128)),
            struct((half, 128)),
        ],
        in_specs=[HBM] * 5,
        out_specs=[VMEM] * 3,
        scratch_shapes=[
            pltpu.SMEM((waves,), jnp.int32),
            pltpu.VMEM((rows, cols), f32),
            pltpu.VMEM((2, rows, 128), f32),
            pltpu.VMEM((2, rows, cols - back), f32),
            pltpu.VMEM((rows, 128), jnp.int32),
            pltpu.VMEM((rows, cols - back), jnp.int32),
            pltpu.VMEM((4 * waves, width), bf16),
            pltpu.VMEM((2 * rows, width), bf16),
            DMA((8,)),
        ],
        name="transform",
        compiler_params=LIMIT,
    )(*in_hbm(wavenumbers, *fields))
    core = lax.ppermute(send, "lon", [(i, i ^ 1) for i in range(sectors)])
    neighbours = (1, chips - 1)
    own, *outgoing = pl.pallas_call(
        mix_kernel,
        out_shape=[struct((group, 128))]
        + [
            struct((group + (half if shift in neighbours else 0), 128))
            for shift in range(1, chips)
        ],
        in_specs=[VMEM] * 3,
        out_specs=[VMEM] * chips,
        name="mix",
        compiler_params=LIMIT,
    )(keep, tile, core)
    arrived = []
    for shift, block in enumerate(outgoing, 1):
        across = [
            (i, 2 * chip_at(i // 2, shift, chips) + 1 - i % 2) for i in range(sectors)
        ]
        arrived.append(lax.ppermute(block, "lon", across))
    sides = (core, arrived[0], arrived[-1])

    even, odd, legendre = pl.pallas_call(
        stage_kernel,
        out_shape=[struct((4, MARGIN, width))] * 2 + [struct(legendre.shape)],
        in_specs=[VMEM] + [HBM] * 5,
        out_specs=[VMEM] * 3,
        scratch_shapes=[
            pltpu.VMEM((2, 3, MARGIN, cols), f32),
            pltpu.VMEM((2, MARGIN, cols), jnp.int32),
            DMA((9,)),
        ],
        name="stage",
        compiler_params=LIMIT,
    )(own, *in_hbm(*fields, legendre))
    links = [[(i, (i + 1) % bands) for i in range(first, bands, 2)] for first in (0, 1)]
    links = [pairs + [(j, i) for i, j in pairs] for pairs in links]
    even, odd = [lax.ppermute(block, "lat", pairs) for block, pairs in zip((even, odd), links)]

    def analysis(*refs):
        analysis_kernel(refs[:chips], *refs[chips:])

    together = bands == 4
    message = 128 + (degrees if together else 0)
    spectral, *corners = pl.pallas_call(
        analysis,
        out_shape=[struct((group, degrees))] + [struct((MARGIN, message))] * 2,
        in_specs=[VMEM] * (chips + 2),
        out_specs=[VMEM] * 3,
        name="analysis",
        compiler_params=LIMIT,
    )(own, *arrived, core, legendre)
    if together:
        *corners, across = [
            lax.ppermute(block, "lat", [(i, i ^ step) for i in range(bands)])
            for block, step in ((corners[0], 1), (corners[1], 3), (spectral, 2))
        ]
        pieces = [spectral, corners[1], corners[0], across]
    else:
        corners = [
            lax.ppermute(block, "lat", pairs) for block, pairs in zip(corners, links)
        ]
        pieces = [lax.psum(spectral, "lat")]

    def synthesis(*refs):
        synthesis_kernel(refs[: len(pieces)], *refs[len(pieces) :])

    synth = pl.pallas_call(
        synthesis,
        out_shape=struct((bands * sectors, slots, 128)),
        in_specs=[VMEM] * (len(pieces) + 2),
        out_specs=VMEM,
        scratch_shapes=[pltpu.VMEM((group, degrees), f32)],
        name="synthesis",
        cost_estimate=pl.CostEstimate(flops=100000000000, bytes_accessed=400000000, transcendentals=0),
        compiler_params=LIMIT,
    )(*pieces, love_numbers.reshape(1, degrees), legendre)
    everyone = lax.all_to_all(synth, ("lat", "lon"), 0, 0, tiled=True)

    *windows, harmonics = pl.pallas_call(
        functools.partial(windows_kernel, period, slots, chips, bands),
        out_shape=[struct((taller, width))] * 5 + [struct((4 * waves, width), bf16)],
        in_specs=[HBM] * 5 + [VMEM] * 7,
        out_specs=[VMEM] * 6,
        scratch_shapes=[
            pltpu.SMEM((waves,), jnp.int32),
            pltpu.VMEM((3, rows, cols), f32),
            pltpu.VMEM((rows, cols), jnp.int32),
            pltpu.VMEM((width // 128, taller, 128), f32),
            DMA((5,)),
        ],
        name="windows",
        cost_estimate=pl.CostEstimate(flops=10**11, bytes_accessed=4 * 10**8, transcendentals=0),
        compiler_params=LIMIT,
    )(*in_hbm(wavenumbers, *fields), *sides, even, odd, *corners)

    return pl.pallas_call(
        functools.partial(substep_kernel, sectors, bands),
        out_shape=[struct((rows, cols))] * 4,
        in_specs=[VMEM] * 7,
        out_specs=[HBM] * 4,
        scratch_shapes=[
            pltpu.VMEM((2, taller, 128), f32),
            pltpu.VMEM((taller, width), f32),
            pltpu.VMEM((taller, width), f32),
            pltpu.VMEM((taller, width), f32),
            pltpu.VMEM((taller, width), f32),
            pltpu.VMEM((4, width // 128, taller, 128), f32),
        ]
        + [pltpu.VMEM((rows, cols), f32)] * 4
        + [DMA((4,))],
        name="substeps",
        compiler_params=LIMIT,
    )(everyone, harmonics, *windows)


def solution(mesh):
    return jax.shard_map(
        shards,
        mesh=mesh,
        in_specs=(
            P("lat", "lon"),
            P("lat", "lon"),
            P("lat", "lon"),
            P("lon", "lat", None),
            P(),
            P(),
            P("lat", "lon"),
        ),
        out_specs=(P("lat", "lon"), P("lat", "lon"), P("lat", "lon"), P("lat", "lon")),
        check_vma=False,
    )
```
